32 devices in a mesh: fsdp: 16 (over z, y, core), rep: 2 (over x).
Axes of the slice: x: 2, y: 2, z: 4, core: 2. Of those that a mesh axis runs over, the one named last changes fastest.
Arguments:
- inputs: bfloat16 [4096, 2048], P(('fsdp', 'rep')), may hold values from -12 to 12
- norm_one_gain: bfloat16 [2048], P(('fsdp', 'rep')), may hold values from 0.5 to 1.5
- norm_one_bias: bfloat16 [2048], P(('fsdp', 'rep')), may hold values from -1.25 to 1.25
- w_query: bfloat16 [2048, 2048], P(('fsdp', 'rep')), may hold values from -0.125 to 0.125
- b_query: bfloat16 [2048], P(('fsdp', 'rep')), may hold values from -1.75 to 1.75
- w_key: bfloat16 [2048, 2048], P(('fsdp', 'rep')), may hold values from -0.125 to 0.125
- w_value: bfloat16 [2048, 2048], P(('fsdp', 'rep')), may hold values from -0.125 to 0.125
- b_value: bfloat16 [2048], P(('fsdp', 'rep')), may hold values from -1.75 to 1.75
- w_out: bfloat16 [2048, 2048], P(('fsdp', 'rep')), may hold values from -0.5 to 0.5
- b_out: bfloat16 [2048], P(('fsdp', 'rep')), may hold values from -1.25 to 1.25
- norm_two_gain: bfloat16 [2048], P(('fsdp', 'rep')), may hold values from 0.5 to 1.5
- norm_two_bias: bfloat16 [2048], P(('fsdp', 'rep')), may hold values from -1.25 to 1.25
- w_up: bfloat16 [2048, 8192], P(('fsdp', 'rep')), may hold values from -0.125 to 0.125
- b_up: bfloat16 [8192], P(('fsdp', 'rep')), may hold values from -1.75 to 1.75
- w_down: bfloat16 [2048, 8192], P(('fsdp', 'rep')), may hold values from -0.0625 to 0.0625
- b_down: bfloat16 [2048], P(('fsdp', 'rep')), may hold values from -1.25 to 1.25
- parents: int32 [32], replicated, may hold values from -1 to 23, as said below
- cotangent: bfloat16 [4096, 2048], P(('fsdp', 'rep')), may hold values from -12 to 12
Outputs:
- layer_output: bfloat16 [4096, 2048], P(('fsdp', 'rep'))
- grad_inputs: float32 [4096, 2048], P(('fsdp', 'rep'))
- grad_norm_one_gain: float32 [2048], P(('fsdp', 'rep'))
- grad_norm_one_bias: float32 [2048], P(('fsdp', 'rep'))
- grad_w_query: float32 [2048, 2048], P(('fsdp', 'rep'))
- grad_b_query: float32 [2048], P(('fsdp', 'rep'))
- grad_w_key: float32 [2048, 2048], P(('fsdp', 'rep'))
- grad_w_value: float32 [2048, 2048], P(('fsdp', 'rep'))
- grad_b_value: float32 [2048], P(('fsdp', 'rep'))
- grad_w_out: float32 [2048, 2048], P(('fsdp', 'rep'))
- grad_b_out: float32 [2048], P(('fsdp', 'rep'))
- grad_norm_two_gain: float32 [2048], P(('fsdp', 'rep'))
- grad_norm_two_bias: float32 [2048], P(('fsdp', 'rep'))
- grad_w_up: float32 [2048, 8192], P(('fsdp', 'rep'))
- grad_b_up: float32 [8192], P(('fsdp', 'rep'))
- grad_w_down: float32 [2048, 8192], P(('fsdp', 'rep'))
- grad_b_down: float32 [2048], P(('fsdp', 'rep'))
The draws below stay inside these ranges and needn't reach their ends.
Inputs may be any that keep to these rules, and one draw needn't show every extreme that they name: parents[s] is -1 for the first segment of a tree, else the segment before s on its path. Each tree fills 16 consecutive segments: a chain of 4 trunk segments in order, then four branch segments whose parent is the trunk's last, then eight leaf segments, two on each branch, in an order drawn from the seed.
All inputs are finite; a program needn't handle non-finite values.
Results may differ from the reference program's by a relative error of at most 0.014.
Values may be sent and summed in bfloat16 or wider, within the bound.
A program may use at most 384 MiB of HBM per device.

```python
import jax
import jax.numpy as jnp
from jax import lax

D = 2048
HEADS = 16
HEAD_DIM = 128
FF = 8192
TOK_DEV = 128
TRUNK_SEGS = 4
TREE_SEGS = 16
SEGS = 32
TOKENS = 4096
TREES = 2
N_REP = 2


def draw_parents(key, part):
    tree_total = SEGS // TREE_SEGS

    def one_tree(tree_index):
        tree_key = jax.random.fold_in(jax.random.fold_in(key, 7), tree_index)
        leaf_order = jax.random.permutation(tree_key, 8).astype(jnp.int32)
        base_seg = tree_index * TREE_SEGS
        trunk_pos = jnp.arange(TRUNK_SEGS, dtype=jnp.int32)
        trunk = jnp.where(trunk_pos == 0, -1, base_seg + trunk_pos - 1)
        branches = jnp.full((4,), 0, jnp.int32) + base_seg + TRUNK_SEGS - 1
        leaves = base_seg + TRUNK_SEGS + leaf_order // 2
        return jnp.concatenate([trunk, branches, leaves]).astype(jnp.int32)
    return jax.vmap(one_tree)(jnp.arange(tree_total, dtype=jnp.int32)).reshape(-1)


def raised(drawn, rng, source, target, blocks, factor):
    def block_of(dim):
        return (jnp.arange(drawn.shape[dim]) // (drawn.shape[dim] // blocks)).reshape((-1,) + (1,) * (drawn.ndim - 1 - dim))

    one_side = jax.random.permutation(rng, blocks)[block_of(target)]
    far = (block_of(target) + blocks // 2) % blocks
    return jnp.where((block_of(source) == one_side) | (block_of(source) == far), factor * drawn, drawn)


def level_of(stream_key, extent, cuts, smallest, high):
    gain = 1.0
    for axis_at, shards_of in cuts:
        steps = jax.random.uniform(jax.random.fold_in(jax.random.fold_in(stream_key, 6), axis_at), (shards_of,), jnp.float32, smallest / len(cuts), high / len(cuts))
        gain = gain * jnp.repeat(jnp.exp(steps), extent[axis_at] // shards_of).reshape((-1,) + (1,) * (len(extent) - 1 - axis_at))
    return gain


def bell_draw(stream_key, dims, deviation, reach, cuts=(), kind=jnp.bfloat16):
    entries = deviation * jax.random.normal(stream_key, dims, jnp.float32)
    if cuts:
        entries = entries * level_of(stream_key, dims, cuts, -0.22, 0.18)
    return jnp.clip(entries, -reach, reach).astype(kind)


def noise_with(stream_key, shape, scale, bound, pieces, heavy, kind=jnp.bfloat16):
    drawn = scale * jax.random.normal(stream_key, shape, jnp.float32)
    if pieces:
        drawn = drawn * level_of(stream_key, shape, pieces, -0.22, 0.18)
    return jnp.clip(raised(drawn, jax.random.fold_in(stream_key, 3), *heavy), -bound, bound).astype(kind)


def setup_inputs(seed: int = 0) -> dict:
    seeds = jax.random.split(jax.random.key(seed), 19)
    inputs = noise_with(seeds[0], (TOKENS, D), 1.0, 12.0, ((0, 32),), (0, 1, 32, 2.75))
    norm_one_gain = jnp.clip(1.0 + 0.1 * jax.random.normal(seeds[1], (D,), jnp.float32), 0.5, 1.5).astype(jnp.bfloat16)
    norm_one_bias = bell_draw(seeds[2], (D,), 0.2, 1.25, ((0, 32),))
    w_query = bell_draw(seeds[3], (D, D), D ** -0.5, 0.125, ((0, 32),))
    b_query = bell_draw(seeds[4], (D,), 0.3, 1.75, ((0, 32),))
    w_key = bell_draw(seeds[5], (D, D), D ** -0.5, 0.125, ((0, 32),))
    w_value = bell_draw(seeds[6], (D, D), D ** -0.5, 0.125, ((0, 32),))
    b_value = bell_draw(seeds[7], (D,), 0.3, 1.75, ((0, 32),))
    w_out = bell_draw(seeds[8], (D, D), (D // 16) ** -0.5, 0.5, ((0, 32),))
    b_out = bell_draw(seeds[9], (D,), 0.2, 1.25, ((0, 32),))
    norm_two_gain = jnp.clip(1.0 + 0.1 * jax.random.normal(seeds[10], (D,), jnp.float32), 0.5, 1.5).astype(jnp.bfloat16)
    norm_two_bias = bell_draw(seeds[11], (D,), 0.2, 1.25, ((0, 32),))
    w_up = bell_draw(seeds[12], (D, FF), D ** -0.5, 0.125, ((0, 32),))
    b_up = bell_draw(seeds[13], (FF,), 0.3, 1.75, ((0, 32),))
    w_down = bell_draw(seeds[14], (D, FF), FF ** -0.5, 0.0625, ((0, 32),))
    b_down = bell_draw(seeds[15], (D,), 0.2, 1.25, ((0, 32),))
    parents = draw_parents(jax.random.fold_in(seeds[18], 71), 0)
    cotangent = noise_with(seeds[17], (TOKENS, D), 1.0, 12.0, ((0, 32),), (0, 1, 32, 2.75))
    return dict(inputs=inputs, norm_one_gain=norm_one_gain, norm_one_bias=norm_one_bias, w_query=w_query, b_query=b_query, w_key=w_key, w_value=w_value, b_value=b_value, w_out=w_out, b_out=b_out, norm_two_gain=norm_two_gain, norm_two_bias=norm_two_bias, w_up=w_up, b_up=b_up, w_down=w_down, b_down=b_down, parents=parents, cotangent=cotangent)


@jax.custom_vjp
def low(v):
    return lax.optimization_barrier(v.astype(jnp.bfloat16)).astype(jnp.float32)

@jax.custom_vjp
def low_back(v):
    return v

def low_keep(v):
    return (low(v), None)

def low_pass(kept, grad):
    return (grad,)

def back_keep(v):
    return (v, None)

def back_low(kept, grad):
    return (low(grad),)
low.defvjp(low_keep, low_pass)
low_back.defvjp(back_keep, back_low)

def layer_norm(values, gain_vec, offset_vec):
    row_mean = lax.optimization_barrier(jnp.mean(values, axis=-1, keepdims=True))
    centred = values - row_mean
    spread = lax.optimization_barrier(jnp.mean(centred * centred, axis=-1, keepdims=True))
    return centred * lax.rsqrt(spread + 1e-05) * gain_vec + offset_vec

def matmul(left_side, right_side):
    return jnp.dot(left_side, right_side, precision=lax.Precision.HIGHEST)

def ancestry(parents):
    current = jnp.arange(SEGS, dtype=jnp.int32)
    all_segs = jnp.arange(SEGS, dtype=jnp.int32)
    seen_any = jnp.zeros((SEGS, SEGS), dtype=jnp.bool_)
    for level_index in range(TRUNK_SEGS + 1):
        upper_seg = jnp.take(parents, jnp.maximum(current, 0))
        current = jnp.where(current >= 0, upper_seg, -1).astype(jnp.int32)
        seen_any = seen_any | (current[:, None] == all_segs[None, :])
    return seen_any

def tree_attention(queries, keys, values, seen):
    tree_tok = TREE_SEGS * TOK_DEV
    block_rows = N_REP * TOK_DEV
    block_count = TREE_SEGS // N_REP
    score_scale = HEAD_DIM ** (-0.5)
    shape_tree = (TREES, tree_tok, HEADS, HEAD_DIM)

    def one_tree(tree_args):
        tree_index, tree_q, tree_k, tree_v = tree_args
        key_pos = jnp.arange(tree_tok, dtype=jnp.int32)
        key_seg = tree_index * TREE_SEGS + key_pos // TOK_DEV

        def one_block(block_args):
            block_index, block_q = block_args
            query_pos = block_index * block_rows + jnp.arange(block_rows, dtype=jnp.int32)
            query_seg = tree_index * TREE_SEGS + query_pos // TOK_DEV
            upward = jnp.take(jnp.take(seen, query_seg, axis=0), key_seg, axis=1)
            same_seg = (query_seg[:, None] == key_seg[None, :]) & (key_pos[None, :] <= query_pos[:, None])
            visible = upward | same_seg
            raw_scores = low_back(jnp.einsum('qhd,khd->hqk', block_q, tree_k, precision=lax.Precision.HIGHEST) * score_scale)
            masked = jnp.where(visible[None], raw_scores, -jnp.inf)
            row_max = lax.optimization_barrier(jnp.max(masked, axis=-1, keepdims=True))
            exp_rows = jnp.exp(masked - row_max)
            prob_rows = exp_rows / lax.optimization_barrier(jnp.sum(exp_rows, axis=-1, keepdims=True))
            return jnp.einsum('hqk,khd->qhd', low(prob_rows), tree_v, precision=lax.Precision.HIGHEST)
        blocks_q = tree_q.reshape(block_count, block_rows, HEADS, HEAD_DIM)
        result = lax.map(jax.checkpoint(one_block), (jnp.arange(block_count, dtype=jnp.int32), blocks_q))
        return result.reshape(tree_tok, HEADS * HEAD_DIM)
    outcome = lax.map(one_tree, (jnp.arange(TREES, dtype=jnp.int32), queries.reshape(shape_tree), keys.reshape(shape_tree), values.reshape(shape_tree)))
    return outcome.reshape(TREES * tree_tok, HEADS * HEAD_DIM)

def reference(inputs, norm_one_gain, norm_one_bias, w_query, b_query, w_key, w_value, b_value, w_out, b_out, norm_two_gain, norm_two_bias, w_up, b_up, w_down, b_down, parents, cotangent):
    seen = ancestry(parents)

    def layer(x_rows, gain_one, bias_one, wq_mat, bq_vec, wk_mat, wv_mat, bv_vec, wo_mat, bo_vec, gain_two, bias_two, wu_mat, bu_vec, wd_mat, bd_vec):
        norm_one = low(layer_norm(x_rows, gain_one, bias_one))
        queries = low_back(low(matmul(norm_one, wq_mat) + bq_vec))
        keys = low_back(low(matmul(norm_one, wk_mat)))
        values = low_back(low(matmul(norm_one, wv_mat) + bv_vec))
        context = low_back(low(tree_attention(queries, keys, values, seen)))
        attended = low_back(matmul(context, wo_mat) + bo_vec)
        residual = x_rows + attended
        norm_two = low(layer_norm(residual, gain_two, bias_two))
        upward = low_back(matmul(norm_two, wu_mat) + bu_vec)
        active = low(jax.nn.gelu(upward, approximate=True))
        return residual + matmul(active, wd_mat.T) + bd_vec
    params = [a.astype(jnp.float32) for a in (inputs, norm_one_gain, norm_one_bias, w_query, b_query, w_key, w_value, b_value, w_out, b_out, norm_two_gain, norm_two_bias, w_up, b_up, w_down, b_down)]
    result, pullback = jax.vjp(layer, *params)
    grads = pullback(cotangent.astype(jnp.float32))
    return (result.astype(jnp.bfloat16), grads[0], grads[1], grads[2], grads[3], grads[4], grads[5], grads[6], grads[7], grads[8], grads[9], grads[10], grads[11], grads[12], grads[13], grads[14], grads[15])
```

```python
import functools

import jax
import jax.numpy as jnp
from jax import lax
from jax.experimental import pallas as pl
from jax.experimental.pallas import tpu as pltpu
from jax.sharding import Mesh, PartitionSpec as P

HEAD_DIM = 128
TRUNK_SEGS = 4
TREE_SEGS = 16
EPS = 1e-05
GROUP = ("blk", "rep")
ALL = ("tree", "blk", "rep")
f32 = jnp.float32
bf16 = jnp.bfloat16


def dot(a, b, ca, cb):
    return lax.dot_general(a, b, (((ca,), (cb,)), ((), ())), preferred_element_type=f32)


MESH = pl.DeviceIdType.MESH
X, Y, Z = 1, 2, 4
ORDERS = ((X, Y, Z), (Y, Z, X), (Z, X, Y))


class Place:
    def __init__(self):
        self.tree = lax.axis_index("tree")
        blk = lax.axis_index("blk")
        self.x = lax.axis_index("rep")
        self.c = lax.rem(blk, 2)
        self.y = lax.rem(blk // 2, 2)
        self.z = blk // 4

    def flipped(self, r, other=0):
        flip = lambda v, on: 1 - v if on else v
        return flip(self.z, r & Z), flip(self.y, r & Y), flip(self.c, other), flip(self.x, r & X)

    def device(self, r, other=0):
        z, y, c, x = self.flipped(r, other)
        return (self.tree, (z * 2 + y) * 2 + c, x)

    def index(self, r, other=0):
        z, y, c, x = self.flipped(r, other)
        return ((z * 2 + y) * 2 + c) * 2 + x


def greet(place):
    barrier = pltpu.get_barrier_semaphore()
    for r, other in ((X, 0), (Y, 0), (Z, 0), (0, 1)):
        pl.semaphore_signal(barrier, inc=1, device_id=place.device(r, other), device_id_type=MESH)
    pl.semaphore_wait(barrier, 4)


def part_columns(width):
    tiles = width // 128
    first = tiles - 2 * (tiles // 3)
    cuts = (0, first, first + tiles // 3, tiles)
    return [(cuts[p] * 128, (cuts[p + 1] - cuts[p]) * 128) for p in range(3)]


def gather_kernel(x_ref, o_ref, send, recv, psend, precv, local):
    place = Place()
    tok, width = x_ref.shape
    cols = part_columns(width)
    greet(place)

    def rows(r, other=0):
        return pl.ds(pl.multiple_of(place.index(r, other) * tok, tok), tok)

    def remote(src, r, p, dim):
        lo, n = cols[p]
        slot = r | dim
        return pltpu.make_async_remote_copy(
            src_ref=src, dst_ref=o_ref.at[rows(r), pl.ds(lo, n)],
            send_sem=send.at[p, slot - 1], recv_sem=recv.at[p, slot - 1],
            device_id=place.device(dim), device_id_type=MESH,
        )

    def pair(r, p):
        lo, n = cols[p]
        src = o_ref.at[rows(r), pl.ds(lo, n)]
        return pltpu.make_async_remote_copy(
            src_ref=src, dst_ref=src, send_sem=psend.at[p, r], recv_sem=precv.at[p, r],
            device_id=place.device(0, 1), device_id_type=MESH,
        )

    started = []
    own = [x_ref.at[:, pl.ds(lo, n)] for lo, n in cols]
    for step in range(3):
        for p in range(3):
            copy = remote(own[p], 0, p, ORDERS[p][step])
            copy.start()
            started.append(copy)
    keep = pltpu.make_async_copy(x_ref, o_ref.at[rows(0)], local)
    keep.start()
    for p in range(3):
        lo, n = cols[p]
        copy = pltpu.make_async_remote_copy(
            src_ref=own[p], dst_ref=o_ref.at[rows(0), pl.ds(lo, n)], send_sem=psend.at[p, 0], recv_sem=precv.at[p, 0],
            device_id=place.device(0, 1), device_id_type=MESH,
        )
        copy.start()
        started.append(copy)

    def arrived(p, slot):
        lo, n = cols[p]
        ref = o_ref.at[rows(slot), pl.ds(lo, n)]
        pltpu.make_async_remote_copy(
            src_ref=ref, dst_ref=ref, send_sem=send.at[p, slot - 1], recv_sem=recv.at[p, slot - 1],
            device_id=place.device(X), device_id_type=MESH,
        ).wait_recv()

    for which in ((1, 0, 0), (0, 1, 0), (1, 1, 0), (0, 0, 1), (1, 0, 1), (0, 1, 1), (1, 1, 1)):
        for p in range(3):
            dims = ORDERS[p]
            slot = sum(d for d, on in zip(dims, which) if on)
            arrived(p, slot)
            lo, n = cols[p]
            src = o_ref.at[rows(slot), pl.ds(lo, n)]
            top = max(j for j in range(3) if which[j])
            for j in range(top + 1, 3):
                copy = remote(src, slot, p, dims[j])
                copy.start()
                started.append(copy)
            copy = pair(slot, p)
            copy.start()
            started.append(copy)
    for copy in started:
        copy.wait_send()
    for p in range(3):
        lo, n = cols[p]
        for r in range(8):
            ref = o_ref.at[rows(r, 1), pl.ds(lo, n)]
            pltpu.make_async_remote_copy(
                src_ref=ref, dst_ref=ref, send_sem=psend.at[p, r], recv_sem=precv.at[p, r],
                device_id=place.device(0, 1), device_id_type=MESH,
            ).wait_recv()
    keep.wait()


def tree_gather(x, cid, name):
    tok, width = x.shape
    dma = pltpu.SemaphoreType.DMA
    return pl.pallas_call(
        gather_kernel,
        out_shape=jax.ShapeDtypeStruct((16 * tok, width), x.dtype),
        in_specs=[pl.BlockSpec(memory_space=pl.ANY)],
        out_specs=pl.BlockSpec(memory_space=pl.ANY),
        scratch_shapes=[dma((3, 7)), dma((3, 7)), dma((3, 8)), dma((3, 8)), dma],
        compiler_params=pltpu.CompilerParams(collective_id=cid, has_side_effects=True),
        cost_estimate=pl.CostEstimate(flops=0, bytes_accessed=64 * x.size, transcendentals=0),
        name=name,
    )(x)


def scatter_kernel(rhs_dim, tok, l_ref, r_ref, o_ref, acc, pout, pin, stage, inbox, psend, precv, send, recv):
    place = Place()
    width = o_ref.shape[1]
    cols = part_columns(width)
    greet(place)
    tile = 512

    def product(zy, other, put):
        z, y, c, _ = place.flipped(zy, other)
        start = pl.multiple_of(((z * 2 + y) * 2 + c) * 2 * tok, 2 * tok)

        def one(j):
            at = pl.multiple_of(j * tile, tile)
            left = l_ref[pl.ds(start, 2 * tok), :]
            if rhs_dim == 1:
                res = lax.dot_general(left, r_ref[pl.ds(at, tile), :], (((1,), (1,)), ((), ())), preferred_element_type=f32)
            else:
                res = lax.dot_general(left, r_ref[:, pl.ds(at, tile)], (((1,), (0,)), ((), ())), preferred_element_type=f32)
            put(at, res)

        pl.loop(0, width // tile)(one)

    def pair(k):
        return pltpu.make_async_remote_copy(
            src_ref=pout.at[k], dst_ref=pin.at[k], send_sem=psend.at[k], recv_sem=precv.at[k],
            device_id=place.device(0, 1), device_id_type=MESH,
        )

    groups = (Z | Y, Z, Y, 0)
    for k, zy in enumerate(groups):
        def put_out(at, res, k=k):
            pout[k, :, pl.ds(at, tile)] = res.astype(bf16)
        product(zy, 1, put_out)
        pair(k).start()

    def hop(p, r, step, slot):
        lo, n = cols[p]
        return pltpu.make_async_remote_copy(
            src_ref=stage.at[r - 1, :, pl.ds(lo, n)], dst_ref=inbox.at[slot, :, pl.ds(lo, n)],
            send_sem=send.at[p, r - 1], recv_sem=recv.at[p, slot],
            device_id=place.device(ORDERS[p][step]), device_id_type=MESH,
        )

    started = []
    for k, zy in enumerate(groups):
        def put_own(at, res, k=k):
            acc[k, :, pl.ds(at, tile)] = res
        product(zy, 0, put_own)
        pair(k).wait_recv()
        for rx in (X, 0):
            r = zy | rx
            xx = place.flipped(rx)[3]
            at = pl.ds(pl.multiple_of(xx * tok, tok), tok)
            for p in range(3):
                lo, n = cols[p]
                total = acc[k, at, pl.ds(lo, n)] + pin[k, at, pl.ds(lo, n)].astype(f32)
                first, second, third = ORDERS[p]
                if r & first:
                    stage[r - 1, :, pl.ds(lo, n)] = total.astype(bf16)
                    slot = 3 - (2 * bool(r & second) + bool(r & third))
                    copy = hop(p, r, 0, slot)
                    copy.start()
                    started.append(copy)
                else:
                    acc[k, at, pl.ds(lo, n)] = total

    def held(p, r):
        k = groups.index(r & (Z | Y))
        xx = place.flipped(r & X)[3]
        lo, n = cols[p]
        return acc[k, pl.ds(pl.multiple_of(xx * tok, tok), tok), pl.ds(lo, n)]

    def take(p, slot):
        lo, n = cols[p]
        hop(p, 1, 0, slot).wait_recv()
        return inbox[slot, :, pl.ds(lo, n)].astype(f32)

    for q in ((1, 1), (1, 0)):
        for p in range(3):
            first, second, third = ORDERS[p]
            lo, n = cols[p]
            r = second + third * q[1]
            stage[r - 1, :, pl.ds(lo, n)] = (held(p, r) + take(p, 3 - (2 * q[0] + q[1]))).astype(bf16)
            copy = hop(p, r, 1, 4 + (1 - q[1]))
            copy.start()
            started.append(copy)
    for p in range(3):
        third = ORDERS[p][2]
        lo, n = cols[p]
        stage[third - 1, :, pl.ds(lo, n)] = (held(p, third) + take(p, 2) + take(p, 4)).astype(bf16)
        copy = hop(p, third, 2, 6)
        copy.start()
        started.append(copy)
    for p in range(3):
        lo, n = cols[p]
        o_ref[:, pl.ds(lo, n)] = held(p, 0) + take(p, 3) + take(p, 5)
    for p in range(3):
        lo, n = cols[p]
        o_ref[:, pl.ds(lo, n)] += take(p, 6)
    for copy in started:
        copy.wait_send()
    for k in range(4):
        pair(k).wait_send()


def product_scatter(left, right, rhs_dim, cid, name):
    tokens = left.shape[0]
    width = right.shape[1 - rhs_dim]
    tok = tokens // 16
    dma = pltpu.SemaphoreType.DMA
    vmem = pl.BlockSpec(memory_space=pltpu.VMEM)
    return pl.pallas_call(
        functools.partial(scatter_kernel, rhs_dim, tok),
        out_shape=jax.ShapeDtypeStruct((tok, width), f32),
        in_specs=[vmem, vmem],
        out_specs=vmem,
        scratch_shapes=[
            pltpu.VMEM((4, 2 * tok, width), f32),
            pltpu.VMEM((4, 2 * tok, width), bf16),
            pltpu.VMEM((4, 2 * tok, width), bf16),
            pltpu.VMEM((7, tok, width), bf16),
            pltpu.VMEM((7, tok, width), bf16),
            dma((4,)), dma((4,)), dma((3, 7)), dma((3, 7)),
        ],
        compiler_params=pltpu.CompilerParams(collective_id=cid, has_side_effects=True, vmem_limit_bytes=48 * 2**20),
        cost_estimate=pl.CostEstimate(flops=2 * tokens * width * left.shape[1], bytes_accessed=64 * tok * width, transcendentals=0),
        name=name,
    )(left, right)


def norm_stats(v):
    mean = jnp.mean(v, axis=-1, keepdims=True)
    centred = v - mean
    root = lax.rsqrt(jnp.mean(centred * centred, axis=-1, keepdims=True) + EPS)
    return centred * root, root


def norm_back(d, n, root, gain):
    g = d * gain
    return root * (g - jnp.mean(g, axis=-1, keepdims=True) - n * jnp.mean(g * n, axis=-1, keepdims=True))


def gelu_pair(u):
    c = (2.0 / jnp.pi) ** 0.5
    t = jnp.tanh(c * (u + 0.044715 * u * u * u))
    act = 0.5 * u * (1.0 + t)
    der = 0.5 * (1.0 + t) + 0.5 * u * (1.0 - t * t) * c * (1.0 + 3 * 0.044715 * u * u)
    return act, der


def to_columns(w):
    rows, n = w.shape
    w = w.reshape(rows, TREE_SEGS, n // TREE_SEGS)
    w = lax.all_to_all(w, GROUP, split_axis=1, concat_axis=0, tiled=True)
    w = w.reshape(rows * TREE_SEGS, n // TREE_SEGS)
    return lax.all_gather(w, "tree", axis=0, tiled=True)


def to_rows(g, rows):
    g = lax.psum_scatter(g.astype(bf16), "tree", scatter_dimension=0, tiled=True)
    c = g.shape[1]
    g = g.reshape(TREE_SEGS, rows, c)
    g = lax.all_to_all(g, GROUP, split_axis=0, concat_axis=2, tiled=True)
    return g.reshape(rows, TREE_SEGS * c).astype(f32)


def visible_mask(parents, tok):
    tree = lax.axis_index("tree")
    own = tree * TREE_SEGS + jnp.arange(TREE_SEGS, dtype=jnp.int32)
    cur = own
    seen = jnp.zeros((TREE_SEGS, TREE_SEGS), jnp.bool_)
    for _ in range(TRUNK_SEGS + 1):
        up = jnp.take(parents, jnp.maximum(cur, 0))
        cur = jnp.where(cur >= 0, up, -1)
        seen = seen | (cur[:, None] == own[None, :])
    tri = jnp.arange(tok)[None, :] <= jnp.arange(tok)[:, None]
    full = seen[:, None, :, None] | (jnp.eye(TREE_SEGS, dtype=jnp.bool_)[:, None, :, None] & tri[None, :, None, :])
    return full.reshape(TREE_SEGS * tok, TREE_SEGS * tok)


def body(
    inputs, gain_one, bias_one, w_query, b_query, w_key, w_value, b_value, w_out, b_out,
    gain_two, bias_two, w_up, b_up, w_down, b_down, parents, cotangent,
):
    tok, width = inputs.shape
    rows = w_query.shape[0]
    ff = w_up.shape[1]
    trees = lax.axis_size("tree")
    me = lax.axis_index(GROUP)
    scale = HEAD_DIM ** -0.5

    smalls = (gain_one, bias_one, b_query, b_value, b_out, gain_two, bias_two, b_down)
    packed = jnp.concatenate([jnp.stack(smalls).reshape(-1), b_up])
    packed = lax.all_gather(packed, ALL, axis=0, tiled=False)
    n_small = len(smalls)
    small_part = packed[:, : n_small * rows].reshape(-1, n_small, rows)
    vecs = small_part.transpose(1, 0, 2).reshape(n_small, width).astype(f32)
    gain_one, bias_one, b_query, b_value, b_out, gain_two, bias_two, b_down = vecs
    b_up = packed[:, n_small * rows :].reshape(-1).astype(f32)
    head = lambda v: lax.dynamic_slice_in_dim(v, me * HEAD_DIM, HEAD_DIM)

    x_full = tree_gather(inputs, 0, "gather_inputs")
    c_full = tree_gather(cotangent, 1, "gather_cotangent")

    w_qkv = to_columns(jnp.concatenate(
        [w.reshape(rows, TREE_SEGS, HEAD_DIM) for w in (w_query, w_key, w_value, w_out)], axis=2
    ).reshape(rows, -1))
    w_ocol = w_qkv[:, 3 * HEAD_DIM :]
    w_qkv = w_qkv[:, : 3 * HEAD_DIM]
    w_orow = lax.all_to_all(
        w_ocol.reshape(TREE_SEGS, HEAD_DIM, HEAD_DIM), GROUP, split_axis=0, concat_axis=2, tiled=True
    ).reshape(HEAD_DIM, width)
    fs = ff // TREE_SEGS
    w_mlp = to_columns(jnp.concatenate(
        [w.reshape(rows, TREE_SEGS, fs) for w in (w_up, w_down)], axis=2
    ).reshape(rows, -1))
    wu, wd = w_mlp[:, :fs], w_mlp[:, fs:]

    n_full, _ = norm_stats(x_full.astype(f32))
    norm_one = (n_full * gain_one + bias_one).astype(bf16)
    qkv = dot(norm_one, w_qkv, 1, 0)
    bias = jnp.concatenate([head(b_query), jnp.zeros((HEAD_DIM,), f32), head(b_value)])
    qkv = (qkv + bias).astype(bf16)
    q, k, v = qkv[:, :HEAD_DIM], qkv[:, HEAD_DIM : 2 * HEAD_DIM], qkv[:, 2 * HEAD_DIM :]
    mask = visible_mask(parents, tok)
    s = jnp.where(mask, dot(q, k, 1, 1) * scale, -jnp.inf)
    e = jnp.exp(s - jnp.max(s, axis=-1, keepdims=True))
    probs = e / jnp.sum(e, axis=-1, keepdims=True)
    probs_low = probs.astype(bf16)
    context = dot(probs_low, v, 1, 0).astype(bf16)

    att = product_scatter(context, w_orow, 0, 2, "scatter_attended")
    x_own = inputs.astype(f32)
    residual = x_own + att + b_out
    n_two, root_two = norm_stats(residual)
    norm_two = (n_two * gain_two + bias_two).astype(bf16)
    nt_full = tree_gather(norm_two, 3, "gather_norm_two")

    upward = dot(nt_full, wu, 1, 0) + lax.dynamic_slice_in_dim(b_up, me * fs, fs)
    act, der = gelu_pair(upward)
    active = act.astype(bf16)
    d_up = (dot(c_full, wd, 1, 0) * der).astype(bf16)
    d_norm_two = product_scatter(d_up, wu, 1, 4, "scatter_d_norm_two")
    mlp = product_scatter(active, wd, 1, 5, "scatter_mlp")
    layer_output = (residual + mlp + b_down).astype(bf16)
    g_up = dot(nt_full, d_up, 0, 0)
    g_down = dot(c_full, active, 0, 0)
    g_mlp = to_rows(jnp.concatenate([g_up, g_down], axis=1), rows).reshape(rows, TREE_SEGS, 2, fs)
    g_up = g_mlp[:, :, 0].reshape(rows, ff)
    g_down = g_mlp[:, :, 1].reshape(rows, ff)
    gb_up = jnp.sum(d_up.astype(f32), axis=0)

    cot = cotangent.astype(f32)
    d_res = cot + norm_back(d_norm_two, n_two, root_two, gain_two)
    d_att = d_res.astype(bf16)
    da_full = tree_gather(d_att, 6, "gather_d_attended")
    d_ctx = dot(da_full, w_orow, 1, 1).astype(bf16)
    g_orow = dot(context, da_full, 0, 0).astype(bf16)
    g_out = lax.all_to_all(
        g_orow.reshape(HEAD_DIM, TREE_SEGS, HEAD_DIM), GROUP, split_axis=1, concat_axis=0, tiled=True
    ).reshape(width, HEAD_DIM)
    dp = dot(d_ctx, v, 1, 1)
    ds = (probs * (dp - jnp.sum(probs * dp, axis=-1, keepdims=True))).astype(bf16)
    d_q = (dot(ds, k, 1, 0) * scale).astype(bf16)
    d_k = (dot(ds, q, 0, 0) * scale).astype(bf16)
    d_v = dot(probs_low, d_ctx, 0, 0).astype(bf16)
    d_qkv = jnp.concatenate([d_q, d_k, d_v], axis=1)
    d_norm_one = product_scatter(d_qkv, w_qkv, 1, 7, "scatter_d_norm_one")
    g_att = to_rows(jnp.concatenate([dot(norm_one, d_qkv, 0, 0).astype(bf16), g_out], axis=1), rows)
    g_att = g_att.reshape(rows, TREE_SEGS, 4, HEAD_DIM)
    g_q, g_k, g_v, g_o = (g_att[:, :, j].reshape(rows, width) for j in range(4))

    n_one, root_one = norm_stats(x_own)
    grad_inputs = d_res + norm_back(d_norm_one, n_one, root_one, gain_one)

    def placed(vec, total):
        return lax.dynamic_update_slice_in_dim(jnp.zeros((total,), f32), vec, me * vec.shape[0], axis=0)

    col = lambda a: jnp.sum(a, axis=0)
    sums = [
        col(d_norm_one * n_one), col(d_norm_one),
        placed(col(d_q.astype(f32)), width), placed(col(d_v.astype(f32)), width),
        col(d_att.astype(f32)), col(d_norm_two * n_two), col(d_norm_two), col(cot),
    ]
    sums = jnp.stack(sums).reshape(len(sums), -1, rows).transpose(1, 0, 2).reshape(-1, len(sums) * rows)
    sums = jnp.concatenate([sums, placed(gb_up, ff).reshape(sums.shape[0], -1)], axis=1)
    sums = lax.psum_scatter(sums, ALL, scatter_dimension=0, tiled=True)[0]
    parts = [sums[j * rows : (j + 1) * rows] for j in range(8)]
    gb_up = sums[8 * rows :]
    return (
        layer_output, grad_inputs, parts[0], parts[1], g_q, parts[2], g_k, g_v, parts[3], g_o, parts[4],
        parts[5], parts[6], g_up, gb_up, g_down, parts[7],
    )


def solution(mesh):
    names = mesh.axis_names
    shape = mesh.devices.shape
    blk = TREE_SEGS // shape[1]
    inner = Mesh(mesh.devices.reshape(shape[0] // blk, blk, shape[1]), ALL)
    mat, vec = P(ALL, None), P(ALL)
    in_specs = (
        mat, vec, vec, mat, vec, mat, mat, vec, mat, vec, vec, vec, mat, vec, mat, vec, P(), mat,
    )
    out_specs = (
        mat, mat, vec, vec, mat, vec, mat, mat, vec, mat, vec, vec, vec, mat, vec, mat, vec,
    )
    return jax.shard_map(body, mesh=inner, in_specs=in_specs, out_specs=out_specs, check_vma=False)
```

```python
import functools

import jax
import jax.numpy as jnp
from jax import lax
from jax.experimental import pallas as pl
from jax.experimental.pallas import tpu as pltpu
from jax.sharding import Mesh, PartitionSpec as P

HEAD_DIM = 128
TRUNK_SEGS = 4
TREE_SEGS = 16
EPS = 1e-05
GROUP = ("blk", "rep")
ALL = ("tree", "blk", "rep")
f32 = jnp.float32
bf16 = jnp.bfloat16


def dot(a, b, ca, cb):
    return lax.dot_general(a, b, (((ca,), (cb,)), ((), ())), preferred_element_type=f32)


MESH = pl.DeviceIdType.MESH
X, Y, Z = 1, 2, 4
COMM_BYTES = 120_000_000
EVEN = ((6, (X, Y, Z)), (5, (Y, Z, X)), (5, (Z, X, Y)))
ROOM = ((8, (X, Z, Y)), (8, (Y, Z, X)))
LIGHT = ((7, (Z, X, Y)), (7, (Z, Y, X)), (2, (X, Y, Z)))


class Place:
    def __init__(self, trees):
        self.trees = trees
        self.tree = lax.axis_index("tree")
        blk = lax.axis_index("blk")
        self.x = lax.axis_index("rep")
        self.c = lax.rem(blk, 2)
        self.y = lax.rem(blk // 2, 2)
        self.z = blk // 4
        self.at = blk * 2 + self.x
        self.flat = self.tree * TREE_SEGS + self.at
        self.closing = False

    def flipped(self, r, other=0):
        flip = lambda v, on: 1 - v if on else v
        return flip(self.z, r & Z), flip(self.y, r & Y), flip(self.c, other), flip(self.x, r & X)

    def device(self, r, other=0):
        z, y, c, x = self.flipped(r, other)
        return (self.tree, (z * 2 + y) * 2 + c, x)

    def index(self, r, other=0):
        z, y, c, x = self.flipped(r, other)
        return ((z * 2 + y) * 2 + c) * 2 + x

    def in_tree(self, k):
        return (lax.rem(self.tree + k, self.trees), self.at // 2, self.x)

    def peer(self, k):
        j = lax.rem(self.at + k, TREE_SEGS)
        return j, (self.tree, j // 2, lax.rem(j, 2))

    def of_flat(self, flat):
        j = lax.rem(flat, TREE_SEGS)
        return (flat // TREE_SEGS, j // 2, lax.rem(j, 2))


def signal(device):
    pl.semaphore_signal(pltpu.get_barrier_semaphore(), inc=1, device_id=device, device_id_type=MESH)


def greet(place, extras=()):
    count = 0
    if any(e.peers for e in extras):
        pl.loop(1, TREE_SEGS)(lambda k: signal(place.peer(k)[1]))
        count += TREE_SEGS - 1
    else:
        for r, other in ((X, 0), (Y, 0), (Z, 0), (0, 1)):
            signal(place.device(r, other))
        count += 4
    if any(e.trees for e in extras):
        for k in range(1, place.trees):
            signal(place.in_tree(k))
        count += place.trees - 1
    for e in extras:
        count += e.greet(place)
    pl.semaphore_wait(pltpu.get_barrier_semaphore(), count)


def push(src, dst, send, recv, device):
    return pltpu.make_async_remote_copy(
        src_ref=src, dst_ref=dst, send_sem=send, recv_sem=recv, device_id=device, device_id_type=MESH
    )


def drain(ref, sem):
    pltpu.make_async_copy(ref, ref, sem).wait()


DMA = pltpu.SemaphoreType.DMA
ANYWHERE = pl.BlockSpec(memory_space=pl.ANY)
IN_VMEM = pl.BlockSpec(memory_space=pltpu.VMEM)


class Extra:
    peers = trees = False
    ins, in_specs, outs, out_specs, scratch = (), (), (), (), ()

    def greet(self, place):
        return 0


class SpreadSmall(Extra):
    trees = True

    def __init__(self, block):
        n = lax.axis_size("tree")
        self.ins, self.in_specs = (block,), (IN_VMEM,)
        self.outs, self.out_specs = (jax.ShapeDtypeStruct((16, n) + block.shape, block.dtype),), (IN_VMEM,)
        self.scratch = (DMA((14 + n,)), DMA((14 + n,)))

    def stages(self, place, src, box, send, recv):
        here = place.at
        box[here, place.tree] = src[...]
        new = []
        for k in range(1, place.trees):
            new.append(push(src, box.at[here, place.tree], send.at[14 + k], recv.at[14 + k], place.in_tree(k)))
            new[-1].start()
        done = list(new)
        yield
        for j, dim in enumerate(((X, 0), (Y, 0), (Z, 0), (0, 1))):
            for copy in new:
                copy.wait_recv()
            new = []
            for sub in range(1 << j):
                block = box.at[place.index(sub)]
                slot = (1 << j) - 1 + sub
                new.append(push(block, block, send.at[slot], recv.at[slot], place.device(*dim)))
                new[-1].start()
            done += new
            yield
        for copy in new:
            copy.wait_recv()
        for copy in done:
            copy.wait_send()


class ReduceSmall(Extra):
    trees = True

    def __init__(self, sums):
        n = sums.shape[1]
        tail = sums.shape[2:]
        self.ins, self.in_specs = (sums,), (IN_VMEM,)
        self.outs, self.out_specs = (jax.ShapeDtypeStruct(tail, f32),), (IN_VMEM,)
        self.scratch = (
            pltpu.VMEM((8, n) + tail, f32), pltpu.VMEM((15, n) + tail, f32), pltpu.VMEM((max(n - 1, 1),) + tail, f32),
            DMA((14 + n,)), DMA((14 + n,)),
        )

    def stages(self, place, src, out, acc, inbox, tbox, send, recv):
        done = []

        def go(block, slot, target):
            done.append(push(block, inbox.at[slot], send.at[slot], recv.at[slot], target))
            done[-1].start()

        for r in range(8):
            go(src.at[place.index(r, 1)], r, place.device(0, 1))
        yield
        for r in range(8):
            done[r].wait_recv()
            acc[r] = src[place.index(r)] + inbox[r]
        at = 8
        for bit in (Z, Y, X):
            for r in range(bit):
                go(acc.at[bit | r], at + r, place.device(bit))
            yield
            for r in range(bit):
                done[at + r].wait_recv()
                acc[r] = acc[r] + inbox[at + r]
            at += bit
        far = []
        for k in range(1, place.trees):
            tree = lax.rem(place.tree + k, place.trees)
            far.append(push(acc.at[0, tree], tbox.at[k - 1], send.at[14 + k], recv.at[14 + k], place.in_tree(k)))
            far[-1].start()
        yield
        total = acc[0, place.tree]
        for k in range(1, place.trees):
            far[k - 1].wait_recv()
            total = total + tbox[k - 1]
        out[...] = total
        for copy in done + far:
            copy.wait_send()


class ToTrees(Extra):
    trees = True

    def __init__(self, src):
        n = lax.axis_size("tree")
        self.ins, self.in_specs = (src,), (ANYWHERE,)
        self.outs, self.out_specs = (jax.ShapeDtypeStruct((n,) + src.shape, src.dtype),), (ANYWHERE,)
        self.scratch = (DMA((n,)), DMA((n,)))

    def stages(self, place, src, dst, send, recv):
        copies = [
            push(src, dst.at[place.tree], send.at[k - 1], recv.at[k - 1], place.in_tree(k)) for k in range(1, place.trees)
        ]
        copies.append(pltpu.make_async_copy(src, dst.at[place.tree], send.at[place.trees - 1]))
        for copy in copies:
            copy.start()
        while not place.closing:
            yield
        for copy in copies:
            copy.wait()


class SwapTrees(Extra):
    trees = True

    def __init__(self, src):
        n = lax.axis_size("tree")
        self.ins, self.in_specs = (src,), (ANYWHERE,)
        shape = (max(n - 1, 1), src.shape[0] // n) + src.shape[1:]
        self.outs, self.out_specs = (jax.ShapeDtypeStruct(shape, src.dtype),), (ANYWHERE,)
        self.scratch = (DMA((n,)), DMA((n,)))

    def stages(self, place, src, dst, send, recv):
        share = dst.shape[1]
        copies = []
        for k in range(1, place.trees):
            tree = lax.rem(place.tree + k, place.trees)
            rows = src.at[pl.ds(pl.multiple_of(tree * share, share), share)]
            copies.append(push(rows, dst.at[k - 1], send.at[k - 1], recv.at[k - 1], place.in_tree(k)))
            copies[-1].start()
        while not place.closing:
            yield
        for copy in copies:
            copy.wait()


class DealColumns(Extra):
    peers = True

    def __init__(self, mats, all_trees=False):
        n = lax.axis_size("tree")
        self.trees = self.all_trees = all_trees
        self.widths = [m.shape[1] // TREE_SEGS for m in mats]
        rows, total = mats[0].shape[0], sum(self.widths)
        self.ins, self.in_specs = tuple(mats), (ANYWHERE,) * len(mats)
        shape = (TREE_SEGS, rows, total)
        shape = (n,) + shape if all_trees else shape
        self.outs, self.out_specs = (jax.ShapeDtypeStruct(shape, bf16),), (ANYWHERE,)
        self.scratch = (DMA, DMA, DMA, DMA((n,)), DMA((n,)))

    def start(self, place, *refs):
        mats, (out, send, recv, keep, _, _) = refs[:-6], refs[-6:]
        box = out.at[place.tree] if self.all_trees else out

        def pieces(j):
            lo = 0
            for m, c in zip(mats, self.widths):
                yield m.at[:, pl.ds(pl.multiple_of(j * c, c), c)], box.at[place.at, :, pl.ds(lo, c)]
                lo += c

        def one(k):
            j, device = place.peer(k)
            for src, dst in pieces(j):
                push(src, dst, send, recv, device).start()

        pl.loop(1, TREE_SEGS)(one)
        for src, dst in pieces(place.at):
            pltpu.make_async_copy(src, dst, keep).start()

    def finish(self, place, *refs):
        mats, (out, send, recv, keep, _, _) = refs[:-6], refs[-6:]
        box = out.at[place.tree] if self.all_trees else out
        most = box.at[pl.ds(0, TREE_SEGS - 1)]
        drain(most, send)
        drain(most, recv)
        drain(box.at[0], keep)

    def stages(self, place, *refs):
        self.start(place, *refs)
        copies = []
        if self.all_trees:
            self.finish(place, *refs)
            mine, far_send, far_recv = refs[-6].at[place.tree], refs[-2], refs[-1]
            for k in range(1, place.trees):
                copies.append(push(mine, mine, far_send.at[k - 1], far_recv.at[k - 1], place.in_tree(k)))
                copies[-1].start()
        while not place.closing:
            yield
        if not self.all_trees:
            self.finish(place, *refs)
        for copy in copies:
            copy.wait()


class DealRows(Extra):
    peers = True

    def __init__(self, src, widths):
        self.widths = widths
        rows = src.shape[1]
        self.ins, self.in_specs = (src,), (ANYWHERE,)
        self.outs = tuple(jax.ShapeDtypeStruct((rows, TREE_SEGS * c), bf16) for c in widths)
        self.out_specs = (ANYWHERE,) * len(widths)
        self.scratch = (DMA, DMA, DMA)

    def start(self, place, src, *refs):
        outs, (send, recv, keep) = refs[:-3], refs[-3:]

        def pieces(j):
            lo = 0
            for out, c in zip(outs, self.widths):
                yield src.at[j, :, pl.ds(lo, c)], out.at[:, pl.ds(pl.multiple_of(place.at * c, c), c)]
                lo += c

        def one(k):
            j, device = place.peer(k)
            for block, dst in pieces(j):
                push(block, dst, send, recv, device).start()

        pl.loop(1, TREE_SEGS)(one)
        for block, dst in pieces(place.at):
            pltpu.make_async_copy(block, dst, keep).start()

    def finish(self, place, src, *refs):
        send, recv, keep = refs[-3:]
        most = src.at[pl.ds(0, TREE_SEGS - 1)]
        drain(most, send)
        drain(most, recv)
        drain(src.at[0], keep)

    def stages(self, place, *refs):
        self.start(place, *refs)
        while not place.closing:
            yield
        self.finish(place, *refs)


class SwapAndDeal(DealRows):
    trees = True

    def __init__(self, src, rows, widths):
        n = lax.axis_size("tree")
        self.widths = widths
        self.ins, self.in_specs = (src,), (IN_VMEM,)
        self.outs = tuple(jax.ShapeDtypeStruct((rows, TREE_SEGS * c), bf16) for c in widths)
        self.out_specs = (ANYWHERE,) * len(widths)
        block = (TREE_SEGS * rows, src.shape[1])
        self.scratch = (
            pltpu.VMEM((max(n - 1, 1),) + block, bf16), pltpu.VMEM((TREE_SEGS, rows, src.shape[1]), bf16),
            DMA((n,)), DMA((n,)), DMA, DMA, DMA,
        )

    def stages(self, place, src, *refs):
        n = len(self.widths)
        outs, (box, total, far_send, far_recv), sems = refs[:n], refs[n : n + 4], refs[n + 4 :]
        rows = total.shape[1]
        share = TREE_SEGS * rows
        copies = []
        for k in range(1, place.trees):
            tree = lax.rem(place.tree + k, place.trees)
            theirs = src.at[pl.ds(pl.multiple_of(tree * share, share), share)]
            copies.append(push(theirs, box.at[k - 1], far_send.at[k - 1], far_recv.at[k - 1], place.in_tree(k)))
            copies[-1].start()
        while not place.closing:
            yield
        for copy in copies:
            copy.wait_recv()

        def add(j):
            at = pl.ds(pl.multiple_of(j * rows, rows), rows)
            value = src[pl.ds(pl.multiple_of(place.tree * share + j * rows, rows), rows), :].astype(f32)
            for k in range(1, place.trees):
                value = value + box[k - 1, at, :].astype(f32)
            total[j] = value.astype(bf16)

        pl.loop(0, TREE_SEGS)(add)
        self.start(place, total, *outs, *sems)
        self.finish(place, total, *outs, *sems)
        for copy in copies:
            copy.wait_send()


class HeadRows(Extra):
    def __init__(self, shard):
        self.rows = shard.shape[0]
        self.ins, self.in_specs = (shard,), (ANYWHERE,)
        self.outs = (jax.ShapeDtypeStruct((HEAD_DIM, shard.shape[1]), shard.dtype),)
        self.out_specs = (ANYWHERE,)
        self.scratch = (DMA((lax.axis_size("tree"),)), DMA)

    def greet(self, place):
        per_head = HEAD_DIM // self.rows
        for b in range(per_head):
            signal(place.of_flat(place.at * per_head + b))
        return place.trees

    def stages(self, place, src, out, send, recv):
        at = place.flat * self.rows
        head = at // HEAD_DIM
        dst = out.at[pl.ds(pl.multiple_of(lax.rem(at, HEAD_DIM), self.rows), self.rows)]

        def each(do_far, do_own):
            for t in range(place.trees):
                own = (place.tree == t) & (place.at == head)
                pl.when(jnp.logical_not(own))(lambda t=t: do_far(
                    push(src, dst, send.at[t], recv, (t, head // 2, lax.rem(head, 2)))
                ))
                if do_own:
                    pl.when(own)(lambda: do_own(pltpu.make_async_copy(src, dst, recv)))

        each(lambda copy: copy.start(), lambda copy: copy.start())
        while not place.closing:
            yield
        each(lambda copy: copy.wait_send(), None)
        drain(out, recv)


class HeadRowsBack(Extra):
    def __init__(self, grad, rows):
        self.rows = rows
        n = lax.axis_size("tree")
        self.ins, self.in_specs = (grad,), (ANYWHERE,)
        self.outs, self.out_specs = (jax.ShapeDtypeStruct((n, rows, grad.shape[1]), grad.dtype),), (ANYWHERE,)
        self.scratch = (DMA((HEAD_DIM // rows,)), DMA)

    def greet(self, place):
        head = place.flat * self.rows // HEAD_DIM
        for t in range(place.trees):
            signal((t, head // 2, lax.rem(head, 2)))
        return HEAD_DIM // self.rows

    def each(self, place, src, out, send, recv, do_far, do_own):
        per_head = HEAD_DIM // self.rows
        for b in range(per_head):
            flat = place.at * per_head + b
            own = place.flat == flat
            block, dst = src.at[pl.ds(b * self.rows, self.rows)], out.at[place.tree]
            pl.when(jnp.logical_not(own))(lambda b=b, block=block, dst=dst, flat=flat: do_far(
                push(block, dst, send.at[b], recv, place.of_flat(flat))
            ))
            if do_own:
                pl.when(own)(lambda block=block, dst=dst: do_own(pltpu.make_async_copy(block, dst, recv)))

    def start(self, place, *refs):
        self.each(place, *refs, lambda copy: copy.start(), lambda copy: copy.start())

    def finish(self, place, *refs):
        self.each(place, *refs, lambda copy: copy.wait_send(), None)
        drain(refs[1], refs[3])


def finish(place, extras, running):
    place.closing = True
    order = [s for e, s in zip(extras, running) if isinstance(e, GatherRows)]
    order += [s for s in running if s not in order]
    for stages in order:
        for _ in stages:
            pass


def sorted_refs(extras, refs, n_in, n_out):
    refs = list(refs)
    take = lambda n: [refs.pop(0) for _ in range(n)]
    own_in, ins = take(n_in), [take(len(e.ins)) for e in extras]
    own_out, outs = take(n_out), [take(len(e.outs)) for e in extras]
    scratch = [take(len(e.scratch)) for e in extras]
    return own_in, own_out, refs, [i + o + s for i, o, s in zip(ins, outs, scratch)]


def call(kernel, extras, args, in_specs, out_shape, out_specs, scratch, cid, name, flops=0, vmem=None):
    out = pl.pallas_call(
        functools.partial(kernel, extras, lax.axis_size("tree")),
        out_shape=out_shape + [o for e in extras for o in e.outs],
        in_specs=in_specs + [i for e in extras for i in e.in_specs],
        out_specs=out_specs + [o for e in extras for o in e.out_specs],
        scratch_shapes=[i for e in extras for i in e.scratch] + scratch,
        compiler_params=pltpu.CompilerParams(collective_id=cid, has_side_effects=True, vmem_limit_bytes=vmem),
        cost_estimate=pl.CostEstimate(flops=flops, bytes_accessed=COMM_BYTES, transcendentals=0),
        name=name,
    )(*args, *[a for e in extras for a in e.ins])
    return out if len(out) > 1 else out[0]


def part_columns(width, plan):
    cuts = [0]
    for share, _ in plan:
        cuts.append(cuts[-1] + share * width // 16)
    return [(cuts[p], cuts[p + 1] - cuts[p]) for p in range(len(plan))]


class GatherRows(Extra):
    def __init__(self, x, plan):
        tok, width = x.shape
        self.plan = plan
        n = len(plan)
        self.ins, self.in_specs = (x,), (ANYWHERE,)
        self.outs, self.out_specs = (jax.ShapeDtypeStruct((16 * tok, width), x.dtype),), (ANYWHERE,)
        self.scratch = (DMA((n, 7)), DMA((n, 7)), DMA((n, 8)), DMA((n, 8)), DMA)

    def stages(self, place, x_ref, o_ref, send, recv, psend, precv, local):
        orders = [order for _, order in self.plan]
        tok, width = x_ref.shape
        cols = part_columns(width, self.plan)

        def rows(r, other=0):
            return pl.ds(pl.multiple_of(place.index(r, other) * tok, tok), tok)

        def remote(src, r, p, dim):
            lo, n = cols[p]
            slot = r | dim
            return pltpu.make_async_remote_copy(
                src_ref=src, dst_ref=o_ref.at[rows(r), pl.ds(lo, n)],
                send_sem=send.at[p, slot - 1], recv_sem=recv.at[p, slot - 1],
                device_id=place.device(dim), device_id_type=MESH,
            )

        def pair(r, p):
            lo, n = cols[p]
            src = o_ref.at[rows(r), pl.ds(lo, n)]
            return pltpu.make_async_remote_copy(
                src_ref=src, dst_ref=src, send_sem=psend.at[p, r], recv_sem=precv.at[p, r],
                device_id=place.device(0, 1), device_id_type=MESH,
            )

        started = []
        own = [x_ref.at[:, pl.ds(lo, n)] for lo, n in cols]
        for step in range(3):
            for p in range(len(orders)):
                copy = remote(own[p], 0, p, orders[p][step])
                copy.start()
                started.append(copy)
        keep = pltpu.make_async_copy(x_ref, o_ref.at[rows(0)], local)
        keep.start()
        for p in range(len(orders)):
            lo, n = cols[p]
            copy = pltpu.make_async_remote_copy(
                src_ref=own[p], dst_ref=o_ref.at[rows(0), pl.ds(lo, n)], send_sem=psend.at[p, 0], recv_sem=precv.at[p, 0],
                device_id=place.device(0, 1), device_id_type=MESH,
            )
            copy.start()
            started.append(copy)

        def arrived(p, slot):
            lo, n = cols[p]
            ref = o_ref.at[rows(slot), pl.ds(lo, n)]
            pltpu.make_async_remote_copy(
                src_ref=ref, dst_ref=ref, send_sem=send.at[p, slot - 1], recv_sem=recv.at[p, slot - 1],
                device_id=place.device(X), device_id_type=MESH,
            ).wait_recv()

        for which in ((1, 0, 0), (0, 1, 0), (1, 1, 0), (0, 0, 1), (1, 0, 1), (0, 1, 1), (1, 1, 1)):
            yield
            for p in range(len(orders)):
                dims = orders[p]
                slot = sum(d for d, on in zip(dims, which) if on)
                arrived(p, slot)
                lo, n = cols[p]
                src = o_ref.at[rows(slot), pl.ds(lo, n)]
                top = max(j for j in range(3) if which[j])
                for j in range(top + 1, 3):
                    copy = remote(src, slot, p, dims[j])
                    copy.start()
                    started.append(copy)
                copy = pair(slot, p)
                copy.start()
                started.append(copy)
        for copy in started:
            copy.wait_send()
        for p in range(len(orders)):
            lo, n = cols[p]
            for r in range(8):
                ref = o_ref.at[rows(r, 1), pl.ds(lo, n)]
                pltpu.make_async_remote_copy(
                    src_ref=ref, dst_ref=ref, send_sem=psend.at[p, r], recv_sem=precv.at[p, r],
                    device_id=place.device(0, 1), device_id_type=MESH,
                ).wait_recv()
        keep.wait()


def gather_kernel(extras, trees, *refs):
    _, _, _, extra_refs = sorted_refs(extras, refs, 0, 0)
    place = Place(trees)
    greet(place, extras)
    running = [e.stages(place, *r) for e, r in zip(extras, extra_refs)]
    for _ in range(8):
        for stages in running:
            next(stages, None)
    finish(place, extras, running)


def tree_gather(x, cid, name, plan=EVEN, extras=()):
    out = call(gather_kernel, tuple(extras) + (GatherRows(x, plan),), [], [], [], [], [], cid, name)
    return (out[-1], *out[:-1]) if extras else out


def scatter_kernel(plan, rhs_dim, tok, extras, trees, *refs):
    orders = [order[::-1] for _, order in plan]
    (l_ref, r_ref), (o_ref,), scratch, extra_refs = sorted_refs(extras, refs, 2, 1)
    acc, pout, pin, stage, inbox, psend, precv, send, recv = scratch
    place = Place(trees)
    width = o_ref.shape[1]
    cols = part_columns(width, plan)
    greet(place, extras)
    tile = 512

    running = [e.stages(place, *r) for e, r in zip(extras, extra_refs)]

    def advance():
        for stages in running:
            next(stages, None)

    advance()

    def product(zy, other, put):
        z, y, c, _ = place.flipped(zy, other)
        start = pl.multiple_of(((z * 2 + y) * 2 + c) * 2 * tok, 2 * tok)

        def one(j):
            at = pl.multiple_of(j * tile, tile)
            left = l_ref[pl.ds(start, 2 * tok), :]
            if rhs_dim == 1:
                res = lax.dot_general(left, r_ref[pl.ds(at, tile), pl.ds(0, l_ref.shape[1])], (((1,), (1,)), ((), ())), preferred_element_type=f32)
            else:
                res = lax.dot_general(left, r_ref[:, pl.ds(at, tile)], (((1,), (0,)), ((), ())), preferred_element_type=f32)
            put(at, res)

        pl.loop(0, width // tile)(one)

    def pair(k):
        return pltpu.make_async_remote_copy(
            src_ref=pout.at[k], dst_ref=pin.at[k], send_sem=psend.at[k], recv_sem=precv.at[k],
            device_id=place.device(0, 1), device_id_type=MESH,
        )

    groups = (Z | Y, Z, Y, 0)
    for k, zy in enumerate(groups):
        def put_out(at, res, k=k):
            pout[k, :, pl.ds(at, tile)] = res.astype(bf16)
        product(zy, 1, put_out)
        pair(k).start()
    advance()

    def hop(p, r, step, slot):
        lo, n = cols[p]
        return pltpu.make_async_remote_copy(
            src_ref=stage.at[r - 1, :, pl.ds(lo, n)], dst_ref=inbox.at[slot, :, pl.ds(lo, n)],
            send_sem=send.at[p, r - 1], recv_sem=recv.at[p, slot],
            device_id=place.device(orders[p][step]), device_id_type=MESH,
        )

    started = []
    for k, zy in enumerate(groups):
        def put_own(at, res, k=k):
            acc[k, :, pl.ds(at, tile)] = res
        product(zy, 0, put_own)
        pair(k).wait_recv()
        for rx in (X, 0):
            r = zy | rx
            xx = place.flipped(rx)[3]
            at = pl.ds(pl.multiple_of(xx * tok, tok), tok)
            for p in range(len(plan)):
                lo, n = cols[p]
                total = acc[k, at, pl.ds(lo, n)] + pin[k, at, pl.ds(lo, n)].astype(f32)
                first, second, third = orders[p]
                if r & first:
                    stage[r - 1, :, pl.ds(lo, n)] = total.astype(bf16)
                    slot = 3 - (2 * bool(r & second) + bool(r & third))
                    copy = hop(p, r, 0, slot)
                    copy.start()
                    started.append(copy)
                else:
                    acc[k, at, pl.ds(lo, n)] = total

    def held(p, r):
        k = groups.index(r & (Z | Y))
        xx = place.flipped(r & X)[3]
        lo, n = cols[p]
        return acc[k, pl.ds(pl.multiple_of(xx * tok, tok), tok), pl.ds(lo, n)]

    def take(p, slot):
        lo, n = cols[p]
        hop(p, 1, 0, slot).wait_recv()
        return inbox[slot, :, pl.ds(lo, n)].astype(f32)

    advance()
    for q in ((1, 1), (1, 0)):
        for p in range(len(plan)):
            first, second, third = orders[p]
            lo, n = cols[p]
            r = second + third * q[1]
            stage[r - 1, :, pl.ds(lo, n)] = (held(p, r) + take(p, 3 - (2 * q[0] + q[1]))).astype(bf16)
            copy = hop(p, r, 1, 4 + (1 - q[1]))
            copy.start()
            started.append(copy)
        advance()
    for p in range(len(plan)):
        third = orders[p][2]
        lo, n = cols[p]
        stage[third - 1, :, pl.ds(lo, n)] = (held(p, third) + take(p, 2) + take(p, 4)).astype(bf16)
        copy = hop(p, third, 2, 6)
        copy.start()
        started.append(copy)
    advance()
    for p in range(len(plan)):
        lo, n = cols[p]
        o_ref[:, pl.ds(lo, n)] = held(p, 0) + take(p, 3) + take(p, 5)
    for p in range(len(plan)):
        lo, n = cols[p]
        o_ref[:, pl.ds(lo, n)] += take(p, 6)
    advance()
    for copy in started:
        copy.wait_send()
    for k in range(4):
        pair(k).wait_send()
    finish(place, extras, running)


def product_scatter(left, right, rhs_dim, cid, name, plan=EVEN, extras=()):
    tokens, inner = left.shape
    width = right.shape[1 - rhs_dim]
    tok = tokens // 16
    n = len(plan)
    scratch = [
        pltpu.VMEM((4, 2 * tok, width), f32),
        pltpu.VMEM((4, 2 * tok, width), bf16),
        pltpu.VMEM((4, 2 * tok, width), bf16),
        pltpu.VMEM((7, tok, width), bf16),
        pltpu.VMEM((7, tok, width), bf16),
        DMA((4,)), DMA((4,)), DMA((n, 7)), DMA((n, 7)),
    ]
    return call(
        functools.partial(scatter_kernel, plan, rhs_dim, tok), extras, [left, right], [IN_VMEM, IN_VMEM],
        [jax.ShapeDtypeStruct((tok, width), f32)], [IN_VMEM],
        scratch, cid, name, 2 * tokens * width * inner, 48 * 2**20,
    )


def norm_stats(v):
    mean = jnp.mean(v, axis=-1, keepdims=True)
    centred = v - mean
    root = lax.rsqrt(jnp.mean(centred * centred, axis=-1, keepdims=True) + EPS)
    return centred * root, root


def norm_back(d, n, root, gain):
    g = d * gain
    return root * (g - jnp.mean(g, axis=-1, keepdims=True) - n * jnp.mean(g * n, axis=-1, keepdims=True))


def gelu_pair(u):
    c = (2.0 / jnp.pi) ** 0.5
    t = jnp.tanh(c * (u + 0.044715 * u * u * u))
    act = 0.5 * u * (1.0 + t)
    der = 0.5 * (1.0 + t) + 0.5 * u * (1.0 - t * t) * c * (1.0 + 3 * 0.044715 * u * u)
    return act, der


def own_rows(g, swapped, rows):
    share = swapped.shape[1]
    mine = lax.dynamic_slice_in_dim(g, lax.axis_index("tree") * share, share)
    if lax.axis_size("tree") > 1:
        mine = (mine.astype(f32) + jnp.sum(swapped.astype(f32), axis=0)).astype(bf16)
    return mine.reshape(TREE_SEGS, rows, -1)


def scores_of(qkv_ref, parent_ref, s, tok):
    hd = HEAD_DIM
    own = pl.ds(pl.multiple_of(s * tok, tok), tok)
    branches = [pl.ds((TRUNK_SEGS + b) * tok, tok) for b in range(4)]
    trunk = pl.ds(0, TRUNK_SEGS * tok)
    parent = parent_ref[s]

    def rows(col):
        up = qkv_ref[branches[0], col]
        for b in range(1, 4):
            up = jnp.where(parent == TRUNK_SEGS + b, qkv_ref[branches[b], col], up)
        return jnp.concatenate([qkv_ref[trunk, col], up, qkv_ref[own, col]], axis=0)

    q = qkv_ref[own, pl.ds(0, hd)]
    k, v = rows(pl.ds(hd, hd)), rows(pl.ds(2 * hd, hd))
    raw = dot(q, k, 1, 1) * HEAD_DIM ** -0.5
    n_trunk = TRUNK_SEGS * tok
    row = lax.broadcasted_iota(jnp.int32, raw.shape, 0)
    col = lax.broadcasted_iota(jnp.int32, raw.shape, 1)
    limit_up = jnp.where(s >= 2 * TRUNK_SEGS, n_trunk + tok, 0)
    limit_own = jnp.where(s >= TRUNK_SEGS, n_trunk + tok, -1)
    in_trunk = (col < n_trunk) & (col <= s * tok + row)
    in_up = (col >= n_trunk) & (col < limit_up)
    in_own = (col >= n_trunk + tok) & (col <= limit_own + row)
    seen = in_trunk | in_up | in_own
    raw = jnp.where(seen, raw, -jnp.inf)
    e = jnp.exp(raw - jnp.max(raw, axis=-1, keepdims=True))
    probs = e / jnp.sum(e, axis=-1, keepdims=True)
    return q, k, v, probs, own, trunk, branches, parent


def attend_kernel(deal, trees, *refs):
    (parent_ref, x_ref, gain_ref, bias_ref, w_ref, b_ref), (n_ref, qkv_ref, ctx_ref), (held,), deal_refs = sorted_refs(
        (deal,), refs, 6, 3
    )
    place = Place(trees)

    @pl.when(pl.program_id(0) == 0)
    def _():
        greet(place, (deal,))
        deal.start(place, *deal_refs[0])

    step = pl.program_id(0)
    rows = x_ref.shape[0]
    tok = held.shape[0] // TREE_SEGS
    n, _ = norm_stats(x_ref[...].astype(f32))
    norm = (n * gain_ref[...] + bias_ref[...]).astype(bf16)
    n_ref[...] = norm
    qkv = (dot(norm, w_ref[...], 1, 0) + b_ref[...]).astype(bf16)
    qkv_ref[...] = qkv
    held[pl.ds(pl.multiple_of(step * rows, rows), rows), :] = qkv

    @pl.when(step == pl.num_programs(0) - 1)
    def _():
        def one(s):
            _, _, v, probs, own, _, _, _ = scores_of(held, parent_ref, s, tok)
            ctx_ref[own, :] = dot(probs.astype(bf16), v, 1, 0).astype(bf16)

        pl.loop(0, TREE_SEGS, unroll=2)(one)
        deal.finish(place, *deal_refs[0])


def attend(parent, x_full, gain, bias, w, b, deal, cid):
    tokens, width = x_full.shape
    n = 3 * HEAD_DIM
    rows = 256
    whole = lambda shape: pl.BlockSpec(shape, lambda i: (0,) * len(shape))
    by_row = lambda cols: pl.BlockSpec((rows, cols), lambda i: (i, 0))
    return pl.pallas_call(
        functools.partial(attend_kernel, deal, lax.axis_size("tree")),
        grid=(tokens // rows,),
        in_specs=[
            pl.BlockSpec(memory_space=pltpu.SMEM), by_row(width), whole((1, width)), whole((1, width)), whole((width, n)),
            whole((1, n)), *deal.in_specs,
        ],
        out_specs=[by_row(width), by_row(n), whole((tokens, HEAD_DIM)), *deal.out_specs],
        scratch_shapes=[*deal.scratch, pltpu.VMEM((tokens, n), bf16)],
        out_shape=[
            jax.ShapeDtypeStruct((tokens, width), bf16),
            jax.ShapeDtypeStruct((tokens, n), bf16),
            jax.ShapeDtypeStruct((tokens, HEAD_DIM), bf16),
            *deal.outs,
        ],
        compiler_params=pltpu.CompilerParams(collective_id=cid, has_side_effects=True, vmem_limit_bytes=40 * 2**20),
        cost_estimate=pl.CostEstimate(flops=2 * tokens * width * n, bytes_accessed=60_000_000, transcendentals=0),
        name="attend",
    )(parent, x_full, gain, bias, w, b, *deal.ins)


def attend_back_kernel(extras, trees, *refs):
    (parent_ref, qkv_ref, d_ref, w_ref), (o_ref,), (dk, dv, d_ctx), extra_refs = sorted_refs(extras, refs, 4, 1)
    place = Place(trees)
    step = pl.program_id(0)

    @pl.when(step == 0)
    def _():
        greet(place, extras)
        for e, r in zip(extras, extra_refs):
            e.start(place, *r)

    rows = d_ref.shape[0]
    tok = qkv_ref.shape[0] // TREE_SEGS
    hd = HEAD_DIM
    scale = HEAD_DIM ** -0.5
    d_ctx[pl.ds(pl.multiple_of(step * rows, rows), rows), :] = dot(d_ref[...], w_ref[...], 1, 1).astype(bf16)

    @pl.when(step == pl.num_programs(0) - 1)
    def _():
        dk[...] = jnp.zeros_like(dk)
        dv[...] = jnp.zeros_like(dv)

        def one(s):
            q, k, v, probs, own, trunk, branches, parent = scores_of(qkv_ref, parent_ref, s, tok)
            dc = d_ctx[own, :]
            dp = dot(dc, v, 1, 1)
            ds = (probs * (dp - jnp.sum(probs * dp, axis=-1, keepdims=True))).astype(bf16)
            o_ref[own, pl.ds(0, hd)] = (dot(ds, k, 1, 0) * scale).astype(bf16)
            gk = dot(ds, q, 0, 0)
            gv = dot(probs.astype(bf16), dc, 0, 0)
            n_trunk = TRUNK_SEGS * tok
            for acc, g in ((dk, gk), (dv, gv)):
                acc[trunk, :] += g[:n_trunk]
                for b in range(4):
                    acc[branches[b], :] += jnp.where(parent == TRUNK_SEGS + b, g[n_trunk : n_trunk + tok], 0.0)
                acc[own, :] += g[n_trunk + tok :]

        pl.loop(0, TREE_SEGS, unroll=2)(one)
        o_ref[:, pl.ds(hd, hd)] = (dk[...] * scale).astype(bf16)
        o_ref[:, pl.ds(2 * hd, hd)] = dv[...].astype(bf16)
        for e, r in zip(extras, extra_refs):
            e.finish(place, *r)


def attend_back(parent, qkv, d_full, w_rows, extras, cid):
    tokens, width = d_full.shape
    n = qkv.shape[1]
    rows = 256
    whole = lambda shape: pl.BlockSpec(shape, lambda i: (0,) * len(shape))
    return pl.pallas_call(
        functools.partial(attend_back_kernel, extras, lax.axis_size("tree")),
        grid=(tokens // rows,),
        in_specs=[
            pl.BlockSpec(memory_space=pltpu.SMEM), whole((tokens, n)), pl.BlockSpec((rows, width), lambda i: (i, 0)),
            whole((HEAD_DIM, width)), *[i for e in extras for i in e.in_specs],
        ],
        out_specs=[whole((tokens, n)), *[o for e in extras for o in e.out_specs]],
        scratch_shapes=[
            *[i for e in extras for i in e.scratch],
            pltpu.VMEM((tokens, HEAD_DIM), f32), pltpu.VMEM((tokens, HEAD_DIM), f32), pltpu.VMEM((tokens, HEAD_DIM), bf16),
        ],
        out_shape=[jax.ShapeDtypeStruct((tokens, n), bf16), *[o for e in extras for o in e.outs]],
        compiler_params=pltpu.CompilerParams(collective_id=cid, has_side_effects=True, vmem_limit_bytes=40 * 2**20),
        cost_estimate=pl.CostEstimate(flops=2 * tokens * width * HEAD_DIM, bytes_accessed=60_000_000, transcendentals=0),
        name="attend_back",
    )(parent, qkv, d_full, w_rows, *[a for e in extras for a in e.ins])


def body(
    inputs, gain_one, bias_one, w_query, b_query, w_key, w_value, b_value, w_out, b_out,
    gain_two, bias_two, w_up, b_up, w_down, b_down, parents, cotangent,
):
    tok, width = inputs.shape
    rows = w_query.shape[0]
    ff = w_up.shape[1]
    fs = ff // TREE_SEGS
    trees = lax.axis_size("tree")
    devices = trees * TREE_SEGS
    tree = lax.axis_index("tree")
    me = lax.axis_index(GROUP)
    head = lambda v: lax.dynamic_slice_in_dim(v, me * HEAD_DIM, HEAD_DIM)

    smalls = jnp.concatenate([gain_one, bias_one, b_query, b_value, b_out, gain_two, bias_two, b_down, b_up])
    n_small = smalls.shape[0]
    block = jnp.pad(smalls, (0, 16 * 128 - n_small)).reshape(16, 128)

    x_full, box, w_orow, w_att, share_up = tree_gather(inputs, 0, "gather_inputs", ROOM, extras=(
        SpreadSmall(block), HeadRows(w_out), DealColumns((w_query, w_key, w_value), all_trees=True), DealColumns((w_up,)),
    ))
    w_att = w_att.reshape(width, -1)
    packed = box.transpose(1, 0, 2, 3).reshape(devices, -1)[:, :n_small]
    vecs = packed[:, : 8 * rows].reshape(devices, 8, rows).transpose(1, 0, 2).reshape(8, width).astype(f32)
    gain_one, bias_one, b_query, b_value, b_out, gain_two, bias_two, b_down = vecs
    b_up = packed[:, 8 * rows :].reshape(-1).astype(f32)

    local_seg = jnp.arange(TREE_SEGS, dtype=jnp.int32)
    own_parents = lax.dynamic_slice_in_dim(parents, tree * TREE_SEGS, TREE_SEGS) - tree * TREE_SEGS
    parent = jnp.where(local_seg >= 2 * TRUNK_SEGS, own_parents, local_seg)

    b_qkv = jnp.concatenate([head(b_query), jnp.zeros((HEAD_DIM,), f32), head(b_value)])
    norm_one, qkv, context, share_down = attend(
        parent, x_full, gain_one[None], bias_one[None], w_att, b_qkv[None], DealColumns((w_down,)), 9
    )
    att, wu, c_full = product_scatter(context, w_orow, 0, 2, "scatter_attended", ROOM, extras=(
        ToTrees(share_up.reshape(-1, fs)), GatherRows(cotangent, ROOM),
    ))
    wu = wu.reshape(width, fs)
    x_own = inputs.astype(f32)
    residual = x_own + att + b_out
    n_two, root_two = norm_stats(residual)
    norm_two = (n_two * gain_two + bias_two).astype(bf16)
    nt_full, wd = tree_gather(norm_two, 3, "gather_norm_two", ROOM, extras=(ToTrees(share_down.reshape(-1, fs)),))
    wd = wd.reshape(width, fs)

    upward = dot(nt_full, wu, 1, 0) + lax.dynamic_slice_in_dim(b_up, me * fs, fs)
    act, der = gelu_pair(upward)
    active = act.astype(bf16)
    d_up = (dot(c_full, wd, 1, 0) * der).astype(bf16)
    g_up = dot(nt_full, d_up, 0, 0).astype(bf16)
    g_down = dot(c_full, active, 0, 0).astype(bf16)
    g_up, g_down, d_up = lax.optimization_barrier((g_up, g_down, d_up))
    d_norm_two, swap_up = product_scatter(d_up, wu, 1, 4, "scatter_d_norm_two", LIGHT, extras=(SwapTrees(g_up),))

    cot = cotangent.astype(f32)
    d_res = cot + norm_back(d_norm_two, n_two, root_two, gain_two)
    d_att = d_res.astype(bf16)
    mlp, swap_down, da_full = product_scatter(active, wd, 1, 5, "scatter_mlp", ROOM, extras=(
        SwapTrees(g_down), GatherRows(d_att, ROOM),
    ))
    g_up, g_down = own_rows(g_up, swap_up, rows), own_rows(g_down, swap_down, rows)
    g_orow = dot(context, da_full, 0, 0).astype(bf16)
    d_qkv, g_up, g_o = attend_back(
        parent, qkv, da_full, w_orow, (DealRows(g_up, (fs,)), HeadRowsBack(g_orow, rows)), 10
    )

    g_qkv = dot(norm_one, d_qkv, 0, 0)
    s_qkv = jnp.sum(d_qkv.astype(f32), axis=0)
    w_f = w_att.astype(f32)
    gb_one = jnp.sum(w_f * s_qkv, axis=1)
    gg_one = (jnp.sum(w_f * g_qkv, axis=1) - bias_one * gb_one) / gain_one
    g_att = g_qkv.astype(bf16)

    def placed(vec, total):
        return lax.dynamic_update_slice_in_dim(jnp.zeros((total,), f32), vec, me * vec.shape[0], axis=0)

    col = lambda a: jnp.sum(a, axis=0)
    sums = [
        gg_one, gb_one, placed(s_qkv[:HEAD_DIM], width), placed(s_qkv[2 * HEAD_DIM :], width),
        col(d_att.astype(f32)), col(d_norm_two * n_two), col(d_norm_two), col(cot),
    ]
    sums = jnp.stack(sums).reshape(8, devices, rows).transpose(1, 0, 2).reshape(devices, 8 * rows)
    sums = jnp.concatenate([sums, placed(col(d_up.astype(f32)), ff).reshape(devices, -1)], axis=1)
    sums = jnp.pad(sums, ((0, 0), (0, 1024 - n_small))).reshape(trees, TREE_SEGS, 8, 128).transpose(1, 0, 2, 3)
    d_norm_one, g_q, g_k, g_v, sums, g_down = product_scatter(d_qkv, w_att, 1, 7, "scatter_d_norm_one", LIGHT, extras=(
        SwapAndDeal(g_att, rows, (HEAD_DIM,) * 3), ReduceSmall(sums), DealRows(g_down, (fs,)),
    ))
    sums = sums.reshape(-1)
    parts = [sums[j * rows : (j + 1) * rows] for j in range(8)]
    gb_up = sums[8 * rows : n_small]

    n_one, root_one = norm_stats(x_own)
    grad_inputs = d_res + norm_back(d_norm_one, n_one, root_one, gain_one)

    layer_output = (residual + mlp + b_down).astype(bf16)
    g_q, g_k, g_v, g_up, g_down = (g.astype(f32) for g in (g_q, g_k, g_v, g_up, g_down))
    g_o = jnp.sum(g_o.astype(f32), axis=0)
    return (
        layer_output, grad_inputs, parts[0], parts[1], g_q, parts[2], g_k, g_v, parts[3], g_o, parts[4],
        parts[5], parts[6], g_up, gb_up, g_down, parts[7],
    )


def solution(mesh):
    names = mesh.axis_names
    shape = mesh.devices.shape
    blk = TREE_SEGS // shape[1]
    inner = Mesh(mesh.devices.reshape(shape[0] // blk, blk, shape[1]), ALL)
    mat, vec = P(ALL, None), P(ALL)
    in_specs = (
        mat, vec, vec, mat, vec, mat, mat, vec, mat, vec, vec, vec, mat, vec, mat, vec, P(), mat,
    )
    out_specs = (
        mat, mat, vec, vec, mat, vec, mat, mat, vec, mat, vec, vec, vec, mat, vec, mat, vec,
    )
    return jax.shard_map(body, mesh=inner, in_specs=in_specs, out_specs=out_specs, check_vma=False)
```

```python
import functools

import jax
import jax.numpy as jnp
from jax import lax
from jax.experimental import pallas as pl
from jax.experimental.pallas import tpu as pltpu
from jax.sharding import Mesh, PartitionSpec as P

HEAD_DIM = 128
TRUNK_SEGS = 4
TREE_SEGS = 16
EPS = 1e-05
GROUP = ("blk", "rep")
ALL = ("tree", "blk", "rep")
f32 = jnp.float32
bf16 = jnp.bfloat16


def dot(a, b, ca, cb):
    return lax.dot_general(a, b, (((ca,), (cb,)), ((), ())), preferred_element_type=f32)


MESH = pl.DeviceIdType.MESH
X, Y, Z = 1, 2, 4
COMM_BYTES = 120_000_000
EVEN = ((6, (X, Y, Z)), (5, (Y, Z, X)), (5, (Z, X, Y)))
ROOM = ((8, (X, Z, Y)), (8, (Y, Z, X)))
LIGHT = ((7, (Z, X, Y)), (7, (Z, Y, X)), (2, (X, Y, Z)))
MIXED = ((6, (X, Z, Y)), (6, (Y, Z, X)), (4, (Z, X, Y)))


class Place:
    def __init__(self, trees):
        self.trees = trees
        self.tree = lax.axis_index("tree")
        blk = lax.axis_index("blk")
        self.x = lax.axis_index("rep")
        self.c = lax.rem(blk, 2)
        self.y = lax.rem(blk // 2, 2)
        self.z = blk // 4
        self.at = blk * 2 + self.x
        self.flat = self.tree * TREE_SEGS + self.at
        self.closing = False

    def flipped(self, r, other=0):
        flip = lambda v, on: 1 - v if on else v
        return flip(self.z, r & Z), flip(self.y, r & Y), flip(self.c, other), flip(self.x, r & X)

    def device(self, r, other=0):
        z, y, c, x = self.flipped(r, other)
        return (self.tree, (z * 2 + y) * 2 + c, x)

    def index(self, r, other=0):
        z, y, c, x = self.flipped(r, other)
        return ((z * 2 + y) * 2 + c) * 2 + x

    def in_tree(self, k):
        return (lax.rem(self.tree + k, self.trees), self.at // 2, self.x)

    def peer(self, k):
        j = lax.rem(self.at + k, TREE_SEGS)
        return j, (self.tree, j // 2, lax.rem(j, 2))

    def of_flat(self, flat):
        j = lax.rem(flat, TREE_SEGS)
        return (flat // TREE_SEGS, j // 2, lax.rem(j, 2))


def signal(device):
    pl.semaphore_signal(pltpu.get_barrier_semaphore(), inc=1, device_id=device, device_id_type=MESH)


def greet(place, extras=()):
    count = 0
    if any(e.everyone for e in extras):
        devices = place.trees * TREE_SEGS
        pl.loop(1, devices)(lambda k: signal(place.of_flat(lax.rem(place.flat + k, devices))))
        pl.semaphore_wait(pltpu.get_barrier_semaphore(), devices - 1)
        return
    if any(e.peers for e in extras):
        pl.loop(1, TREE_SEGS)(lambda k: signal(place.peer(k)[1]))
        count += TREE_SEGS - 1
    else:
        for r, other in ((X, 0), (Y, 0), (Z, 0), (0, 1)):
            signal(place.device(r, other))
        count += 4
    if any(e.trees for e in extras):
        for k in range(1, place.trees):
            signal(place.in_tree(k))
        count += place.trees - 1
    for e in extras:
        count += e.greet(place)
    pl.semaphore_wait(pltpu.get_barrier_semaphore(), count)


def push(src, dst, send, recv, device):
    return pltpu.make_async_remote_copy(
        src_ref=src, dst_ref=dst, send_sem=send, recv_sem=recv, device_id=device, device_id_type=MESH
    )


def drain(ref, sem):
    pltpu.make_async_copy(ref, ref, sem).wait()


DMA = pltpu.SemaphoreType.DMA
ANYWHERE = pl.BlockSpec(memory_space=pl.ANY)
IN_VMEM = pl.BlockSpec(memory_space=pltpu.VMEM)


class Extra:
    peers = trees = everyone = False
    bulk = 2
    ins, in_specs, outs, out_specs, scratch = (), (), (), (), ()

    def greet(self, place):
        return 0


class SpreadSmall(Extra):
    trees = True
    bulk = 0

    def __init__(self, block):
        n = lax.axis_size("tree")
        self.ins, self.in_specs = (block,), (IN_VMEM,)
        self.outs, self.out_specs = (jax.ShapeDtypeStruct((16, n) + block.shape, block.dtype),), (IN_VMEM,)
        self.scratch = (DMA((14 + n,)), DMA((14 + n,)))

    def stages(self, place, src, box, send, recv):
        here = place.at
        box[here, place.tree] = src[...]
        new = []
        for k in range(1, place.trees):
            new.append(push(src, box.at[here, place.tree], send.at[14 + k], recv.at[14 + k], place.in_tree(k)))
            new[-1].start()
        done = list(new)
        yield
        for j, dim in enumerate(((X, 0), (Y, 0), (Z, 0), (0, 1))):
            for copy in new:
                copy.wait_recv()
            new = []
            for sub in range(1 << j):
                block = box.at[place.index(sub)]
                slot = (1 << j) - 1 + sub
                new.append(push(block, block, send.at[slot], recv.at[slot], place.device(*dim)))
                new[-1].start()
            done += new
            yield
        for copy in new:
            copy.wait_recv()
        for copy in done:
            copy.wait_send()


class ReduceSmall(Extra):
    trees = True

    def __init__(self, sums):
        n = sums.shape[1]
        tail = sums.shape[2:]
        self.ins, self.in_specs = (sums,), (IN_VMEM,)
        self.outs, self.out_specs = (jax.ShapeDtypeStruct(tail, f32),), (IN_VMEM,)
        self.scratch = (
            pltpu.VMEM((8, n) + tail, f32), pltpu.VMEM((15, n) + tail, f32), pltpu.VMEM((max(n - 1, 1),) + tail, f32),
            DMA((14 + n,)), DMA((14 + n,)),
        )

    def stages(self, place, src, out, acc, inbox, tbox, send, recv):
        done = []

        def go(block, slot, target):
            done.append(push(block, inbox.at[slot], send.at[slot], recv.at[slot], target))
            done[-1].start()

        for r in range(8):
            go(src.at[place.index(r, 1)], r, place.device(0, 1))
        yield
        for r in range(8):
            done[r].wait_recv()
            acc[r] = src[place.index(r)] + inbox[r]
        at = 8
        for bit in (Z, Y, X):
            for r in range(bit):
                go(acc.at[bit | r], at + r, place.device(bit))
            yield
            for r in range(bit):
                done[at + r].wait_recv()
                acc[r] = acc[r] + inbox[at + r]
            at += bit
        far = []
        for k in range(1, place.trees):
            tree = lax.rem(place.tree + k, place.trees)
            far.append(push(acc.at[0, tree], tbox.at[k - 1], send.at[14 + k], recv.at[14 + k], place.in_tree(k)))
            far[-1].start()
        yield
        total = acc[0, place.tree]
        for k in range(1, place.trees):
            far[k - 1].wait_recv()
            total = total + tbox[k - 1]
        out[...] = total
        for copy in done + far:
            copy.wait_send()


class ToTrees(Extra):
    trees = True

    def __init__(self, src):
        n = lax.axis_size("tree")
        self.ins, self.in_specs = (src,), (ANYWHERE,)
        self.outs, self.out_specs = (jax.ShapeDtypeStruct((n,) + src.shape, src.dtype),), (ANYWHERE,)
        self.scratch = (DMA((n,)), DMA((n,)))

    def stages(self, place, src, dst, send, recv):
        copies = [
            push(src, dst.at[place.tree], send.at[k - 1], recv.at[k - 1], place.in_tree(k)) for k in range(1, place.trees)
        ]
        copies.append(pltpu.make_async_copy(src, dst.at[place.tree], send.at[place.trees - 1]))
        for copy in copies:
            copy.start()
        while not place.closing:
            yield
        for copy in copies:
            copy.wait()


class SwapTrees(Extra):
    trees = True

    def __init__(self, src):
        n = lax.axis_size("tree")
        self.ins, self.in_specs = (src,), (ANYWHERE,)
        shape = (max(n - 1, 1), src.shape[0] // n) + src.shape[1:]
        self.outs, self.out_specs = (jax.ShapeDtypeStruct(shape, src.dtype),), (ANYWHERE,)
        self.scratch = (DMA((n,)), DMA((n,)))

    def stages(self, place, src, dst, send, recv):
        share = dst.shape[1]
        copies = []
        for k in range(1, place.trees):
            tree = lax.rem(place.tree + k, place.trees)
            rows = src.at[pl.ds(pl.multiple_of(tree * share, share), share)]
            copies.append(push(rows, dst.at[k - 1], send.at[k - 1], recv.at[k - 1], place.in_tree(k)))
            copies[-1].start()
        while not place.closing:
            yield
        for copy in copies:
            copy.wait()


class DealColumns(Extra):
    peers = True

    def __init__(self, mat):
        rows, c = mat.shape[0], mat.shape[1] // TREE_SEGS
        self.ins, self.in_specs = (mat,), (ANYWHERE,)
        self.outs, self.out_specs = (jax.ShapeDtypeStruct((TREE_SEGS, rows, c), bf16),), (ANYWHERE,)
        self.scratch = (DMA, DMA, DMA)

    def start(self, place, mat, out, send, recv, keep):
        c = out.shape[2]
        columns = lambda j: mat.at[:, pl.ds(pl.multiple_of(j * c, c), c)]

        def one(k):
            j, device = place.peer(k)
            push(columns(j), out.at[place.at], send, recv, device).start()

        pl.loop(1, TREE_SEGS)(one)
        pltpu.make_async_copy(columns(place.at), out.at[place.at], keep).start()

    def finish(self, place, mat, out, send, recv, keep):
        most = out.at[pl.ds(0, TREE_SEGS - 1)]
        drain(most, send)
        drain(most, recv)
        drain(out.at[0], keep)

    def stages(self, place, *refs):
        self.start(place, *refs)
        while not place.closing:
            yield
        self.finish(place, *refs)


class DealAll(Extra):
    everyone = True

    def __init__(self, *mats):
        devices = lax.axis_size("tree") * TREE_SEGS
        self.widths = [m.shape[1] // TREE_SEGS for m in mats]
        self.ins, self.in_specs = tuple(mats), (ANYWHERE,) * len(mats)
        self.outs = (jax.ShapeDtypeStruct((devices, mats[0].shape[0], sum(self.widths)), bf16),)
        self.out_specs = (ANYWHERE,)
        self.scratch = (DMA, DMA, DMA)

    def pieces(self, place, refs, tree, j):
        mats, out = refs[:-4], refs[-4]
        lo = 0
        for m, c in zip(mats, self.widths):
            yield m.at[:, pl.ds(pl.multiple_of(j * c, c), c)], out.at[place.flat, :, pl.ds(lo, c)]
            lo += c

    def blocks(self, refs):
        return refs[-4]

    def stages(self, place, *refs):
        send, recv, keep = refs[-3:]

        def one(tree, j):
            device = (tree, j // 2, lax.rem(j, 2))
            for src, dst in self.pieces(place, refs, tree, j):
                push(src, dst, send, recv, device).start()

        for k in range(1, place.trees):
            tree = lax.rem(place.tree + k, place.trees)
            pl.loop(0, TREE_SEGS)(lambda i: one(tree, lax.rem(place.at + i, TREE_SEGS)))
        pl.loop(1, TREE_SEGS)(lambda i: one(place.tree, lax.rem(place.at + i, TREE_SEGS)))
        for src, dst in self.pieces(place, refs, place.tree, place.at):
            pltpu.make_async_copy(src, dst, keep).start()
        while not place.closing:
            yield
        whole = self.blocks(refs)
        most = whole.at[pl.ds(0, whole.shape[0] - 1)]
        drain(most, send)
        drain(most, recv)
        drain(whole.at[0], keep)


class DealAllRows(DealAll):
    def __init__(self, src, widths):
        self.widths = widths
        rows = src.shape[1]
        self.ins, self.in_specs = (src,), (ANYWHERE,)
        shape = lambda c: (src.shape[0] // TREE_SEGS, rows, TREE_SEGS * c)
        self.outs = tuple(jax.ShapeDtypeStruct(shape(c), bf16) for c in widths)
        self.out_specs = (ANYWHERE,) * len(widths)
        self.scratch = (DMA, DMA, DMA)

    def pieces(self, place, refs, tree, j):
        src, outs = refs[0], refs[1:-3]
        lo = 0
        for out, c in zip(outs, self.widths):
            columns = pl.ds(pl.multiple_of(place.at * c, c), c)
            yield src.at[tree * TREE_SEGS + j, :, pl.ds(lo, c)], out.at[place.tree, :, columns]
            lo += c

    def blocks(self, refs):
        return refs[0]


class DealRows(Extra):
    peers = True

    def __init__(self, src, widths):
        self.widths = widths
        rows = src.shape[1]
        self.ins, self.in_specs = (src,), (ANYWHERE,)
        self.outs = tuple(jax.ShapeDtypeStruct((rows, TREE_SEGS * c), bf16) for c in widths)
        self.out_specs = (ANYWHERE,) * len(widths)
        self.scratch = (DMA, DMA, DMA)

    def start(self, place, src, *refs):
        outs, (send, recv, keep) = refs[:-3], refs[-3:]

        def pieces(j):
            lo = 0
            for out, c in zip(outs, self.widths):
                yield src.at[j, :, pl.ds(lo, c)], out.at[:, pl.ds(pl.multiple_of(place.at * c, c), c)]
                lo += c

        def one(k):
            j, device = place.peer(k)
            for block, dst in pieces(j):
                push(block, dst, send, recv, device).start()

        pl.loop(1, TREE_SEGS)(one)
        for block, dst in pieces(place.at):
            pltpu.make_async_copy(block, dst, keep).start()

    def finish(self, place, src, *refs):
        send, recv, keep = refs[-3:]
        most = src.at[pl.ds(0, TREE_SEGS - 1)]
        drain(most, send)
        drain(most, recv)
        drain(src.at[0], keep)

    def stages(self, place, *refs):
        self.start(place, *refs)
        while not place.closing:
            yield
        self.finish(place, *refs)


class HeadRows(Extra):
    def __init__(self, shard):
        self.rows = shard.shape[0]
        self.ins, self.in_specs = (shard,), (ANYWHERE,)
        self.outs = (jax.ShapeDtypeStruct((HEAD_DIM, shard.shape[1]), shard.dtype),)
        self.out_specs = (ANYWHERE,)
        self.scratch = (DMA((lax.axis_size("tree"),)), DMA)

    def greet(self, place):
        per_head = HEAD_DIM // self.rows
        for b in range(per_head):
            signal(place.of_flat(place.at * per_head + b))
        return place.trees

    def each(self, place, src, out, send, recv, do_far, do_own):
        at = place.flat * self.rows
        head = at // HEAD_DIM
        dst = out.at[pl.ds(pl.multiple_of(lax.rem(at, HEAD_DIM), self.rows), self.rows)]
        for t in range(place.trees):
            own = (place.tree == t) & (place.at == head)
            pl.when(jnp.logical_not(own))(lambda t=t: do_far(
                push(src, dst, send.at[t], recv, (t, head // 2, lax.rem(head, 2)))
            ))
            if do_own:
                pl.when(own)(lambda: do_own(pltpu.make_async_copy(src, dst, recv)))

    def start(self, place, *refs):
        self.each(place, *refs, lambda copy: copy.start(), lambda copy: copy.start())

    def finish(self, place, *refs):
        self.each(place, *refs, lambda copy: copy.wait_send(), None)
        drain(refs[1], refs[3])


class HeadRowsBack(Extra):
    def __init__(self, grad, rows):
        self.rows = rows
        n = lax.axis_size("tree")
        self.ins, self.in_specs = (grad,), (ANYWHERE,)
        self.outs, self.out_specs = (jax.ShapeDtypeStruct((n, rows, grad.shape[1]), grad.dtype),), (ANYWHERE,)
        self.scratch = (DMA((HEAD_DIM // rows,)), DMA)

    def greet(self, place):
        head = place.flat * self.rows // HEAD_DIM
        for t in range(place.trees):
            signal((t, head // 2, lax.rem(head, 2)))
        return HEAD_DIM // self.rows

    def each(self, place, src, out, send, recv, do_far, do_own):
        per_head = HEAD_DIM // self.rows
        for b in range(per_head):
            flat = place.at * per_head + b
            own = place.flat == flat
            block, dst = src.at[pl.ds(b * self.rows, self.rows)], out.at[place.tree]
            pl.when(jnp.logical_not(own))(lambda b=b, block=block, dst=dst, flat=flat: do_far(
                push(block, dst, send.at[b], recv, place.of_flat(flat))
            ))
            if do_own:
                pl.when(own)(lambda block=block, dst=dst: do_own(pltpu.make_async_copy(block, dst, recv)))

    def start(self, place, *refs):
        self.each(place, *refs, lambda copy: copy.start(), lambda copy: copy.start())

    def finish(self, place, *refs):
        self.each(place, *refs, lambda copy: copy.wait_send(), None)
        drain(refs[1], refs[3])


class Product(Extra):
    def __init__(self, left, right, dim, kind):
        self.dim = dim
        m, n = left.shape[1 - dim], right.shape[1]
        self.ins, self.in_specs = (left, right), (ANYWHERE, IN_VMEM)
        self.outs, self.out_specs = (jax.ShapeDtypeStruct((m, n), kind),), (IN_VMEM,)
        self.scratch = (pltpu.VMEM(left.shape, left.dtype), DMA)

    def stages(self, place, left, right, out, held, sem):
        copy = pltpu.make_async_copy(left, held, sem)
        copy.start()
        yield
        copy.wait()
        count = 4
        block = out.shape[0] // count
        for j in range(count):
            at = pl.ds(j * block, block)
            part = held[at, :] if self.dim == 1 else held[:, at]
            out[at, :] = dot(part, right[...], self.dim, 0).astype(out.dtype)
            yield


def finish(place, extras, running):
    place.closing = True
    order = [s for e, s in zip(extras, running) if isinstance(e, GatherRows)]
    order += [s for s in running if s not in order]
    for stages in order:
        for _ in stages:
            pass


def sorted_refs(extras, refs, n_in, n_out):
    refs = list(refs)
    take = lambda n: [refs.pop(0) for _ in range(n)]
    own_in, ins = take(n_in), [take(len(e.ins)) for e in extras]
    own_out, outs = take(n_out), [take(len(e.outs)) for e in extras]
    scratch = [take(len(e.scratch)) for e in extras]
    return own_in, own_out, refs, [i + o + s for i, o, s in zip(ins, outs, scratch)]


def call(kernel, extras, args, in_specs, out_shape, out_specs, scratch, cid, name, flops=0, vmem=None):
    out = pl.pallas_call(
        functools.partial(kernel, extras, lax.axis_size("tree")),
        out_shape=out_shape + [o for e in extras for o in e.outs],
        in_specs=in_specs + [i for e in extras for i in e.in_specs],
        out_specs=out_specs + [o for e in extras for o in e.out_specs],
        scratch_shapes=[i for e in extras for i in e.scratch] + scratch,
        compiler_params=pltpu.CompilerParams(collective_id=cid, has_side_effects=True, vmem_limit_bytes=vmem),
        cost_estimate=pl.CostEstimate(flops=flops, bytes_accessed=COMM_BYTES, transcendentals=0),
        name=name,
    )(*args, *[a for e in extras for a in e.ins])
    return out if len(out) > 1 else out[0]


def part_columns(width, plan):
    cuts = [0]
    for share, _ in plan:
        cuts.append(cuts[-1] + share * width // 16)
    return [(cuts[p], cuts[p + 1] - cuts[p]) for p in range(len(plan))]


class GatherRows(Extra):
    bulk = 1

    def __init__(self, x, plan):
        tok, width = x.shape
        self.plan = plan
        n = len(plan)
        self.ins, self.in_specs = (x,), (ANYWHERE,)
        self.outs, self.out_specs = (jax.ShapeDtypeStruct((16 * tok, width), x.dtype),), (ANYWHERE,)
        self.scratch = (DMA((n, 7)), DMA((n, 7)), DMA((n, 8)), DMA((n, 8)), DMA)

    def stages(self, place, x_ref, o_ref, send, recv, psend, precv, local):
        orders = [order for _, order in self.plan]
        tok, width = x_ref.shape
        cols = part_columns(width, self.plan)

        def rows(r, other=0):
            return pl.ds(pl.multiple_of(place.index(r, other) * tok, tok), tok)

        def remote(src, r, p, dim):
            lo, n = cols[p]
            slot = r | dim
            return pltpu.make_async_remote_copy(
                src_ref=src, dst_ref=o_ref.at[rows(r), pl.ds(lo, n)],
                send_sem=send.at[p, slot - 1], recv_sem=recv.at[p, slot - 1],
                device_id=place.device(dim), device_id_type=MESH,
            )

        def pair(r, p):
            lo, n = cols[p]
            src = o_ref.at[rows(r), pl.ds(lo, n)]
            return pltpu.make_async_remote_copy(
                src_ref=src, dst_ref=src, send_sem=psend.at[p, r], recv_sem=precv.at[p, r],
                device_id=place.device(0, 1), device_id_type=MESH,
            )

        started = []
        own = [x_ref.at[:, pl.ds(lo, n)] for lo, n in cols]
        for step in range(3):
            for p in range(len(orders)):
                copy = remote(own[p], 0, p, orders[p][step])
                copy.start()
                started.append(copy)
        keep = pltpu.make_async_copy(x_ref, o_ref.at[rows(0)], local)
        keep.start()
        for p in range(len(orders)):
            lo, n = cols[p]
            copy = pltpu.make_async_remote_copy(
                src_ref=own[p], dst_ref=o_ref.at[rows(0), pl.ds(lo, n)], send_sem=psend.at[p, 0], recv_sem=precv.at[p, 0],
                device_id=place.device(0, 1), device_id_type=MESH,
            )
            copy.start()
            started.append(copy)

        def arrived(p, slot):
            lo, n = cols[p]
            ref = o_ref.at[rows(slot), pl.ds(lo, n)]
            pltpu.make_async_remote_copy(
                src_ref=ref, dst_ref=ref, send_sem=send.at[p, slot - 1], recv_sem=recv.at[p, slot - 1],
                device_id=place.device(X), device_id_type=MESH,
            ).wait_recv()

        for which in ((1, 0, 0), (0, 1, 0), (1, 1, 0), (0, 0, 1), (1, 0, 1), (0, 1, 1), (1, 1, 1)):
            yield
            for p in range(len(orders)):
                dims = orders[p]
                slot = sum(d for d, on in zip(dims, which) if on)
                arrived(p, slot)
                lo, n = cols[p]
                src = o_ref.at[rows(slot), pl.ds(lo, n)]
                top = max(j for j in range(3) if which[j])
                for j in range(top + 1, 3):
                    copy = remote(src, slot, p, dims[j])
                    copy.start()
                    started.append(copy)
                copy = pair(slot, p)
                copy.start()
                started.append(copy)
        for copy in started:
            copy.wait_send()
        for p in range(len(orders)):
            lo, n = cols[p]
            for r in range(8):
                ref = o_ref.at[rows(r, 1), pl.ds(lo, n)]
                pltpu.make_async_remote_copy(
                    src_ref=ref, dst_ref=ref, send_sem=psend.at[p, r], recv_sem=precv.at[p, r],
                    device_id=place.device(0, 1), device_id_type=MESH,
                ).wait_recv()
        keep.wait()


def gather_kernel(extras, trees, *refs):
    _, _, _, extra_refs = sorted_refs(extras, refs, 0, 0)
    place = Place(trees)
    greet(place, extras)
    running = [e.stages(place, *r) for e, r in zip(extras, extra_refs)]
    turn = sorted(zip(extras, running), key=lambda e: e[0].bulk)
    for _ in range(8):
        for _, stages in turn:
            next(stages, None)
    finish(place, extras, running)


def tree_gather(x, cid, name, plan=EVEN, extras=()):
    out = call(gather_kernel, tuple(extras) + (GatherRows(x, plan),), [], [], [], [], [], cid, name)
    return (out[-1], *out[:-1]) if extras else out


def scatter_kernel(plan, rhs_dim, tok, extras, trees, *refs):
    orders = [order[::-1] for _, order in plan]
    (l_ref, r_ref), (o_ref,), scratch, extra_refs = sorted_refs(extras, refs, 2, 1)
    acc, pout, pin, stage, inbox, psend, precv, send, recv = scratch
    place = Place(trees)
    width = o_ref.shape[1]
    cols = part_columns(width, plan)
    greet(place, extras)
    tile = 512

    running = [e.stages(place, *r) for e, r in zip(extras, extra_refs)]

    def advance():
        for stages in running:
            next(stages, None)

    advance()

    def product(zy, other, put):
        z, y, c, _ = place.flipped(zy, other)
        start = pl.multiple_of(((z * 2 + y) * 2 + c) * 2 * tok, 2 * tok)

        def one(j):
            at = pl.multiple_of(j * tile, tile)
            left = l_ref[pl.ds(start, 2 * tok), :]
            if rhs_dim == 1:
                res = lax.dot_general(left, r_ref[pl.ds(at, tile), pl.ds(0, l_ref.shape[1])], (((1,), (1,)), ((), ())), preferred_element_type=f32)
            else:
                res = lax.dot_general(left, r_ref[:, pl.ds(at, tile)], (((1,), (0,)), ((), ())), preferred_element_type=f32)
            put(at, res)

        pl.loop(0, width // tile)(one)

    def pair(k):
        return pltpu.make_async_remote_copy(
            src_ref=pout.at[k], dst_ref=pin.at[k], send_sem=psend.at[k], recv_sem=precv.at[k],
            device_id=place.device(0, 1), device_id_type=MESH,
        )

    groups = (Z | Y, Z, Y, 0)

    def for_partner(k):
        def put_out(at, res):
            pout[k, :, pl.ds(at, tile)] = res.astype(bf16)
        product(groups[k], 1, put_out)
        pair(k).start()

    for_partner(0)
    for_partner(1)

    def hop(p, r, step, slot):
        lo, n = cols[p]
        return pltpu.make_async_remote_copy(
            src_ref=stage.at[r - 1, :, pl.ds(lo, n)], dst_ref=inbox.at[slot, :, pl.ds(lo, n)],
            send_sem=send.at[p, r - 1], recv_sem=recv.at[p, slot],
            device_id=place.device(orders[p][step]), device_id_type=MESH,
        )

    started = []
    for k, zy in enumerate(groups):
        def put_own(at, res, k=k):
            acc[k, :, pl.ds(at, tile)] = res
        product(zy, 0, put_own)
        if k + 2 < len(groups):
            for_partner(k + 2)
        if k == 1:
            advance()
        pair(k).wait_recv()
        for rx in (X, 0):
            r = zy | rx
            xx = place.flipped(rx)[3]
            at = pl.ds(pl.multiple_of(xx * tok, tok), tok)
            for p in range(len(plan)):
                lo, n = cols[p]
                total = acc[k, at, pl.ds(lo, n)] + pin[k, at, pl.ds(lo, n)].astype(f32)
                first, second, third = orders[p]
                if r & first:
                    stage[r - 1, :, pl.ds(lo, n)] = total.astype(bf16)
                    slot = 3 - (2 * bool(r & second) + bool(r & third))
                    copy = hop(p, r, 0, slot)
                    copy.start()
                    started.append(copy)
                else:
                    acc[k, at, pl.ds(lo, n)] = total

    def held(p, r):
        k = groups.index(r & (Z | Y))
        xx = place.flipped(r & X)[3]
        lo, n = cols[p]
        return acc[k, pl.ds(pl.multiple_of(xx * tok, tok), tok), pl.ds(lo, n)]

    def take(p, slot):
        lo, n = cols[p]
        hop(p, 1, 0, slot).wait_recv()
        return inbox[slot, :, pl.ds(lo, n)].astype(f32)

    advance()
    for q in ((1, 1), (1, 0)):
        for p in range(len(plan)):
            first, second, third = orders[p]
            lo, n = cols[p]
            r = second + third * q[1]
            stage[r - 1, :, pl.ds(lo, n)] = (held(p, r) + take(p, 3 - (2 * q[0] + q[1]))).astype(bf16)
            copy = hop(p, r, 1, 4 + (1 - q[1]))
            copy.start()
            started.append(copy)
        advance()
    for p in range(len(plan)):
        third = orders[p][2]
        lo, n = cols[p]
        stage[third - 1, :, pl.ds(lo, n)] = (held(p, third) + take(p, 2) + take(p, 4)).astype(bf16)
        copy = hop(p, third, 2, 6)
        copy.start()
        started.append(copy)
    advance()
    for p in range(len(plan)):
        lo, n = cols[p]
        o_ref[:, pl.ds(lo, n)] = held(p, 0) + take(p, 3) + take(p, 5)
    for p in range(len(plan)):
        lo, n = cols[p]
        o_ref[:, pl.ds(lo, n)] += take(p, 6)
    advance()
    for copy in started:
        copy.wait_send()
    for k in range(4):
        pair(k).wait_send()
    finish(place, extras, running)


def product_scatter(left, right, rhs_dim, cid, name, plan=EVEN, extras=()):
    tokens, inner = left.shape
    width = right.shape[1 - rhs_dim]
    tok = tokens // 16
    n = len(plan)
    scratch = [
        pltpu.VMEM((4, 2 * tok, width), f32),
        pltpu.VMEM((4, 2 * tok, width), bf16),
        pltpu.VMEM((4, 2 * tok, width), bf16),
        pltpu.VMEM((7, tok, width), bf16),
        pltpu.VMEM((7, tok, width), bf16),
        DMA((4,)), DMA((4,)), DMA((n, 7)), DMA((n, 7)),
    ]
    return call(
        functools.partial(scatter_kernel, plan, rhs_dim, tok), extras, [left, right], [IN_VMEM, IN_VMEM],
        [jax.ShapeDtypeStruct((tok, width), f32)], [IN_VMEM],
        scratch, cid, name, 2 * tokens * width * inner, 56 * 2**20,
    )


def norm_stats(v):
    mean = jnp.mean(v, axis=-1, keepdims=True)
    centred = v - mean
    root = lax.rsqrt(jnp.mean(centred * centred, axis=-1, keepdims=True) + EPS)
    return centred * root, root


def norm_back(d, n, root, gain):
    g = d * gain
    return root * (g - jnp.mean(g, axis=-1, keepdims=True) - n * jnp.mean(g * n, axis=-1, keepdims=True))


def gelu_pair(u):
    c = (2.0 / jnp.pi) ** 0.5
    t = jnp.tanh(c * (u + 0.044715 * u * u * u))
    act = 0.5 * u * (1.0 + t)
    der = 0.5 * (1.0 + t) + 0.5 * u * (1.0 - t * t) * c * (1.0 + 3 * 0.044715 * u * u)
    return act, der


def own_rows(g, swapped, rows):
    share = swapped.shape[1]
    mine = lax.dynamic_slice_in_dim(g, lax.axis_index("tree") * share, share)
    if lax.axis_size("tree") > 1:
        mine = (mine.astype(f32) + jnp.sum(swapped.astype(f32), axis=0)).astype(bf16)
    return mine.reshape(TREE_SEGS, rows, -1)


def scores_of(qkv_ref, parent_ref, s, tok):
    hd = HEAD_DIM
    own = pl.ds(pl.multiple_of(s * tok, tok), tok)
    branches = [pl.ds((TRUNK_SEGS + b) * tok, tok) for b in range(4)]
    trunk = pl.ds(0, TRUNK_SEGS * tok)
    parent = parent_ref[s]

    def rows(col):
        up = qkv_ref[branches[0], col]
        for b in range(1, 4):
            up = jnp.where(parent == TRUNK_SEGS + b, qkv_ref[branches[b], col], up)
        return jnp.concatenate([qkv_ref[trunk, col], up, qkv_ref[own, col]], axis=0)

    q = qkv_ref[own, pl.ds(0, hd)]
    k, v = rows(pl.ds(hd, hd)), rows(pl.ds(2 * hd, hd))
    raw = dot(q, k, 1, 1) * HEAD_DIM ** -0.5
    n_trunk = TRUNK_SEGS * tok
    row = lax.broadcasted_iota(jnp.int32, raw.shape, 0)
    col = lax.broadcasted_iota(jnp.int32, raw.shape, 1)
    limit_up = jnp.where(s >= 2 * TRUNK_SEGS, n_trunk + tok, 0)
    limit_own = jnp.where(s >= TRUNK_SEGS, n_trunk + tok, -1)
    in_trunk = (col < n_trunk) & (col <= s * tok + row)
    in_up = (col >= n_trunk) & (col < limit_up)
    in_own = (col >= n_trunk + tok) & (col <= limit_own + row)
    seen = in_trunk | in_up | in_own
    raw = jnp.where(seen, raw, -jnp.inf)
    e = jnp.exp(raw - jnp.max(raw, axis=-1, keepdims=True))
    probs = e / jnp.sum(e, axis=-1, keepdims=True)
    return q, k, v, probs, own, trunk, branches, parent


def attend_kernel(extras, trees, *refs):
    own_in, own_out, (held,), extra_refs = sorted_refs(extras, refs, 6, 3)
    parent_ref, x_ref, gain_ref, bias_ref, w_ref, b_ref = own_in
    n_ref, qkv_ref, ctx_ref = own_out
    place = Place(trees)

    @pl.when(pl.program_id(0) == 0)
    def _():
        greet(place, extras)
        for e, r in zip(extras, extra_refs):
            e.start(place, *r)

    step = pl.program_id(0)
    rows = x_ref.shape[0]
    tok = held.shape[0] // TREE_SEGS
    n, _ = norm_stats(x_ref[...].astype(f32))
    norm = (n * gain_ref[...] + bias_ref[...]).astype(bf16)
    n_ref[...] = norm
    qkv = (dot(norm, w_ref[...], 1, 0) + b_ref[...]).astype(bf16)
    qkv_ref[...] = qkv
    held[pl.ds(pl.multiple_of(step * rows, rows), rows), :] = qkv

    @pl.when(step == pl.num_programs(0) - 1)
    def _():
        def one(s):
            _, _, v, probs, own, _, _, _ = scores_of(held, parent_ref, s, tok)
            ctx_ref[own, :] = dot(probs.astype(bf16), v, 1, 0).astype(bf16)

        pl.loop(0, TREE_SEGS, unroll=2)(one)
        for e, r in zip(extras, extra_refs):
            e.finish(place, *r)


def attend(parent, x_full, gain, bias, w, b, extras, cid):
    tokens, width = x_full.shape
    n = 3 * HEAD_DIM
    rows = 256
    whole = lambda shape: pl.BlockSpec(shape, lambda i: (0,) * len(shape))
    by_row = lambda cols: pl.BlockSpec((rows, cols), lambda i: (i, 0))
    return pl.pallas_call(
        functools.partial(attend_kernel, extras, lax.axis_size("tree")),
        grid=(tokens // rows,),
        in_specs=[
            pl.BlockSpec(memory_space=pltpu.SMEM), by_row(width), whole((1, width)), whole((1, width)), whole((width, n)),
            whole((1, n)), *[i for e in extras for i in e.in_specs],
        ],
        out_specs=[by_row(width), by_row(n), whole((tokens, HEAD_DIM)), *[o for e in extras for o in e.out_specs]],
        scratch_shapes=[*[i for e in extras for i in e.scratch], pltpu.VMEM((tokens, n), bf16)],
        out_shape=[
            jax.ShapeDtypeStruct((tokens, width), bf16),
            jax.ShapeDtypeStruct((tokens, n), bf16),
            jax.ShapeDtypeStruct((tokens, HEAD_DIM), bf16),
            *[o for e in extras for o in e.outs],
        ],
        compiler_params=pltpu.CompilerParams(collective_id=cid, has_side_effects=True, vmem_limit_bytes=40 * 2**20),
        cost_estimate=pl.CostEstimate(flops=2 * tokens * width * n, bytes_accessed=60_000_000, transcendentals=0),
        name="attend",
    )(parent, x_full, gain, bias, w, b, *[a for e in extras for a in e.ins])


def attend_back_kernel(extras, trees, *refs):
    own_in, own_out, own_scratch, extra_refs = sorted_refs(extras, refs, 5, 2)
    parent_ref, qkv_ref, d_ref, w_ref, n_ref = own_in
    o_ref, g_ref = own_out
    dk, dv, d_ctx, held, sem = own_scratch
    place = Place(trees)
    step = pl.program_id(0)

    @pl.when(step == 0)
    def _():
        greet(place, extras)
        for e, r in zip(extras, extra_refs):
            e.start(place, *r)
        pltpu.make_async_copy(n_ref, held, sem).start()

    rows = d_ref.shape[0]
    tok = qkv_ref.shape[0] // TREE_SEGS
    hd = HEAD_DIM
    scale = HEAD_DIM ** -0.5
    d_ctx[pl.ds(pl.multiple_of(step * rows, rows), rows), :] = dot(d_ref[...], w_ref[...], 1, 1).astype(bf16)

    @pl.when(step == pl.num_programs(0) - 1)
    def _():
        dk[...] = jnp.zeros_like(dk)
        dv[...] = jnp.zeros_like(dv)

        def one(s):
            q, k, v, probs, own, trunk, branches, parent = scores_of(qkv_ref, parent_ref, s, tok)
            dc = d_ctx[own, :]
            dp = dot(dc, v, 1, 1)
            ds = (probs * (dp - jnp.sum(probs * dp, axis=-1, keepdims=True))).astype(bf16)
            o_ref[own, pl.ds(0, hd)] = (dot(ds, k, 1, 0) * scale).astype(bf16)
            gk = dot(ds, q, 0, 0)
            gv = dot(probs.astype(bf16), dc, 0, 0)
            n_trunk = TRUNK_SEGS * tok
            for acc, g in ((dk, gk), (dv, gv)):
                acc[trunk, :] += g[:n_trunk]
                for b in range(4):
                    acc[branches[b], :] += jnp.where(parent == TRUNK_SEGS + b, g[n_trunk : n_trunk + tok], 0.0)
                acc[own, :] += g[n_trunk + tok :]

        pl.loop(0, TREE_SEGS, unroll=2)(one)
        o_ref[:, pl.ds(hd, hd)] = (dk[...] * scale).astype(bf16)
        o_ref[:, pl.ds(2 * hd, hd)] = dv[...].astype(bf16)
        drain(held, sem)
        block = 512
        for j in range(held.shape[1] // block):
            at = pl.ds(j * block, block)
            g_ref[at, :] = dot(held[:, at], o_ref[...], 0, 0)
        for e, r in zip(extras, extra_refs):
            e.finish(place, *r)


def attend_back(parent, qkv, d_full, w_rows, norm_one, extras, cid):
    tokens, width = d_full.shape
    n = qkv.shape[1]
    rows = 256
    whole = lambda shape: pl.BlockSpec(shape, lambda i: (0,) * len(shape))
    return pl.pallas_call(
        functools.partial(attend_back_kernel, extras, lax.axis_size("tree")),
        grid=(tokens // rows,),
        in_specs=[
            pl.BlockSpec(memory_space=pltpu.SMEM), whole((tokens, n)), pl.BlockSpec((rows, width), lambda i: (i, 0)),
            whole((HEAD_DIM, width)), ANYWHERE, *[i for e in extras for i in e.in_specs],
        ],
        out_specs=[whole((tokens, n)), whole((width, n)), *[o for e in extras for o in e.out_specs]],
        scratch_shapes=[
            *[i for e in extras for i in e.scratch],
            pltpu.VMEM((tokens, HEAD_DIM), f32), pltpu.VMEM((tokens, HEAD_DIM), f32), pltpu.VMEM((tokens, HEAD_DIM), bf16),
            pltpu.VMEM((tokens, width), bf16), DMA,
        ],
        out_shape=[
            jax.ShapeDtypeStruct((tokens, n), bf16), jax.ShapeDtypeStruct((width, n), f32), *[o for e in extras for o in e.outs],
        ],
        compiler_params=pltpu.CompilerParams(collective_id=cid, has_side_effects=True, vmem_limit_bytes=40 * 2**20),
        cost_estimate=pl.CostEstimate(flops=2 * tokens * width * HEAD_DIM, bytes_accessed=60_000_000, transcendentals=0),
        name="attend_back",
    )(parent, qkv, d_full, w_rows, norm_one, *[a for e in extras for a in e.ins])


def feed_forward_kernel(n_ref, c_ref, wu_ref, wd_ref, b_ref, active_ref, d_ref, sum_ref):
    act, der = gelu_pair(dot(n_ref[...], wu_ref[...], 1, 0) + b_ref[...])
    active_ref[...] = act.astype(bf16)
    d = (dot(c_ref[...], wd_ref[...], 1, 0) * der).astype(bf16)
    d_ref[...] = d

    @pl.when(pl.program_id(0) == 0)
    def _():
        sum_ref[...] = jnp.zeros_like(sum_ref)

    sum_ref[...] += jnp.sum(d.astype(f32).reshape(-1, 8, d.shape[1]), axis=0)


def feed_forward(n_full, c_full, wu, wd, b):
    tokens, width = n_full.shape
    n = wu.shape[1]
    rows = 256
    whole = lambda shape: pl.BlockSpec(shape, lambda i: (0,) * len(shape))
    by_row = lambda cols: pl.BlockSpec((rows, cols), lambda i: (i, 0))
    return pl.pallas_call(
        feed_forward_kernel,
        grid=(tokens // rows,),
        in_specs=[by_row(width), by_row(width), whole((width, n)), whole((width, n)), whole((1, n))],
        out_specs=[by_row(n), by_row(n), whole((8, n))],
        out_shape=[jax.ShapeDtypeStruct((tokens, n), bf16)] * 2 + [jax.ShapeDtypeStruct((8, n), f32)],
        compiler_params=pltpu.CompilerParams(vmem_limit_bytes=40 * 2**20),
        cost_estimate=pl.CostEstimate(flops=4 * tokens * width * n, bytes_accessed=4 * tokens * width, transcendentals=0),
        name="feed_forward",
    )(n_full, c_full, wu, wd, b[None])


def body(
    inputs, gain_one, bias_one, w_query, b_query, w_key, w_value, b_value, w_out, b_out,
    gain_two, bias_two, w_up, b_up, w_down, b_down, parents, cotangent,
):
    tok, width = inputs.shape
    rows = w_query.shape[0]
    ff = w_up.shape[1]
    fs = ff // TREE_SEGS
    trees = lax.axis_size("tree")
    devices = trees * TREE_SEGS
    tree = lax.axis_index("tree")
    me = lax.axis_index(GROUP)
    head = lambda v: lax.dynamic_slice_in_dim(v, me * HEAD_DIM, HEAD_DIM)

    vectors = (gain_one, bias_one, b_query, b_value, b_out, gain_two, bias_two, b_down, b_up)
    n_small = sum(v.shape[0] for v in vectors)
    block = jnp.zeros((16 * 128,), bf16)
    at = 0
    for v in vectors:
        block = block + jnp.pad(v, (at, 16 * 128 - at - v.shape[0]))
        at += v.shape[0]
    block = block.reshape(16, 128)

    x_full, box, w_att = tree_gather(inputs, 0, "gather_inputs", LIGHT, extras=(
        SpreadSmall(block), DealAll(w_query, w_key, w_value),
    ))
    w_att = w_att.reshape(width, -1)
    packed = box.transpose(1, 0, 2, 3).reshape(devices, -1)[:, :n_small]
    vecs = packed[:, : 8 * rows].reshape(devices, 8, rows).transpose(1, 0, 2).reshape(8, width).astype(f32)
    gain_one, bias_one, b_query, b_value, b_out, gain_two, bias_two, b_down = vecs
    b_up = packed[:, 8 * rows :].reshape(-1).astype(f32)

    local_seg = jnp.arange(TREE_SEGS, dtype=jnp.int32)
    own_parents = lax.dynamic_slice_in_dim(parents, tree * TREE_SEGS, TREE_SEGS) - tree * TREE_SEGS
    parent = jnp.where(local_seg >= 2 * TRUNK_SEGS, own_parents, local_seg)

    b_qkv = jnp.concatenate([head(b_query), jnp.zeros((HEAD_DIM,), f32), head(b_value)])
    norm_one, qkv, context, w_orow, share_up, share_down = attend(
        parent, x_full, gain_one[None], bias_one[None], w_att, b_qkv[None],
        (HeadRows(w_out), DealColumns(w_up), DealColumns(w_down)), 9
    )
    att, wd, c_full = product_scatter(context, w_orow, 0, 2, "scatter_attended", LIGHT, extras=(
        ToTrees(share_down.reshape(-1, fs)), GatherRows(cotangent, ROOM),
    ))
    wd = wd.reshape(width, fs)
    x_own = inputs.astype(f32)
    residual = x_own + att + b_out
    n_two, root_two = norm_stats(residual)
    norm_two = (n_two * gain_two + bias_two).astype(bf16)
    nt_full, wu = tree_gather(norm_two, 3, "gather_norm_two", LIGHT, extras=(ToTrees(share_up.reshape(-1, fs)),))
    wu = wu.reshape(width, fs)

    active, d_up, gb_up = feed_forward(nt_full, c_full, wu, wd, lax.dynamic_slice_in_dim(b_up, me * fs, fs))
    g_up = dot(nt_full, d_up, 0, 0).astype(bf16)
    d_norm_two, g_up, g_down = product_scatter(d_up, wu, 1, 4, "scatter_d_norm_two", MIXED, extras=(
        DealAllRows(g_up.reshape(devices, rows, fs), (fs,)), Product(c_full, active, 0, bf16),
    ))

    cot = cotangent.astype(f32)
    d_res = cot + norm_back(d_norm_two, n_two, root_two, gain_two)
    d_att = d_res.astype(bf16)
    mlp, swap_down, da_full = product_scatter(active, wd, 1, 5, "scatter_mlp", LIGHT, extras=(
        SwapTrees(g_down), GatherRows(d_att, ROOM),
    ))
    g_down = own_rows(g_down, swap_down, rows)
    g_orow = dot(context, da_full, 0, 0).astype(bf16)
    d_qkv, g_qkv, g_down, g_o = attend_back(
        parent, qkv, da_full, w_orow, norm_one, (DealRows(g_down, (fs,)), HeadRowsBack(g_orow, rows)), 10
    )

    s_qkv = jnp.sum(d_qkv.astype(f32), axis=0)
    w_f = w_att.astype(f32)
    gb_one = jnp.sum(w_f * s_qkv, axis=1)
    gg_one = (jnp.sum(w_f * g_qkv, axis=1) - bias_one * gb_one) / gain_one
    g_att = g_qkv.astype(bf16)

    def placed(vec, total):
        return lax.dynamic_update_slice_in_dim(jnp.zeros((total,), f32), vec, me * vec.shape[0], axis=0)

    col = lambda a: jnp.sum(a, axis=0)
    sums = [
        gg_one, gb_one, placed(s_qkv[:HEAD_DIM], width), placed(s_qkv[2 * HEAD_DIM :], width),
        col(d_att.astype(f32)), col(d_norm_two * n_two), col(d_norm_two), col(cot),
    ]
    sums = jnp.stack(sums).reshape(8, devices, rows).transpose(1, 0, 2).reshape(devices, 8 * rows)
    sums = jnp.concatenate([sums, placed(col(gb_up), ff).reshape(devices, -1)], axis=1)
    sums = jnp.pad(sums, ((0, 0), (0, 1024 - n_small))).reshape(trees, TREE_SEGS, 8, 128).transpose(1, 0, 2, 3)
    d_norm_one, g_q, g_k, g_v, sums = product_scatter(d_qkv, w_att, 1, 7, "scatter_d_norm_one", LIGHT, extras=(
        DealAllRows(g_att.reshape(devices, rows, -1), (HEAD_DIM,) * 3), ReduceSmall(sums),
    ))
    sums = sums.reshape(-1)
    parts = [sums[j * rows : (j + 1) * rows] for j in range(8)]
    gb_up = sums[8 * rows : n_small]

    n_one, root_one = norm_stats(x_own)
    grad_inputs = d_res + norm_back(d_norm_one, n_one, root_one, gain_one)

    layer_output = (residual + mlp + b_down).astype(bf16)
    g_q, g_k, g_v, g_o, g_up = (jnp.sum(g.astype(f32), axis=0) for g in (g_q, g_k, g_v, g_o, g_up))
    g_down = g_down.astype(f32)
    return (
        layer_output, grad_inputs, parts[0], parts[1], g_q, parts[2], g_k, g_v, parts[3], g_o, parts[4],
        parts[5], parts[6], g_up, gb_up, g_down, parts[7],
    )


def solution(mesh):
    names = mesh.axis_names
    shape = mesh.devices.shape
    blk = TREE_SEGS // shape[1]
    inner = Mesh(mesh.devices.reshape(shape[0] // blk, blk, shape[1]), ALL)
    mat, vec = P(ALL, None), P(ALL)
    in_specs = (
        mat, vec, vec, mat, vec, mat, mat, vec, mat, vec, vec, vec, mat, vec, mat, vec, P(), mat,
    )
    out_specs = (
        mat, mat, vec, vec, mat, vec, mat, mat, vec, mat, vec, vec, vec, mat, vec, mat, vec,
    )
    return jax.shard_map(body, mesh=inner, in_specs=in_specs, out_specs=out_specs, check_vma=False)
```

```python
import functools

import jax
import jax.numpy as jnp
from jax import lax
from jax.experimental import pallas as pl
from jax.experimental.pallas import tpu as pltpu
from jax.sharding import Mesh, PartitionSpec as P

HEAD_DIM = 128
TRUNK_SEGS = 4
TREE_SEGS = 16
EPS = 1e-05
GROUP = ("blk", "rep")
ALL = ("tree", "blk", "rep")
f32 = jnp.float32
bf16 = jnp.bfloat16


def dot(a, b, ca, cb):
    return lax.dot_general(a, b, (((ca,), (cb,)), ((), ())), preferred_element_type=f32)


MESH = pl.DeviceIdType.MESH
X, Y, Z = 1, 2, 4
COMM_BYTES = 120_000_000
EVEN = ((6, (X, Y, Z)), (5, (Y, Z, X)), (5, (Z, X, Y)))
ROOM = ((8, (X, Z, Y)), (8, (Y, Z, X)))
LIGHT = ((7, (Z, X, Y)), (7, (Z, Y, X)), (2, (X, Y, Z)))
MIXED = ((6, (X, Z, Y)), (6, (Y, Z, X)), (2, (Z, X, Y)), (2, (Z, Y, X)))
FIRST = ((6, (Z, X, Y)), (6, (Z, Y, X)), (4, (X, Y, Z)))


class Place:
    def __init__(self, trees):
        self.trees = trees
        self.tree = lax.axis_index("tree")
        blk = lax.axis_index("blk")
        self.x = lax.axis_index("rep")
        self.c = lax.rem(blk, 2)
        self.y = lax.rem(blk // 2, 2)
        self.z = blk // 4
        self.at = blk * 2 + self.x
        self.flat = self.tree * TREE_SEGS + self.at
        self.closing = False

    def flipped(self, r, other=0):
        flip = lambda v, on: 1 - v if on else v
        return flip(self.z, r & Z), flip(self.y, r & Y), flip(self.c, other), flip(self.x, r & X)

    def device(self, r, other=0):
        z, y, c, x = self.flipped(r, other)
        return (self.tree, (z * 2 + y) * 2 + c, x)

    def index(self, r, other=0):
        z, y, c, x = self.flipped(r, other)
        return ((z * 2 + y) * 2 + c) * 2 + x

    def in_tree(self, k):
        return (lax.rem(self.tree + k, self.trees), self.at // 2, self.x)

    def peer(self, k):
        j = lax.rem(self.at + k, TREE_SEGS)
        return j, (self.tree, j // 2, lax.rem(j, 2))

    def of_flat(self, flat):
        j = lax.rem(flat, TREE_SEGS)
        return (flat // TREE_SEGS, j // 2, lax.rem(j, 2))


def signal(device):
    pl.semaphore_signal(pltpu.get_barrier_semaphore(), inc=1, device_id=device, device_id_type=MESH)


def greet(place, extras=()):
    count = 0
    if any(e.everyone for e in extras):
        devices = place.trees * TREE_SEGS
        pl.loop(1, devices)(lambda k: signal(place.of_flat(lax.rem(place.flat + k, devices))))
        pl.semaphore_wait(pltpu.get_barrier_semaphore(), devices - 1)
        return
    if any(e.peers for e in extras):
        pl.loop(1, TREE_SEGS)(lambda k: signal(place.peer(k)[1]))
        count += TREE_SEGS - 1
    else:
        for r, other in ((X, 0), (Y, 0), (Z, 0), (0, 1)):
            signal(place.device(r, other))
        count += 4
    if any(e.trees for e in extras):
        for k in range(1, place.trees):
            signal(place.in_tree(k))
        count += place.trees - 1
    for e in extras:
        count += e.greet(place)
    pl.semaphore_wait(pltpu.get_barrier_semaphore(), count)


def push(src, dst, send, recv, device):
    return pltpu.make_async_remote_copy(
        src_ref=src, dst_ref=dst, send_sem=send, recv_sem=recv, device_id=device, device_id_type=MESH
    )


def drain(ref, sem):
    pltpu.make_async_copy(ref, ref, sem).wait()


DMA = pltpu.SemaphoreType.DMA
ANYWHERE = pl.BlockSpec(memory_space=pl.ANY)
IN_VMEM = pl.BlockSpec(memory_space=pltpu.VMEM)


class Extra:
    peers = trees = everyone = False
    bulk = 2
    ins, in_specs, outs, out_specs, scratch = (), (), (), (), ()

    def greet(self, place):
        return 0


class SpreadSmall(Extra):
    trees = True
    bulk = 0

    def __init__(self, block):
        n = lax.axis_size("tree")
        self.ins, self.in_specs = (block,), (IN_VMEM,)
        self.outs, self.out_specs = (jax.ShapeDtypeStruct((16, n) + block.shape, block.dtype),), (IN_VMEM,)
        self.scratch = (DMA((14 + n,)), DMA((14 + n,)))

    def stages(self, place, src, box, send, recv):
        here = place.at
        box[here, place.tree] = src[...]
        new = []
        for k in range(1, place.trees):
            new.append(push(src, box.at[here, place.tree], send.at[14 + k], recv.at[14 + k], place.in_tree(k)))
            new[-1].start()
        done = list(new)
        yield
        held = [(0, 0)]
        for j, (bit, other) in enumerate(((X, 0), (Y, 0), (0, 1), (Z, 0))):
            for copy in new:
                copy.wait_recv()
            new = []
            for k, (r, o) in enumerate(held):
                block = box.at[place.index(r, o)]
                slot = (1 << j) - 1 + k
                new.append(push(block, block, send.at[slot], recv.at[slot], place.device(bit, other)))
                new[-1].start()
            held += [(r | bit, o | other) for r, o in held]
            done += new
            yield
        while not place.closing:
            yield
        for copy in new:
            copy.wait_recv()
        for copy in done:
            copy.wait_send()


class ReduceSmall(Extra):
    trees = True

    def __init__(self, sums):
        n = sums.shape[1]
        tail = sums.shape[2:]
        self.ins, self.in_specs = (sums,), (IN_VMEM,)
        self.outs, self.out_specs = (jax.ShapeDtypeStruct(tail, f32),), (IN_VMEM,)
        self.scratch = (
            pltpu.VMEM((TREE_SEGS,) + tail, f32), pltpu.VMEM((15,) + tail, f32),
            pltpu.VMEM((max(n - 1, 1), TREE_SEGS) + tail, f32), DMA((14 + n,)), DMA((14 + n,)),
        )

    def stages(self, place, src, out, acc, inbox, tbox, send, recv):
        far = []
        for k in range(1, place.trees):
            tree = lax.rem(place.tree + k, place.trees)
            far.append(push(src.at[:, tree], tbox.at[k - 1], send.at[14 + k], recv.at[14 + k], place.in_tree(k)))
            far[-1].start()
        yield
        for copy in far:
            copy.wait_recv()
        for j in range(TREE_SEGS):
            total = src[j, place.tree]
            for k in range(1, place.trees):
                total = total + tbox[k - 1, j]
            acc[j] = total
        left = [(r, o) for r in range(8) for o in range(2)]
        done = []
        for bit, other in ((0, 1), (X, 0), (Y, 0), (Z, 0)):
            new = []
            keep = [(r, o) for r, o in left if not (r & bit or o & other)]
            for r, o in keep:
                slot = len(done) + len(new)
                block = acc.at[place.index(r | bit, o | other)]
                new.append(push(block, inbox.at[slot], send.at[slot], recv.at[slot], place.device(bit, other)))
                new[-1].start()
            yield
            if bit == Z:
                while not place.closing:
                    yield
            for k, (r, o) in enumerate(keep):
                new[k].wait_recv()
                at = place.index(r, o)
                acc[at] = acc[at] + inbox[len(done) + k]
            done += new
            left = keep
        out[...] = acc[place.index(0)]
        for copy in far + done:
            copy.wait_send()


class ToTrees(Extra):
    trees = True

    def __init__(self, src):
        n = lax.axis_size("tree")
        self.ins, self.in_specs = (src,), (ANYWHERE,)
        self.outs, self.out_specs = (jax.ShapeDtypeStruct((n,) + src.shape, src.dtype),), (ANYWHERE,)
        self.scratch = (DMA((n,)), DMA((n,)))

    def stages(self, place, src, dst, send, recv):
        copies = [
            push(src, dst.at[place.tree], send.at[k - 1], recv.at[k - 1], place.in_tree(k)) for k in range(1, place.trees)
        ]
        copies.append(pltpu.make_async_copy(src, dst.at[place.tree], send.at[place.trees - 1]))
        for copy in copies:
            copy.start()
        while not place.closing:
            yield
        for copy in copies:
            copy.wait()


class SwapTrees(Extra):
    trees = True

    def __init__(self, src):
        n = lax.axis_size("tree")
        self.ins, self.in_specs = (src,), (ANYWHERE,)
        shape = (max(n - 1, 1), src.shape[0] // n) + src.shape[1:]
        self.outs, self.out_specs = (jax.ShapeDtypeStruct(shape, src.dtype),), (ANYWHERE,)
        self.scratch = (DMA((n,)), DMA((n,)))

    def stages(self, place, src, dst, send, recv):
        share = dst.shape[1]
        copies = []
        for k in range(1, place.trees):
            tree = lax.rem(place.tree + k, place.trees)
            rows = src.at[pl.ds(pl.multiple_of(tree * share, share), share)]
            copies.append(push(rows, dst.at[k - 1], send.at[k - 1], recv.at[k - 1], place.in_tree(k)))
            copies[-1].start()
        while not place.closing:
            yield
        for copy in copies:
            copy.wait()


class DealColumns(Extra):
    peers = True

    def __init__(self, mat):
        rows, c = mat.shape[0], mat.shape[1] // TREE_SEGS
        self.ins, self.in_specs = (mat,), (ANYWHERE,)
        self.outs, self.out_specs = (jax.ShapeDtypeStruct((TREE_SEGS, rows, c), bf16),), (ANYWHERE,)
        self.scratch = (DMA, DMA, DMA)

    def start(self, place, mat, out, send, recv, keep):
        c = out.shape[2]
        columns = lambda j: mat.at[:, pl.ds(pl.multiple_of(j * c, c), c)]

        def one(k):
            j, device = place.peer(k)
            push(columns(j), out.at[place.at], send, recv, device).start()

        pl.loop(1, TREE_SEGS)(one)
        pltpu.make_async_copy(columns(place.at), out.at[place.at], keep).start()

    def finish(self, place, mat, out, send, recv, keep):
        most = out.at[pl.ds(0, TREE_SEGS - 1)]
        drain(most, send)
        drain(most, recv)
        drain(out.at[0], keep)

    def stages(self, place, *refs):
        self.start(place, *refs)
        while not place.closing:
            yield
        self.finish(place, *refs)


class DealAll(Extra):
    everyone = True

    def __init__(self, *mats):
        devices = lax.axis_size("tree") * TREE_SEGS
        self.widths = [m.shape[1] // TREE_SEGS for m in mats]
        self.ins, self.in_specs = tuple(mats), (ANYWHERE,) * len(mats)
        self.outs = (jax.ShapeDtypeStruct((devices, mats[0].shape[0], sum(self.widths)), bf16),)
        self.out_specs = (ANYWHERE,)
        self.scratch = (DMA, DMA, DMA)

    def pieces(self, place, refs, tree, j):
        mats, out = refs[:-4], refs[-4]
        lo = 0
        for m, c in zip(mats, self.widths):
            yield m.at[:, pl.ds(pl.multiple_of(j * c, c), c)], out.at[place.flat, :, pl.ds(lo, c)]
            lo += c

    def blocks(self, refs):
        return refs[-4]

    def stages(self, place, *refs):
        send, recv, keep = refs[-3:]

        def one(tree, j):
            device = (tree, j // 2, lax.rem(j, 2))
            for src, dst in self.pieces(place, refs, tree, j):
                push(src, dst, send, recv, device).start()

        for k in range(1, place.trees):
            tree = lax.rem(place.tree + k, place.trees)
            pl.loop(0, TREE_SEGS)(lambda i: one(tree, lax.rem(place.at + i, TREE_SEGS)))
        pl.loop(1, TREE_SEGS)(lambda i: one(place.tree, lax.rem(place.at + i, TREE_SEGS)))
        for src, dst in self.pieces(place, refs, place.tree, place.at):
            pltpu.make_async_copy(src, dst, keep).start()
        while not place.closing:
            yield
        whole = self.blocks(refs)
        most = whole.at[pl.ds(0, whole.shape[0] - 1)]
        drain(most, send)
        drain(most, recv)
        drain(whole.at[0], keep)


class DealAllRows(DealAll):
    def __init__(self, src, widths):
        self.widths = widths
        rows = src.shape[1]
        self.ins, self.in_specs = (src,), (ANYWHERE,)
        shape = lambda c: (src.shape[0] // TREE_SEGS, rows, TREE_SEGS * c)
        self.outs = tuple(jax.ShapeDtypeStruct(shape(c), bf16) for c in widths)
        self.out_specs = (ANYWHERE,) * len(widths)
        self.scratch = (DMA, DMA, DMA)

    def pieces(self, place, refs, tree, j):
        src, outs = refs[0], refs[1:-3]
        lo = 0
        for out, c in zip(outs, self.widths):
            columns = pl.ds(pl.multiple_of(place.at * c, c), c)
            yield src.at[tree * TREE_SEGS + j, :, pl.ds(lo, c)], out.at[place.tree, :, columns]
            lo += c

    def blocks(self, refs):
        return refs[0]


class DealRows(Extra):
    peers = True

    def __init__(self, src, widths):
        self.widths = widths
        rows = src.shape[1]
        self.ins, self.in_specs = (src,), (ANYWHERE,)
        self.outs = tuple(jax.ShapeDtypeStruct((rows, TREE_SEGS * c), bf16) for c in widths)
        self.out_specs = (ANYWHERE,) * len(widths)
        self.scratch = (DMA, DMA, DMA)

    def start(self, place, src, *refs):
        outs, (send, recv, keep) = refs[:-3], refs[-3:]

        def pieces(j):
            lo = 0
            for out, c in zip(outs, self.widths):
                yield src.at[j, :, pl.ds(lo, c)], out.at[:, pl.ds(pl.multiple_of(place.at * c, c), c)]
                lo += c

        def one(k):
            j, device = place.peer(k)
            for block, dst in pieces(j):
                push(block, dst, send, recv, device).start()

        pl.loop(1, TREE_SEGS)(one)
        for block, dst in pieces(place.at):
            pltpu.make_async_copy(block, dst, keep).start()

    def finish(self, place, src, *refs):
        send, recv, keep = refs[-3:]
        most = src.at[pl.ds(0, TREE_SEGS - 1)]
        drain(most, send)
        drain(most, recv)
        drain(src.at[0], keep)

    def stages(self, place, *refs):
        self.start(place, *refs)
        while not place.closing:
            yield
        self.finish(place, *refs)


class HeadRows(Extra):
    def __init__(self, shard):
        self.rows = shard.shape[0]
        self.ins, self.in_specs = (shard,), (ANYWHERE,)
        self.outs = (jax.ShapeDtypeStruct((HEAD_DIM, shard.shape[1]), shard.dtype),)
        self.out_specs = (ANYWHERE,)
        self.scratch = (DMA((lax.axis_size("tree"),)), DMA)

    def greet(self, place):
        per_head = HEAD_DIM // self.rows
        for b in range(per_head):
            signal(place.of_flat(place.at * per_head + b))
        return place.trees

    def each(self, place, src, out, send, recv, do_far, do_own):
        at = place.flat * self.rows
        head = at // HEAD_DIM
        dst = out.at[pl.ds(pl.multiple_of(lax.rem(at, HEAD_DIM), self.rows), self.rows)]
        for t in range(place.trees):
            own = (place.tree == t) & (place.at == head)
            pl.when(jnp.logical_not(own))(lambda t=t: do_far(
                push(src, dst, send.at[t], recv, (t, head // 2, lax.rem(head, 2)))
            ))
            if do_own:
                pl.when(own)(lambda: do_own(pltpu.make_async_copy(src, dst, recv)))

    def start(self, place, *refs):
        self.each(place, *refs, lambda copy: copy.start(), lambda copy: copy.start())

    def finish(self, place, *refs):
        self.each(place, *refs, lambda copy: copy.wait_send(), None)
        drain(refs[1], refs[3])


class HeadRowsBack(Extra):
    def __init__(self, grad, rows):
        self.rows = rows
        n = lax.axis_size("tree")
        self.ins, self.in_specs = (grad,), (ANYWHERE,)
        self.outs, self.out_specs = (jax.ShapeDtypeStruct((n, rows, grad.shape[1]), grad.dtype),), (ANYWHERE,)
        self.scratch = (DMA((HEAD_DIM // rows,)), DMA)

    def greet(self, place):
        head = place.flat * self.rows // HEAD_DIM
        for t in range(place.trees):
            signal((t, head // 2, lax.rem(head, 2)))
        return HEAD_DIM // self.rows

    def each(self, place, src, out, send, recv, do_far, do_own):
        per_head = HEAD_DIM // self.rows
        for b in range(per_head):
            flat = place.at * per_head + b
            own = place.flat == flat
            block, dst = src.at[pl.ds(b * self.rows, self.rows)], out.at[place.tree]
            pl.when(jnp.logical_not(own))(lambda b=b, block=block, dst=dst, flat=flat: do_far(
                push(block, dst, send.at[b], recv, place.of_flat(flat))
            ))
            if do_own:
                pl.when(own)(lambda block=block, dst=dst: do_own(pltpu.make_async_copy(block, dst, recv)))

    def start(self, place, *refs):
        self.each(place, *refs, lambda copy: copy.start(), lambda copy: copy.start())

    def finish(self, place, *refs):
        self.each(place, *refs, lambda copy: copy.wait_send(), None)
        drain(refs[1], refs[3])


class Product(Extra):
    def __init__(self, left, right, dim, kind):
        self.dim = dim
        m, n = left.shape[1 - dim], right.shape[1]
        self.ins, self.in_specs = (left, right), (ANYWHERE, IN_VMEM)
        self.outs, self.out_specs = (jax.ShapeDtypeStruct((m, n), kind),), (IN_VMEM,)
        self.scratch = (pltpu.VMEM(left.shape, left.dtype), DMA)

    def stages(self, place, left, right, out, held, sem):
        copy = pltpu.make_async_copy(left, held, sem)
        copy.start()
        yield
        copy.wait()
        count = 4
        block = out.shape[0] // count
        for j in range(count):
            at = pl.ds(j * block, block)
            part = held[at, :] if self.dim == 1 else held[:, at]
            out[at, :] = dot(part, right[...], self.dim, 0).astype(out.dtype)
            yield


def finish(place, extras, running):
    place.closing = True
    order = [s for e, s in zip(extras, running) if isinstance(e, GatherRows)]
    order += [s for s in running if s not in order]
    for stages in order:
        for _ in stages:
            pass


def sorted_refs(extras, refs, n_in, n_out):
    refs = list(refs)
    take = lambda n: [refs.pop(0) for _ in range(n)]
    own_in, ins = take(n_in), [take(len(e.ins)) for e in extras]
    own_out, outs = take(n_out), [take(len(e.outs)) for e in extras]
    scratch = [take(len(e.scratch)) for e in extras]
    return own_in, own_out, refs, [i + o + s for i, o, s in zip(ins, outs, scratch)]


def call(kernel, extras, args, in_specs, out_shape, out_specs, scratch, cid, name, flops=0, vmem=None):
    out = pl.pallas_call(
        functools.partial(kernel, extras, lax.axis_size("tree")),
        out_shape=out_shape + [o for e in extras for o in e.outs],
        in_specs=in_specs + [i for e in extras for i in e.in_specs],
        out_specs=out_specs + [o for e in extras for o in e.out_specs],
        scratch_shapes=[i for e in extras for i in e.scratch] + scratch,
        compiler_params=pltpu.CompilerParams(collective_id=cid, has_side_effects=True, vmem_limit_bytes=vmem),
        cost_estimate=pl.CostEstimate(flops=flops, bytes_accessed=COMM_BYTES, transcendentals=0),
        name=name,
    )(*args, *[a for e in extras for a in e.ins])
    return out if len(out) > 1 else out[0]


def part_columns(width, plan):
    cuts = [0]
    for share, _ in plan:
        cuts.append(cuts[-1] + share * width // 16)
    return [(cuts[p], cuts[p + 1] - cuts[p]) for p in range(len(plan))]


class GatherRows(Extra):
    bulk = 1

    def __init__(self, x, plan):
        tok, width = x.shape
        self.plan = plan
        n = len(plan)
        self.ins, self.in_specs = (x,), (ANYWHERE,)
        self.outs, self.out_specs = (jax.ShapeDtypeStruct((16 * tok, width), x.dtype),), (ANYWHERE,)
        self.scratch = (DMA((n, 7)), DMA((n, 7)), DMA((n, 8)), DMA((n, 8)), DMA)

    def stages(self, place, x_ref, o_ref, send, recv, psend, precv, local):
        orders = [order for _, order in self.plan]
        tok, width = x_ref.shape
        cols = part_columns(width, self.plan)

        def rows(r, other=0):
            return pl.ds(pl.multiple_of(place.index(r, other) * tok, tok), tok)

        def remote(src, r, p, dim):
            lo, n = cols[p]
            slot = r | dim
            return pltpu.make_async_remote_copy(
                src_ref=src, dst_ref=o_ref.at[rows(r), pl.ds(lo, n)],
                send_sem=send.at[p, slot - 1], recv_sem=recv.at[p, slot - 1],
                device_id=place.device(dim), device_id_type=MESH,
            )

        def pair(r, p):
            lo, n = cols[p]
            src = o_ref.at[rows(r), pl.ds(lo, n)]
            return pltpu.make_async_remote_copy(
                src_ref=src, dst_ref=src, send_sem=psend.at[p, r], recv_sem=precv.at[p, r],
                device_id=place.device(0, 1), device_id_type=MESH,
            )

        started = []
        own = [x_ref.at[:, pl.ds(lo, n)] for lo, n in cols]
        for step in range(3):
            for p in range(len(orders)):
                copy = remote(own[p], 0, p, orders[p][step])
                copy.start()
                started.append(copy)
        keep = pltpu.make_async_copy(x_ref, o_ref.at[rows(0)], local)
        keep.start()
        for p in range(len(orders)):
            lo, n = cols[p]
            copy = pltpu.make_async_remote_copy(
                src_ref=own[p], dst_ref=o_ref.at[rows(0), pl.ds(lo, n)], send_sem=psend.at[p, 0], recv_sem=precv.at[p, 0],
                device_id=place.device(0, 1), device_id_type=MESH,
            )
            copy.start()
            started.append(copy)

        def arrived(p, slot):
            lo, n = cols[p]
            ref = o_ref.at[rows(slot), pl.ds(lo, n)]
            pltpu.make_async_remote_copy(
                src_ref=ref, dst_ref=ref, send_sem=send.at[p, slot - 1], recv_sem=recv.at[p, slot - 1],
                device_id=place.device(X), device_id_type=MESH,
            ).wait_recv()

        for which in ((1, 0, 0), (0, 1, 0), (1, 1, 0), (0, 0, 1), (1, 0, 1), (0, 1, 1), (1, 1, 1)):
            yield
            for p in range(len(orders)):
                dims = orders[p]
                slot = sum(d for d, on in zip(dims, which) if on)
                arrived(p, slot)
                lo, n = cols[p]
                src = o_ref.at[rows(slot), pl.ds(lo, n)]
                top = max(j for j in range(3) if which[j])
                for j in range(top + 1, 3):
                    copy = remote(src, slot, p, dims[j])
                    copy.start()
                    started.append(copy)
                copy = pair(slot, p)
                copy.start()
                started.append(copy)
        for copy in started:
            copy.wait_send()
        for p in range(len(orders)):
            lo, n = cols[p]
            for r in range(8):
                ref = o_ref.at[rows(r, 1), pl.ds(lo, n)]
                pltpu.make_async_remote_copy(
                    src_ref=ref, dst_ref=ref, send_sem=psend.at[p, r], recv_sem=precv.at[p, r],
                    device_id=place.device(0, 1), device_id_type=MESH,
                ).wait_recv()
        keep.wait()


def gather_kernel(extras, trees, *refs):
    _, _, _, extra_refs = sorted_refs(extras, refs, 0, 0)
    place = Place(trees)
    greet(place, extras)
    running = [e.stages(place, *r) for e, r in zip(extras, extra_refs)]
    turn = sorted(zip(extras, running), key=lambda e: e[0].bulk)
    for _ in range(8):
        for _, stages in turn:
            next(stages, None)
    finish(place, extras, running)


def tree_gather(x, cid, name, plan=EVEN, extras=()):
    out = call(gather_kernel, tuple(extras) + (GatherRows(x, plan),), [], [], [], [], [], cid, name)
    return (out[-1], *out[:-1]) if extras else out


def scatter_kernel(plan, rhs_dim, tok, extras, trees, *refs):
    orders = [order[::-1] for _, order in plan]
    (l_ref, r_ref), (o_ref,), scratch, extra_refs = sorted_refs(extras, refs, 2, 1)
    acc, pout, pin, stage, inbox, psend, precv, send, recv = scratch
    place = Place(trees)
    width = o_ref.shape[1]
    cols = part_columns(width, plan)
    greet(place, extras)
    tile = 512

    running = [e.stages(place, *r) for e, r in zip(extras, extra_refs)]

    def advance():
        for stages in running:
            next(stages, None)

    advance()

    def product(zy, other, put):
        z, y, c, _ = place.flipped(zy, other)
        start = pl.multiple_of(((z * 2 + y) * 2 + c) * 2 * tok, 2 * tok)

        def one(j):
            at = pl.multiple_of(j * tile, tile)
            left = l_ref[pl.ds(start, 2 * tok), :]
            if rhs_dim == 1:
                res = lax.dot_general(left, r_ref[pl.ds(at, tile), pl.ds(0, l_ref.shape[1])], (((1,), (1,)), ((), ())), preferred_element_type=f32)
            else:
                res = lax.dot_general(left, r_ref[:, pl.ds(at, tile)], (((1,), (0,)), ((), ())), preferred_element_type=f32)
            put(at, res)

        pl.loop(0, width // tile)(one)

    def pair(k):
        return pltpu.make_async_remote_copy(
            src_ref=pout.at[k], dst_ref=pin.at[k], send_sem=psend.at[k], recv_sem=precv.at[k],
            device_id=place.device(0, 1), device_id_type=MESH,
        )

    groups = (Z | Y, Z, Y, 0)

    def for_partner(k):
        def put_out(at, res):
            pout[k, :, pl.ds(at, tile)] = res.astype(bf16)
        product(groups[k], 1, put_out)
        pair(k).start()

    for_partner(0)
    for_partner(1)

    def hop(p, r, step, slot):
        lo, n = cols[p]
        return pltpu.make_async_remote_copy(
            src_ref=stage.at[r - 1, :, pl.ds(lo, n)], dst_ref=inbox.at[slot, :, pl.ds(lo, n)],
            send_sem=send.at[p, r - 1], recv_sem=recv.at[p, slot],
            device_id=place.device(orders[p][step]), device_id_type=MESH,
        )

    started = []
    for k, zy in enumerate(groups):
        def put_own(at, res, k=k):
            acc[k, :, pl.ds(at, tile)] = res
        product(zy, 0, put_own)
        if k + 2 < len(groups):
            for_partner(k + 2)
        if k == 1:
            advance()
        pair(k).wait_recv()
        for rx in (X, 0):
            r = zy | rx
            xx = place.flipped(rx)[3]
            at = pl.ds(pl.multiple_of(xx * tok, tok), tok)
            for p in range(len(plan)):
                lo, n = cols[p]
                total = acc[k, at, pl.ds(lo, n)] + pin[k, at, pl.ds(lo, n)].astype(f32)
                first, second, third = orders[p]
                if r & first:
                    stage[r - 1, :, pl.ds(lo, n)] = total.astype(bf16)
                    slot = 3 - (2 * bool(r & second) + bool(r & third))
                    copy = hop(p, r, 0, slot)
                    copy.start()
                    started.append(copy)
                else:
                    acc[k, at, pl.ds(lo, n)] = total

    def held(p, r):
        k = groups.index(r & (Z | Y))
        xx = place.flipped(r & X)[3]
        lo, n = cols[p]
        return acc[k, pl.ds(pl.multiple_of(xx * tok, tok), tok), pl.ds(lo, n)]

    def take(p, slot):
        lo, n = cols[p]
        hop(p, 1, 0, slot).wait_recv()
        return inbox[slot, :, pl.ds(lo, n)].astype(f32)

    advance()
    for q in ((1, 1), (1, 0)):
        for p in range(len(plan)):
            first, second, third = orders[p]
            lo, n = cols[p]
            r = second + third * q[1]
            stage[r - 1, :, pl.ds(lo, n)] = (held(p, r) + take(p, 3 - (2 * q[0] + q[1]))).astype(bf16)
            copy = hop(p, r, 1, 4 + (1 - q[1]))
            copy.start()
            started.append(copy)
        advance()
    for p in range(len(plan)):
        third = orders[p][2]
        lo, n = cols[p]
        stage[third - 1, :, pl.ds(lo, n)] = (held(p, third) + take(p, 2) + take(p, 4)).astype(bf16)
        copy = hop(p, third, 2, 6)
        copy.start()
        started.append(copy)
    advance()
    for p in range(len(plan)):
        lo, n = cols[p]
        o_ref[:, pl.ds(lo, n)] = held(p, 0) + take(p, 3) + take(p, 5)
    for p in range(len(plan)):
        lo, n = cols[p]
        o_ref[:, pl.ds(lo, n)] += take(p, 6)
    advance()
    for copy in started:
        copy.wait_send()
    for k in range(4):
        pair(k).wait_send()
    finish(place, extras, running)


def product_scatter(left, right, rhs_dim, cid, name, plan=EVEN, extras=()):
    tokens, inner = left.shape
    width = right.shape[1 - rhs_dim]
    tok = tokens // 16
    n = len(plan)
    scratch = [
        pltpu.VMEM((4, 2 * tok, width), f32),
        pltpu.VMEM((4, 2 * tok, width), bf16),
        pltpu.VMEM((4, 2 * tok, width), bf16),
        pltpu.VMEM((7, tok, width), bf16),
        pltpu.VMEM((7, tok, width), bf16),
        DMA((4,)), DMA((4,)), DMA((n, 7)), DMA((n, 7)),
    ]
    return call(
        functools.partial(scatter_kernel, plan, rhs_dim, tok), extras, [left, right], [IN_VMEM, IN_VMEM],
        [jax.ShapeDtypeStruct((tok, width), f32)], [IN_VMEM],
        scratch, cid, name, 2 * tokens * width * inner, 56 * 2**20,
    )


def norm_stats(v):
    mean = jnp.mean(v, axis=-1, keepdims=True)
    centred = v - mean
    root = lax.rsqrt(jnp.mean(centred * centred, axis=-1, keepdims=True) + EPS)
    return centred * root, root


def norm_back(d, n, root, gain):
    g = d * gain
    return root * (g - jnp.mean(g, axis=-1, keepdims=True) - n * jnp.mean(g * n, axis=-1, keepdims=True))


def gelu_pair(u):
    c = (2.0 / jnp.pi) ** 0.5
    t = jnp.tanh(c * (u + 0.044715 * u * u * u))
    act = 0.5 * u * (1.0 + t)
    der = 0.5 * (1.0 + t) + 0.5 * u * (1.0 - t * t) * c * (1.0 + 3 * 0.044715 * u * u)
    return act, der


def own_rows(g, swapped, rows):
    share = swapped.shape[1]
    mine = lax.dynamic_slice_in_dim(g, lax.axis_index("tree") * share, share)
    if lax.axis_size("tree") > 1:
        mine = (mine.astype(f32) + jnp.sum(swapped.astype(f32), axis=0)).astype(bf16)
    return mine.reshape(TREE_SEGS, rows, -1)


def scores_of(qkv_ref, parent_ref, s, tok):
    hd = HEAD_DIM
    own = pl.ds(pl.multiple_of(s * tok, tok), tok)
    branches = [pl.ds((TRUNK_SEGS + b) * tok, tok) for b in range(4)]
    trunk = pl.ds(0, TRUNK_SEGS * tok)
    parent = parent_ref[s]

    def rows(col):
        up = qkv_ref[branches[0], col]
        for b in range(1, 4):
            up = jnp.where(parent == TRUNK_SEGS + b, qkv_ref[branches[b], col], up)
        return jnp.concatenate([qkv_ref[trunk, col], up, qkv_ref[own, col]], axis=0)

    q = qkv_ref[own, pl.ds(0, hd)]
    k, v = rows(pl.ds(hd, hd)), rows(pl.ds(2 * hd, hd))
    raw = dot(q, k, 1, 1) * HEAD_DIM ** -0.5
    n_trunk = TRUNK_SEGS * tok
    row = lax.broadcasted_iota(jnp.int32, raw.shape, 0)
    col = lax.broadcasted_iota(jnp.int32, raw.shape, 1)
    limit_up = jnp.where(s >= 2 * TRUNK_SEGS, n_trunk + tok, 0)
    limit_own = jnp.where(s >= TRUNK_SEGS, n_trunk + tok, -1)
    in_trunk = (col < n_trunk) & (col <= s * tok + row)
    in_up = (col >= n_trunk) & (col < limit_up)
    in_own = (col >= n_trunk + tok) & (col <= limit_own + row)
    seen = in_trunk | in_up | in_own
    raw = jnp.where(seen, raw, -jnp.inf)
    e = jnp.exp(raw - jnp.max(raw, axis=-1, keepdims=True))
    probs = e / jnp.sum(e, axis=-1, keepdims=True)
    return q, k, v, probs, own, trunk, branches, parent


def attend_kernel(extras, trees, *refs):
    own_in, own_out, (held,), extra_refs = sorted_refs(extras, refs, 6, 3)
    parent_ref, x_ref, gain_ref, bias_ref, w_ref, b_ref = own_in
    n_ref, qkv_ref, ctx_ref = own_out
    place = Place(trees)

    @pl.when(pl.program_id(0) == 0)
    def _():
        greet(place, extras)
        for e, r in zip(extras, extra_refs):
            e.start(place, *r)

    step = pl.program_id(0)
    rows = x_ref.shape[0]
    tok = held.shape[0] // TREE_SEGS
    n, _ = norm_stats(x_ref[...].astype(f32))
    norm = (n * gain_ref[...] + bias_ref[...]).astype(bf16)
    n_ref[...] = norm
    qkv = (dot(norm, w_ref[...], 1, 0) + b_ref[...]).astype(bf16)
    qkv_ref[...] = qkv
    held[pl.ds(pl.multiple_of(step * rows, rows), rows), :] = qkv

    @pl.when(step == pl.num_programs(0) - 1)
    def _():
        def one(s):
            _, _, v, probs, own, _, _, _ = scores_of(held, parent_ref, s, tok)
            ctx_ref[own, :] = dot(probs.astype(bf16), v, 1, 0).astype(bf16)

        pl.loop(0, TREE_SEGS, unroll=2)(one)
        for e, r in zip(extras, extra_refs):
            e.finish(place, *r)


def attend(parent, x_full, gain, bias, w, b, extras, cid):
    tokens, width = x_full.shape
    n = 3 * HEAD_DIM
    rows = 256
    whole = lambda shape: pl.BlockSpec(shape, lambda i: (0,) * len(shape))
    by_row = lambda cols: pl.BlockSpec((rows, cols), lambda i: (i, 0))
    return pl.pallas_call(
        functools.partial(attend_kernel, extras, lax.axis_size("tree")),
        grid=(tokens // rows,),
        in_specs=[
            pl.BlockSpec(memory_space=pltpu.SMEM), by_row(width), whole((1, width)), whole((1, width)), whole((width, n)),
            whole((1, n)), *[i for e in extras for i in e.in_specs],
        ],
        out_specs=[by_row(width), by_row(n), whole((tokens, HEAD_DIM)), *[o for e in extras for o in e.out_specs]],
        scratch_shapes=[*[i for e in extras for i in e.scratch], pltpu.VMEM((tokens, n), bf16)],
        out_shape=[
            jax.ShapeDtypeStruct((tokens, width), bf16),
            jax.ShapeDtypeStruct((tokens, n), bf16),
            jax.ShapeDtypeStruct((tokens, HEAD_DIM), bf16),
            *[o for e in extras for o in e.outs],
        ],
        compiler_params=pltpu.CompilerParams(collective_id=cid, has_side_effects=True, vmem_limit_bytes=58 * 2**20),
        cost_estimate=pl.CostEstimate(flops=2 * tokens * width * n, bytes_accessed=60_000_000, transcendentals=0),
        name="attend",
    )(parent, x_full, gain, bias, w, b, *[a for e in extras for a in e.ins])


def halves(v):
    high = v.astype(bf16)
    return high, (v - high.astype(f32)).astype(bf16)


def attend_back_kernel(extras, trees, *refs):
    own_in, own_out, own_scratch, extra_refs = sorted_refs(extras, refs, 6, 4)
    parent_ref, qkv_ref, d_ref, w_ref, w_qkv_ref, n_ref = own_in
    o_ref, g_ref, f_ref, s_ref = own_out
    dk, dv, d_ctx, held, sem = own_scratch
    place = Place(trees)
    step = pl.program_id(0)

    @pl.when(step == 0)
    def _():
        greet(place, extras)
        for e, r in zip(extras, extra_refs):
            e.start(place, *r)
        pltpu.make_async_copy(n_ref, held, sem).start()

    rows = d_ref.shape[0]
    tok = qkv_ref.shape[0] // TREE_SEGS
    hd = HEAD_DIM
    scale = HEAD_DIM ** -0.5
    d_ctx[pl.ds(pl.multiple_of(step * rows, rows), rows), :] = dot(d_ref[...], w_ref[...], 1, 1).astype(bf16)

    @pl.when(step == pl.num_programs(0) - 1)
    def _():
        dk[...] = jnp.zeros_like(dk)
        dv[...] = jnp.zeros_like(dv)

        def one(s):
            q, k, v, probs, own, trunk, branches, parent = scores_of(qkv_ref, parent_ref, s, tok)
            dc = d_ctx[own, :]
            dp = dot(dc, v, 1, 1)
            ds = (probs * (dp - jnp.sum(probs * dp, axis=-1, keepdims=True))).astype(bf16)
            o_ref[own, pl.ds(0, hd)] = (dot(ds, k, 1, 0) * scale).astype(bf16)
            gk = dot(ds, q, 0, 0)
            gv = dot(probs.astype(bf16), dc, 0, 0)
            n_trunk = TRUNK_SEGS * tok
            for acc, g in ((dk, gk), (dv, gv)):
                acc[trunk, :] += g[:n_trunk]
                for b in range(4):
                    acc[branches[b], :] += jnp.where(parent == TRUNK_SEGS + b, g[n_trunk : n_trunk + tok], 0.0)
                acc[own, :] += g[n_trunk + tok :]

        pl.loop(0, TREE_SEGS, unroll=2)(one)
        o_ref[:, pl.ds(hd, hd)] = (dk[...] * scale).astype(bf16)
        o_ref[:, pl.ds(2 * hd, hd)] = dv[...].astype(bf16)
        drain(held, sem)
        total = jnp.sum(o_ref[...].astype(f32).reshape(-1, 8, o_ref.shape[1]), axis=0)
        total = jnp.broadcast_to(jnp.sum(total, axis=0, keepdims=True), total.shape)
        s_ref[...] = total
        ones = jnp.ones(total.shape, bf16)
        block = 512
        for j in range(held.shape[1] // block):
            at = pl.ds(j * block, block)
            g = dot(held[:, at], o_ref[...], 0, 0)
            g_ref[at, :] = g.astype(bf16)
            w = w_qkv_ref[at, :]
            f_ref[pl.ds(0, 8), at] = sum(dot(ones, part, 1, 1) for part in halves(w.astype(f32) * g))
            f_ref[pl.ds(8, 8), at] = sum(dot(part, w, 1, 1) for part in halves(total))
        for e, r in zip(extras, extra_refs):
            e.finish(place, *r)


def attend_back(parent, qkv, d_full, w_rows, w_qkv, norm_one, extras, cid):
    tokens, width = d_full.shape
    n = qkv.shape[1]
    rows = 256
    whole = lambda shape: pl.BlockSpec(shape, lambda i: (0,) * len(shape))
    return pl.pallas_call(
        functools.partial(attend_back_kernel, extras, lax.axis_size("tree")),
        grid=(tokens // rows,),
        in_specs=[
            pl.BlockSpec(memory_space=pltpu.SMEM), whole((tokens, n)), pl.BlockSpec((rows, width), lambda i: (i, 0)),
            whole((HEAD_DIM, width)), whole((width, n)), ANYWHERE, *[i for e in extras for i in e.in_specs],
        ],
        out_specs=[whole((tokens, n)), whole((width, n)), whole((16, width)), whole((8, n)), *[o for e in extras for o in e.out_specs]],
        scratch_shapes=[
            *[i for e in extras for i in e.scratch],
            pltpu.VMEM((tokens, HEAD_DIM), f32), pltpu.VMEM((tokens, HEAD_DIM), f32), pltpu.VMEM((tokens, HEAD_DIM), bf16),
            pltpu.VMEM((tokens, width), bf16), DMA,
        ],
        out_shape=[
            jax.ShapeDtypeStruct((tokens, n), bf16), jax.ShapeDtypeStruct((width, n), bf16),
            jax.ShapeDtypeStruct((16, width), f32), jax.ShapeDtypeStruct((8, n), f32), *[o for e in extras for o in e.outs],
        ],
        compiler_params=pltpu.CompilerParams(collective_id=cid, has_side_effects=True, vmem_limit_bytes=58 * 2**20),
        cost_estimate=pl.CostEstimate(flops=2 * tokens * width * HEAD_DIM, bytes_accessed=60_000_000, transcendentals=0),
        name="attend_back",
    )(parent, qkv, d_full, w_rows, w_qkv, norm_one, *[a for e in extras for a in e.ins])


def feed_forward_kernel(n_ref, c_ref, wu_ref, wd_ref, b_ref, active_ref, d_ref, sum_ref):
    act, der = gelu_pair(dot(n_ref[...], wu_ref[...], 1, 0) + b_ref[...])
    active_ref[...] = act.astype(bf16)
    d = (dot(c_ref[...], wd_ref[...], 1, 0) * der).astype(bf16)
    d_ref[...] = d

    @pl.when(pl.program_id(0) == 0)
    def _():
        sum_ref[...] = jnp.zeros_like(sum_ref)

    sum_ref[...] += jnp.sum(d.astype(f32).reshape(-1, 8, d.shape[1]), axis=0)


def feed_forward(n_full, c_full, wu, wd, b):
    tokens, width = n_full.shape
    n = wu.shape[1]
    rows = 256
    whole = lambda shape: pl.BlockSpec(shape, lambda i: (0,) * len(shape))
    by_row = lambda cols: pl.BlockSpec((rows, cols), lambda i: (i, 0))
    return pl.pallas_call(
        feed_forward_kernel,
        grid=(tokens // rows,),
        in_specs=[by_row(width), by_row(width), whole((width, n)), whole((width, n)), whole((1, n))],
        out_specs=[by_row(n), by_row(n), whole((8, n))],
        out_shape=[jax.ShapeDtypeStruct((tokens, n), bf16)] * 2 + [jax.ShapeDtypeStruct((8, n), f32)],
        compiler_params=pltpu.CompilerParams(vmem_limit_bytes=40 * 2**20),
        cost_estimate=pl.CostEstimate(flops=4 * tokens * width * n, bytes_accessed=4 * tokens * width, transcendentals=0),
        name="feed_forward",
    )(n_full, c_full, wu, wd, b[None])


def last_kernel(*refs):
    dn_ref, x_ref, d_res_ref, gain_ref, res_ref, mlp_ref, b_ref, down_ref, *shares = refs[:13]
    grad_ref, out_ref, down_out, *sums = refs[13:]
    n, root = norm_stats(x_ref[...].astype(f32))
    grad_ref[...] = d_res_ref[...] + norm_back(dn_ref[...], n, root, gain_ref[...])
    out_ref[...] = (res_ref[...] + mlp_ref[...] + b_ref[...]).astype(bf16)
    down_out[...] = down_ref[...].astype(f32)
    for share, total in zip(shares, sums):
        total[...] = jnp.sum(share[...].astype(f32), axis=0)


def last(d_norm, x, d_res, gain, residual, mlp, b, g_down, shares):
    tok, width = x.shape
    steps = 4
    by_row = pl.BlockSpec((tok // steps, width), lambda i: (i, 0))
    vector = pl.BlockSpec((1, width), lambda i: (0, 0))
    by_column = lambda v: pl.BlockSpec((v.shape[0], v.shape[1] // steps), lambda i: (0, i))
    by_column_3 = lambda v: pl.BlockSpec(v.shape[:2] + (v.shape[2] // steps,), lambda i: (0, 0, i))
    flat = [jax.ShapeDtypeStruct(v.shape[1:], f32) for v in shares]
    return pl.pallas_call(
        last_kernel,
        grid=(steps,),
        in_specs=[by_row, by_row, by_row, vector, by_row, by_row, vector, by_column(g_down), *map(by_column_3, shares)],
        out_specs=[by_row, by_row, by_column(g_down), *map(by_column, flat)],
        out_shape=[
            jax.ShapeDtypeStruct((tok, width), f32), jax.ShapeDtypeStruct((tok, width), bf16),
            jax.ShapeDtypeStruct(g_down.shape, f32), *flat,
        ],
        compiler_params=pltpu.CompilerParams(vmem_limit_bytes=58 * 2**20),
        name="last",
    )(d_norm, x, d_res, gain[None], residual, mlp, b[None], g_down, *shares)


def body(
    inputs, gain_one, bias_one, w_query, b_query, w_key, w_value, b_value, w_out, b_out,
    gain_two, bias_two, w_up, b_up, w_down, b_down, parents, cotangent,
):
    tok, width = inputs.shape
    rows = w_query.shape[0]
    ff = w_up.shape[1]
    fs = ff // TREE_SEGS
    trees = lax.axis_size("tree")
    devices = trees * TREE_SEGS
    tree = lax.axis_index("tree")
    me = lax.axis_index(GROUP)
    head = lambda v: lax.dynamic_slice_in_dim(v, me * HEAD_DIM, HEAD_DIM)

    vectors = (gain_one, bias_one, b_query, b_value, b_out, gain_two, bias_two, b_down, b_up)
    n_small = sum(v.shape[0] for v in vectors)
    block = jnp.zeros((16 * 128,), bf16)
    at = 0
    for v in vectors:
        block = block + jnp.pad(v, (at, 16 * 128 - at - v.shape[0]))
        at += v.shape[0]
    block = block.reshape(16, 128)

    x_full, box, w_att = tree_gather(inputs, 0, "gather_inputs", FIRST, extras=(
        SpreadSmall(block), DealAll(w_query, w_key, w_value),
    ))
    w_att = w_att.reshape(width, -1)
    packed = box.transpose(1, 0, 2, 3).reshape(devices, -1)[:, :n_small]
    vecs = packed[:, : 8 * rows].reshape(devices, 8, rows).transpose(1, 0, 2).reshape(8, width).astype(f32)
    gain_one, bias_one, b_query, b_value, b_out, gain_two, bias_two, b_down = vecs
    b_up = packed[:, 8 * rows :].reshape(-1).astype(f32)

    local_seg = jnp.arange(TREE_SEGS, dtype=jnp.int32)
    own_parents = lax.dynamic_slice_in_dim(parents, tree * TREE_SEGS, TREE_SEGS) - tree * TREE_SEGS
    parent = jnp.where(local_seg >= 2 * TRUNK_SEGS, own_parents, local_seg)

    b_qkv = jnp.concatenate([head(b_query), jnp.zeros((HEAD_DIM,), f32), head(b_value)])
    norm_one, qkv, context, w_orow, share_up, share_down = attend(
        parent, x_full, gain_one[None], bias_one[None], w_att, b_qkv[None],
        (HeadRows(w_out), DealColumns(w_up), DealColumns(w_down)), 9
    )
    att, wd, c_full = product_scatter(context, w_orow, 0, 2, "scatter_attended", LIGHT, extras=(
        ToTrees(share_down.reshape(-1, fs)), GatherRows(cotangent, ROOM),
    ))
    wd = wd.reshape(width, fs)
    x_own = inputs.astype(f32)
    residual = x_own + att + b_out
    n_two, root_two = norm_stats(residual)
    norm_two = (n_two * gain_two + bias_two).astype(bf16)
    nt_full, wu = tree_gather(norm_two, 3, "gather_norm_two", LIGHT, extras=(ToTrees(share_up.reshape(-1, fs)),))
    wu = wu.reshape(width, fs)

    active, d_up, gb_up = feed_forward(nt_full, c_full, wu, wd, lax.dynamic_slice_in_dim(b_up, me * fs, fs))
    g_up = dot(nt_full, d_up, 0, 0).astype(bf16)
    d_norm_two, g_up, g_down = product_scatter(d_up, wu, 1, 4, "scatter_d_norm_two", MIXED, extras=(
        DealAllRows(g_up.reshape(devices, rows, fs), (fs,)), Product(c_full, active, 0, bf16),
    ))

    cot = cotangent.astype(f32)
    d_res = cot + norm_back(d_norm_two, n_two, root_two, gain_two)
    d_att = d_res.astype(bf16)
    mlp, swap_down, da_full = product_scatter(active, wd, 1, 5, "scatter_mlp", LIGHT, extras=(
        SwapTrees(g_down), GatherRows(d_att, ROOM),
    ))
    g_down = own_rows(g_down, swap_down, rows)
    g_orow = dot(context, da_full, 0, 0).astype(bf16)
    d_qkv, g_att, shares, s_qkv, g_down, g_o = attend_back(
        parent, qkv, da_full, w_orow, w_att, norm_one, (DealRows(g_down, (fs,)), HeadRowsBack(g_orow, rows)), 10
    )

    gb_one = shares[8]
    gg_one = (shares[0] - bias_one * gb_one) / gain_one
    s_qkv = s_qkv[0]

    def placed(vec, total):
        return lax.dynamic_update_slice_in_dim(jnp.zeros((total,), f32), vec, me * vec.shape[0], axis=0)

    col = lambda a: jnp.sum(a, axis=0)
    sums = [
        gg_one, gb_one, placed(s_qkv[:HEAD_DIM], width), placed(s_qkv[2 * HEAD_DIM :], width),
        col(d_att.astype(f32)), col(d_norm_two * n_two), col(d_norm_two), col(cot),
    ]
    sums = jnp.stack(sums).reshape(8, devices, rows).transpose(1, 0, 2).reshape(devices, 8 * rows)
    sums = jnp.concatenate([sums, placed(col(gb_up), ff).reshape(devices, -1)], axis=1)
    sums = jnp.pad(sums, ((0, 0), (0, 1024 - n_small))).reshape(trees, TREE_SEGS, 8, 128).transpose(1, 0, 2, 3)
    d_norm_one, sums, g_q, g_k, g_v = product_scatter(d_qkv, w_att, 1, 7, "scatter_d_norm_one", MIXED, extras=(
        ReduceSmall(sums), DealAllRows(g_att.reshape(devices, rows, -1), (HEAD_DIM,) * 3),
    ))
    sums = sums.reshape(-1)
    parts = [sums[j * rows : (j + 1) * rows] for j in range(8)]
    gb_up = sums[8 * rows : n_small]

    grad_inputs, layer_output, g_down, g_q, g_k, g_v, g_o, g_up = last(
        d_norm_one, inputs, d_res, gain_one, residual, mlp, b_down, g_down, (g_q, g_k, g_v, g_o, g_up)
    )
    return (
        layer_output, grad_inputs, parts[0], parts[1], g_q, parts[2], g_k, g_v, parts[3], g_o, parts[4],
        parts[5], parts[6], g_up, gb_up, g_down, parts[7],
    )


def solution(mesh):
    names = mesh.axis_names
    shape = mesh.devices.shape
    blk = TREE_SEGS // shape[1]
    inner = Mesh(mesh.devices.reshape(shape[0] // blk, blk, shape[1]), ALL)
    mat, vec = P(ALL, None), P(ALL)
    in_specs = (
        mat, vec, vec, mat, vec, mat, mat, vec, mat, vec, vec, vec, mat, vec, mat, vec, P(), mat,
    )
    out_specs = (
        mat, mat, vec, vec, mat, vec, mat, mat, vec, mat, vec, vec, vec, mat, vec, mat, vec,
    )
    return jax.shard_map(body, mesh=inner, in_specs=in_specs, out_specs=out_specs, check_vma=False)
```

```python
import functools

import jax
import jax.numpy as jnp
from jax import lax
from jax.experimental import pallas as pl
from jax.experimental.pallas import tpu as pltpu
from jax.sharding import Mesh, PartitionSpec as P

HEAD_DIM = 128
TRUNK_SEGS = 4
TREE_SEGS = 16
EPS = 1e-05
GROUP = ("blk", "rep")
ALL = ("tree", "blk", "rep")
f32 = jnp.float32
bf16 = jnp.bfloat16


def dot(a, b, ca, cb):
    return lax.dot_general(a, b, (((ca,), (cb,)), ((), ())), preferred_element_type=f32)


MESH = pl.DeviceIdType.MESH
X, Y, Z = 1, 2, 4
COMM_BYTES = 120_000_000
EVEN = ((6, (X, Y, Z)), (5, (Y, Z, X)), (5, (Z, X, Y)))
ROOM = ((8, (X, Z, Y)), (8, (Y, Z, X)))
LIGHT = ((7, (Z, X, Y)), (7, (Z, Y, X)), (2, (X, Y, Z)))
MIXED = ((6, (X, Z, Y)), (6, (Y, Z, X)), (2, (Z, X, Y)), (2, (Z, Y, X)))
FIRST = ((6, (Z, X, Y)), (6, (Z, Y, X)), (4, (X, Y, Z)))


class Place:
    def __init__(self, trees):
        self.trees = trees
        self.tree = lax.axis_index("tree")
        blk = lax.axis_index("blk")
        self.x = lax.axis_index("rep")
        self.c = lax.rem(blk, 2)
        self.y = lax.rem(blk // 2, 2)
        self.z = blk // 4
        self.at = blk * 2 + self.x
        self.flat = self.tree * TREE_SEGS + self.at
        self.closing = False

    def flipped(self, r, other=0):
        flip = lambda v, on: 1 - v if on else v
        return flip(self.z, r & Z), flip(self.y, r & Y), flip(self.c, other), flip(self.x, r & X)

    def device(self, r, other=0):
        z, y, c, x = self.flipped(r, other)
        return (self.tree, (z * 2 + y) * 2 + c, x)

    def index(self, r, other=0):
        z, y, c, x = self.flipped(r, other)
        return ((z * 2 + y) * 2 + c) * 2 + x

    def in_tree(self, k):
        return (lax.rem(self.tree + k, self.trees), self.at // 2, self.x)

    def peer(self, k):
        j = lax.rem(self.at + k, TREE_SEGS)
        return j, (self.tree, j // 2, lax.rem(j, 2))

    def of_flat(self, flat):
        j = lax.rem(flat, TREE_SEGS)
        return (flat // TREE_SEGS, j // 2, lax.rem(j, 2))


def signal(device):
    pl.semaphore_signal(pltpu.get_barrier_semaphore(), inc=1, device_id=device, device_id_type=MESH)


def greet(place, extras=()):
    count = 0
    if any(e.everyone for e in extras):
        devices = place.trees * TREE_SEGS
        pl.loop(1, devices)(lambda k: signal(place.of_flat(lax.rem(place.flat + k, devices))))
        pl.semaphore_wait(pltpu.get_barrier_semaphore(), devices - 1)
        return
    if any(e.peers for e in extras):
        pl.loop(1, TREE_SEGS)(lambda k: signal(place.peer(k)[1]))
        count += TREE_SEGS - 1
    else:
        for r, other in ((X, 0), (Y, 0), (Z, 0), (0, 1)):
            signal(place.device(r, other))
        count += 4
    if any(e.trees for e in extras):
        for k in range(1, place.trees):
            signal(place.in_tree(k))
        count += place.trees - 1
    for e in extras:
        count += e.greet(place)
    pl.semaphore_wait(pltpu.get_barrier_semaphore(), count)


def push(src, dst, send, recv, device):
    return pltpu.make_async_remote_copy(
        src_ref=src, dst_ref=dst, send_sem=send, recv_sem=recv, device_id=device, device_id_type=MESH
    )


def drain(ref, sem):
    pltpu.make_async_copy(ref, ref, sem).wait()


DMA = pltpu.SemaphoreType.DMA
ANYWHERE = pl.BlockSpec(memory_space=pl.ANY)
IN_VMEM = pl.BlockSpec(memory_space=pltpu.VMEM)


class Extra:
    peers = trees = everyone = False
    bulk = 2
    ins, in_specs, outs, out_specs, scratch = (), (), (), (), ()

    def greet(self, place):
        return 0


class SpreadSmall(Extra):
    trees = True
    bulk = 0

    def __init__(self, block):
        n = lax.axis_size("tree")
        self.ins, self.in_specs = (block,), (IN_VMEM,)
        self.outs, self.out_specs = (jax.ShapeDtypeStruct((16, n) + block.shape, block.dtype),), (IN_VMEM,)
        self.scratch = (DMA((14 + n,)), DMA((14 + n,)))

    def stages(self, place, src, box, send, recv):
        here = place.at
        box[here, place.tree] = src[...]
        new = []
        for k in range(1, place.trees):
            new.append(push(src, box.at[here, place.tree], send.at[14 + k], recv.at[14 + k], place.in_tree(k)))
            new[-1].start()
        done = list(new)
        yield
        held = [(0, 0)]
        for j, (bit, other) in enumerate(((X, 0), (Y, 0), (0, 1), (Z, 0))):
            for copy in new:
                copy.wait_recv()
            new = []
            for k, (r, o) in enumerate(held):
                block = box.at[place.index(r, o)]
                slot = (1 << j) - 1 + k
                new.append(push(block, block, send.at[slot], recv.at[slot], place.device(bit, other)))
                new[-1].start()
            held += [(r | bit, o | other) for r, o in held]
            done += new
            yield
        while not place.closing:
            yield
        for copy in new:
            copy.wait_recv()
        for copy in done:
            copy.wait_send()


class ReduceSmall(Extra):
    trees = True

    def __init__(self, sums):
        n = sums.shape[1]
        tail = sums.shape[2:]
        self.ins, self.in_specs = (sums,), (IN_VMEM,)
        self.outs, self.out_specs = (jax.ShapeDtypeStruct(tail, f32),), (IN_VMEM,)
        self.scratch = (
            pltpu.VMEM((TREE_SEGS,) + tail, f32), pltpu.VMEM((15,) + tail, f32),
            pltpu.VMEM((max(n - 1, 1), TREE_SEGS) + tail, f32), DMA((14 + n,)), DMA((14 + n,)),
        )

    def stages(self, place, src, out, acc, inbox, tbox, send, recv):
        far = []
        for k in range(1, place.trees):
            tree = lax.rem(place.tree + k, place.trees)
            far.append(push(src.at[:, tree], tbox.at[k - 1], send.at[14 + k], recv.at[14 + k], place.in_tree(k)))
            far[-1].start()
        yield
        for copy in far:
            copy.wait_recv()
        for j in range(TREE_SEGS):
            total = src[j, place.tree]
            for k in range(1, place.trees):
                total = total + tbox[k - 1, j]
            acc[j] = total
        left = [(r, o) for r in range(8) for o in range(2)]
        done = []
        for bit, other in ((0, 1), (X, 0), (Y, 0), (Z, 0)):
            new = []
            keep = [(r, o) for r, o in left if not (r & bit or o & other)]
            for r, o in keep:
                slot = len(done) + len(new)
                block = acc.at[place.index(r | bit, o | other)]
                new.append(push(block, inbox.at[slot], send.at[slot], recv.at[slot], place.device(bit, other)))
                new[-1].start()
            yield
            if bit == Z:
                while not place.closing:
                    yield
            for k, (r, o) in enumerate(keep):
                new[k].wait_recv()
                at = place.index(r, o)
                acc[at] = acc[at] + inbox[len(done) + k]
            done += new
            left = keep
        out[...] = acc[place.index(0)]
        for copy in far + done:
            copy.wait_send()


class ToTrees(Extra):
    trees = True

    def __init__(self, src):
        n = lax.axis_size("tree")
        self.ins, self.in_specs = (src,), (ANYWHERE,)
        self.outs, self.out_specs = (jax.ShapeDtypeStruct((n,) + src.shape, src.dtype),), (ANYWHERE,)
        self.scratch = (DMA((n,)), DMA((n,)))

    def stages(self, place, src, dst, send, recv):
        copies = [
            push(src, dst.at[place.tree], send.at[k - 1], recv.at[k - 1], place.in_tree(k)) for k in range(1, place.trees)
        ]
        copies.append(pltpu.make_async_copy(src, dst.at[place.tree], send.at[place.trees - 1]))
        for copy in copies:
            copy.start()
        while not place.closing:
            yield
        for copy in copies:
            copy.wait()


class SwapTrees(Extra):
    trees = True

    def __init__(self, src):
        n = lax.axis_size("tree")
        self.ins, self.in_specs = (src,), (ANYWHERE,)
        shape = (max(n - 1, 1), src.shape[0] // n) + src.shape[1:]
        self.outs, self.out_specs = (jax.ShapeDtypeStruct(shape, src.dtype),), (ANYWHERE,)
        self.scratch = (DMA((n,)), DMA((n,)))

    def stages(self, place, src, dst, send, recv):
        share = dst.shape[1]
        copies = []
        for k in range(1, place.trees):
            tree = lax.rem(place.tree + k, place.trees)
            rows = src.at[pl.ds(pl.multiple_of(tree * share, share), share)]
            copies.append(push(rows, dst.at[k - 1], send.at[k - 1], recv.at[k - 1], place.in_tree(k)))
            copies[-1].start()
        while not place.closing:
            yield
        for copy in copies:
            copy.wait()


class DealColumns(Extra):
    peers = True

    def __init__(self, mat):
        rows, c = mat.shape[0], mat.shape[1] // TREE_SEGS
        self.ins, self.in_specs = (mat,), (ANYWHERE,)
        self.outs, self.out_specs = (jax.ShapeDtypeStruct((TREE_SEGS, rows, c), bf16),), (ANYWHERE,)
        self.scratch = (DMA, DMA, DMA)

    def start(self, place, mat, out, send, recv, keep):
        c = out.shape[2]
        columns = lambda j: mat.at[:, pl.ds(pl.multiple_of(j * c, c), c)]

        def one(k):
            j, device = place.peer(k)
            push(columns(j), out.at[place.at], send, recv, device).start()

        pl.loop(1, TREE_SEGS)(one)
        pltpu.make_async_copy(columns(place.at), out.at[place.at], keep).start()

    def finish(self, place, mat, out, send, recv, keep):
        most = out.at[pl.ds(0, TREE_SEGS - 1)]
        drain(most, send)
        drain(most, recv)
        drain(out.at[0], keep)

    def stages(self, place, *refs):
        self.start(place, *refs)
        while not place.closing:
            yield
        self.finish(place, *refs)


class DealAll(Extra):
    everyone = True

    def __init__(self, *mats):
        devices = lax.axis_size("tree") * TREE_SEGS
        self.widths = [m.shape[1] // TREE_SEGS for m in mats]
        self.ins, self.in_specs = tuple(mats), (ANYWHERE,) * len(mats)
        self.outs = (jax.ShapeDtypeStruct((devices, mats[0].shape[0], sum(self.widths)), bf16),)
        self.out_specs = (ANYWHERE,)
        self.scratch = (DMA, DMA, DMA)

    def pieces(self, place, refs, tree, j):
        mats, out = refs[:-4], refs[-4]
        lo = 0
        for m, c in zip(mats, self.widths):
            yield m.at[:, pl.ds(pl.multiple_of(j * c, c), c)], out.at[place.flat, :, pl.ds(lo, c)]
            lo += c

    def blocks(self, refs):
        return refs[-4]

    def stages(self, place, *refs):
        send, recv, keep = refs[-3:]

        def one(tree, j):
            device = (tree, j // 2, lax.rem(j, 2))
            for src, dst in self.pieces(place, refs, tree, j):
                push(src, dst, send, recv, device).start()

        for k in range(1, place.trees):
            tree = lax.rem(place.tree + k, place.trees)
            pl.loop(0, TREE_SEGS)(lambda i: one(tree, lax.rem(place.at + i, TREE_SEGS)))
        pl.loop(1, TREE_SEGS)(lambda i: one(place.tree, lax.rem(place.at + i, TREE_SEGS)))
        for src, dst in self.pieces(place, refs, place.tree, place.at):
            pltpu.make_async_copy(src, dst, keep).start()
        while not place.closing:
            yield
        whole = self.blocks(refs)
        most = whole.at[pl.ds(0, whole.shape[0] - 1)]
        drain(most, send)
        drain(most, recv)
        drain(whole.at[0], keep)


class DealAllRows(DealAll):
    def __init__(self, src, widths):
        self.widths = widths
        rows = src.shape[1]
        self.ins, self.in_specs = (src,), (ANYWHERE,)
        shape = lambda c: (src.shape[0] // TREE_SEGS, rows, TREE_SEGS * c)
        self.outs = tuple(jax.ShapeDtypeStruct(shape(c), bf16) for c in widths)
        self.out_specs = (ANYWHERE,) * len(widths)
        self.scratch = (DMA, DMA, DMA)

    def pieces(self, place, refs, tree, j):
        src, outs = refs[0], refs[1:-3]
        lo = 0
        for out, c in zip(outs, self.widths):
            columns = pl.ds(pl.multiple_of(place.at * c, c), c)
            yield src.at[tree * TREE_SEGS + j, :, pl.ds(lo, c)], out.at[place.tree, :, columns]
            lo += c

    def blocks(self, refs):
        return refs[0]


class DealRows(Extra):
    peers = True

    def __init__(self, src, widths):
        self.widths = widths
        rows = src.shape[1]
        self.ins, self.in_specs = (src,), (ANYWHERE,)
        self.outs = tuple(jax.ShapeDtypeStruct((rows, TREE_SEGS * c), bf16) for c in widths)
        self.out_specs = (ANYWHERE,) * len(widths)
        self.scratch = (DMA, DMA, DMA)

    def start(self, place, src, *refs):
        outs, (send, recv, keep) = refs[:-3], refs[-3:]

        def pieces(j):
            lo = 0
            for out, c in zip(outs, self.widths):
                yield src.at[j, :, pl.ds(lo, c)], out.at[:, pl.ds(pl.multiple_of(place.at * c, c), c)]
                lo += c

        def one(k):
            j, device = place.peer(k)
            for block, dst in pieces(j):
                push(block, dst, send, recv, device).start()

        pl.loop(1, TREE_SEGS)(one)
        for block, dst in pieces(place.at):
            pltpu.make_async_copy(block, dst, keep).start()

    def finish(self, place, src, *refs):
        send, recv, keep = refs[-3:]
        most = src.at[pl.ds(0, TREE_SEGS - 1)]
        drain(most, send)
        drain(most, recv)
        drain(src.at[0], keep)

    def stages(self, place, *refs):
        self.start(place, *refs)
        while not place.closing:
            yield
        self.finish(place, *refs)


class HeadRows(Extra):
    def __init__(self, shard):
        self.rows = shard.shape[0]
        self.ins, self.in_specs = (shard,), (ANYWHERE,)
        self.outs = (jax.ShapeDtypeStruct((HEAD_DIM, shard.shape[1]), shard.dtype),)
        self.out_specs = (ANYWHERE,)
        self.scratch = (DMA((lax.axis_size("tree"),)), DMA)

    def greet(self, place):
        per_head = HEAD_DIM // self.rows
        for b in range(per_head):
            signal(place.of_flat(place.at * per_head + b))
        return place.trees

    def each(self, place, src, out, send, recv, do_far, do_own):
        at = place.flat * self.rows
        head = at // HEAD_DIM
        dst = out.at[pl.ds(pl.multiple_of(lax.rem(at, HEAD_DIM), self.rows), self.rows)]
        for t in range(place.trees):
            own = (place.tree == t) & (place.at == head)
            pl.when(jnp.logical_not(own))(lambda t=t: do_far(
                push(src, dst, send.at[t], recv, (t, head // 2, lax.rem(head, 2)))
            ))
            if do_own:
                pl.when(own)(lambda: do_own(pltpu.make_async_copy(src, dst, recv)))

    def start(self, place, *refs):
        self.each(place, *refs, lambda copy: copy.start(), lambda copy: copy.start())

    def finish(self, place, *refs):
        self.each(place, *refs, lambda copy: copy.wait_send(), None)
        drain(refs[1], refs[3])


class HeadRowsBack(Extra):
    def __init__(self, width, rows):
        self.rows = rows
        n = lax.axis_size("tree")
        self.outs, self.out_specs = (jax.ShapeDtypeStruct((n, rows, width), bf16),), (ANYWHERE,)
        self.scratch = (DMA((HEAD_DIM // rows,)), DMA)

    def greet(self, place):
        head = place.flat * self.rows // HEAD_DIM
        for t in range(place.trees):
            signal((t, head // 2, lax.rem(head, 2)))
        return HEAD_DIM // self.rows

    def each(self, place, src, out, send, recv, do_far, do_own):
        per_head = HEAD_DIM // self.rows
        for b in range(per_head):
            flat = place.at * per_head + b
            own = place.flat == flat
            block, dst = src.at[pl.ds(b * self.rows, self.rows)], out.at[place.tree]
            pl.when(jnp.logical_not(own))(lambda b=b, block=block, dst=dst, flat=flat: do_far(
                push(block, dst, send.at[b], recv, place.of_flat(flat))
            ))
            if do_own:
                pl.when(own)(lambda block=block, dst=dst: do_own(pltpu.make_async_copy(block, dst, recv)))

    def start(self, place, *refs):
        self.each(place, *refs, lambda copy: copy.start(), lambda copy: copy.start())

    def finish(self, place, *refs):
        self.each(place, *refs, lambda copy: copy.wait_send(), None)
        drain(refs[1], refs[3])


class Product(Extra):
    def __init__(self, left, right, dim, kind):
        self.dim = dim
        m, n = left.shape[1 - dim], right.shape[1]
        self.ins, self.in_specs = (left, right), (ANYWHERE, IN_VMEM)
        self.outs, self.out_specs = (jax.ShapeDtypeStruct((m, n), kind),), (IN_VMEM,)
        self.scratch = (pltpu.VMEM(left.shape, left.dtype), DMA)

    def stages(self, place, left, right, out, held, sem):
        copy = pltpu.make_async_copy(left, held, sem)
        copy.start()
        yield
        copy.wait()
        count = 4
        block = out.shape[0] // count
        for j in range(count):
            at = pl.ds(j * block, block)
            part = held[at, :] if self.dim == 1 else held[:, at]
            out[at, :] = dot(part, right[...], self.dim, 0).astype(out.dtype)
            yield


def finish(place, extras, running):
    place.closing = True
    order = [s for e, s in zip(extras, running) if isinstance(e, GatherRows)]
    order += [s for s in running if s not in order]
    for stages in order:
        for _ in stages:
            pass


def sorted_refs(extras, refs, n_in, n_out):
    refs = list(refs)
    take = lambda n: [refs.pop(0) for _ in range(n)]
    own_in, ins = take(n_in), [take(len(e.ins)) for e in extras]
    own_out, outs = take(n_out), [take(len(e.outs)) for e in extras]
    scratch = [take(len(e.scratch)) for e in extras]
    return own_in, own_out, refs, [i + o + s for i, o, s in zip(ins, outs, scratch)]


def call(kernel, extras, args, in_specs, out_shape, out_specs, scratch, cid, name, flops=0, vmem=None):
    out = pl.pallas_call(
        functools.partial(kernel, extras, lax.axis_size("tree")),
        out_shape=out_shape + [o for e in extras for o in e.outs],
        in_specs=in_specs + [i for e in extras for i in e.in_specs],
        out_specs=out_specs + [o for e in extras for o in e.out_specs],
        scratch_shapes=[i for e in extras for i in e.scratch] + scratch,
        compiler_params=pltpu.CompilerParams(collective_id=cid, has_side_effects=True, vmem_limit_bytes=vmem),
        cost_estimate=pl.CostEstimate(flops=flops, bytes_accessed=COMM_BYTES, transcendentals=0),
        name=name,
    )(*args, *[a for e in extras for a in e.ins])
    return out if len(out) > 1 else out[0]


def part_columns(width, plan):
    cuts = [0]
    for share, _ in plan:
        cuts.append(cuts[-1] + share * width // 16)
    return [(cuts[p], cuts[p + 1] - cuts[p]) for p in range(len(plan))]


class GatherRows(Extra):
    bulk = 1

    def __init__(self, x, plan):
        tok, width = x.shape
        self.plan = plan
        n = len(plan)
        self.ins, self.in_specs = (x,), (ANYWHERE,)
        self.outs, self.out_specs = (jax.ShapeDtypeStruct((16 * tok, width), x.dtype),), (ANYWHERE,)
        self.scratch = (DMA((n, 7)), DMA((n, 7)), DMA((n, 8)), DMA((n, 8)), DMA)

    def stages(self, place, x_ref, o_ref, send, recv, psend, precv, local):
        orders = [order for _, order in self.plan]
        tok, width = x_ref.shape
        cols = part_columns(width, self.plan)

        def rows(r, other=0):
            return pl.ds(pl.multiple_of(place.index(r, other) * tok, tok), tok)

        def remote(src, r, p, dim):
            lo, n = cols[p]
            slot = r | dim
            return pltpu.make_async_remote_copy(
                src_ref=src, dst_ref=o_ref.at[rows(r), pl.ds(lo, n)],
                send_sem=send.at[p, slot - 1], recv_sem=recv.at[p, slot - 1],
                device_id=place.device(dim), device_id_type=MESH,
            )

        def pair(r, p):
            lo, n = cols[p]
            src = o_ref.at[rows(r), pl.ds(lo, n)]
            return pltpu.make_async_remote_copy(
                src_ref=src, dst_ref=src, send_sem=psend.at[p, r], recv_sem=precv.at[p, r],
                device_id=place.device(0, 1), device_id_type=MESH,
            )

        started = []
        own = [x_ref.at[:, pl.ds(lo, n)] for lo, n in cols]
        for step in range(3):
            for p in range(len(orders)):
                copy = remote(own[p], 0, p, orders[p][step])
                copy.start()
                started.append(copy)
        keep = pltpu.make_async_copy(x_ref, o_ref.at[rows(0)], local)
        keep.start()
        for p in range(len(orders)):
            lo, n = cols[p]
            copy = pltpu.make_async_remote_copy(
                src_ref=own[p], dst_ref=o_ref.at[rows(0), pl.ds(lo, n)], send_sem=psend.at[p, 0], recv_sem=precv.at[p, 0],
                device_id=place.device(0, 1), device_id_type=MESH,
            )
            copy.start()
            started.append(copy)

        def arrived(p, slot):
            lo, n = cols[p]
            ref = o_ref.at[rows(slot), pl.ds(lo, n)]
            pltpu.make_async_remote_copy(
                src_ref=ref, dst_ref=ref, send_sem=send.at[p, slot - 1], recv_sem=recv.at[p, slot - 1],
                device_id=place.device(X), device_id_type=MESH,
            ).wait_recv()

        for which in ((1, 0, 0), (0, 1, 0), (1, 1, 0), (0, 0, 1), (1, 0, 1), (0, 1, 1), (1, 1, 1)):
            yield
            for p in range(len(orders)):
                dims = orders[p]
                slot = sum(d for d, on in zip(dims, which) if on)
                arrived(p, slot)
                lo, n = cols[p]
                src = o_ref.at[rows(slot), pl.ds(lo, n)]
                top = max(j for j in range(3) if which[j])
                for j in range(top + 1, 3):
                    copy = remote(src, slot, p, dims[j])
                    copy.start()
                    started.append(copy)
                copy = pair(slot, p)
                copy.start()
                started.append(copy)
        for copy in started:
            copy.wait_send()
        for p in range(len(orders)):
            lo, n = cols[p]
            for r in range(8):
                ref = o_ref.at[rows(r, 1), pl.ds(lo, n)]
                pltpu.make_async_remote_copy(
                    src_ref=ref, dst_ref=ref, send_sem=psend.at[p, r], recv_sem=precv.at[p, r],
                    device_id=place.device(0, 1), device_id_type=MESH,
                ).wait_recv()
        keep.wait()


def gather_kernel(extras, trees, *refs):
    _, _, _, extra_refs = sorted_refs(extras, refs, 0, 0)
    place = Place(trees)
    greet(place, extras)
    running = [e.stages(place, *r) for e, r in zip(extras, extra_refs)]
    turn = sorted(zip(extras, running), key=lambda e: e[0].bulk)
    for _ in range(8):
        for _, stages in turn:
            next(stages, None)
    finish(place, extras, running)


def tree_gather(x, cid, name, plan=EVEN, extras=()):
    out = call(gather_kernel, tuple(extras) + (GatherRows(x, plan),), [], [], [], [], [], cid, name)
    return (out[-1], *out[:-1]) if extras else out


def scatter_kernel(plan, rhs_dim, tok, extras, trees, *refs):
    orders = [order[::-1] for _, order in plan]
    (l_ref, r_ref), (o_ref,), scratch, extra_refs = sorted_refs(extras, refs, 2, 1)
    acc, pout, pin, stage, inbox, psend, precv, send, recv = scratch
    place = Place(trees)
    width = o_ref.shape[1]
    cols = part_columns(width, plan)
    greet(place, extras)
    tile = 512

    running = [e.stages(place, *r) for e, r in zip(extras, extra_refs)]

    def advance():
        for stages in running:
            next(stages, None)

    advance()

    def product(zy, other, put):
        z, y, c, _ = place.flipped(zy, other)
        start = pl.multiple_of(((z * 2 + y) * 2 + c) * 2 * tok, 2 * tok)

        def one(j):
            at = pl.multiple_of(j * tile, tile)
            left = l_ref[pl.ds(start, 2 * tok), :]
            if rhs_dim == 1:
                res = lax.dot_general(left, r_ref[pl.ds(at, tile), pl.ds(0, l_ref.shape[1])], (((1,), (1,)), ((), ())), preferred_element_type=f32)
            else:
                res = lax.dot_general(left, r_ref[:, pl.ds(at, tile)], (((1,), (0,)), ((), ())), preferred_element_type=f32)
            put(at, res)

        pl.loop(0, width // tile)(one)

    def pair(k):
        return pltpu.make_async_remote_copy(
            src_ref=pout.at[k], dst_ref=pin.at[k], send_sem=psend.at[k], recv_sem=precv.at[k],
            device_id=place.device(0, 1), device_id_type=MESH,
        )

    groups = (Z | Y, Z, Y, 0)

    def for_partner(k):
        def put_out(at, res):
            pout[k, :, pl.ds(at, tile)] = res.astype(bf16)
        product(groups[k], 1, put_out)
        pair(k).start()

    for_partner(0)
    for_partner(1)

    def hop(p, r, step, slot):
        lo, n = cols[p]
        return pltpu.make_async_remote_copy(
            src_ref=stage.at[r - 1, :, pl.ds(lo, n)], dst_ref=inbox.at[slot, :, pl.ds(lo, n)],
            send_sem=send.at[p, r - 1], recv_sem=recv.at[p, slot],
            device_id=place.device(orders[p][step]), device_id_type=MESH,
        )

    started = []
    for k, zy in enumerate(groups):
        def put_own(at, res, k=k):
            acc[k, :, pl.ds(at, tile)] = res
        product(zy, 0, put_own)
        if k + 2 < len(groups):
            for_partner(k + 2)
        if k == 1:
            advance()
        pair(k).wait_recv()
        for rx in (X, 0):
            r = zy | rx
            xx = place.flipped(rx)[3]
            at = pl.ds(pl.multiple_of(xx * tok, tok), tok)
            for p in range(len(plan)):
                lo, n = cols[p]
                total = acc[k, at, pl.ds(lo, n)] + pin[k, at, pl.ds(lo, n)].astype(f32)
                first, second, third = orders[p]
                if r & first:
                    stage[r - 1, :, pl.ds(lo, n)] = total.astype(bf16)
                    slot = 3 - (2 * bool(r & second) + bool(r & third))
                    copy = hop(p, r, 0, slot)
                    copy.start()
                    started.append(copy)
                else:
                    acc[k, at, pl.ds(lo, n)] = total

    def held(p, r):
        k = groups.index(r & (Z | Y))
        xx = place.flipped(r & X)[3]
        lo, n = cols[p]
        return acc[k, pl.ds(pl.multiple_of(xx * tok, tok), tok), pl.ds(lo, n)]

    def take(p, slot):
        lo, n = cols[p]
        hop(p, 1, 0, slot).wait_recv()
        return inbox[slot, :, pl.ds(lo, n)].astype(f32)

    advance()
    for q in ((1, 1), (1, 0)):
        for p in range(len(plan)):
            first, second, third = orders[p]
            lo, n = cols[p]
            r = second + third * q[1]
            stage[r - 1, :, pl.ds(lo, n)] = (held(p, r) + take(p, 3 - (2 * q[0] + q[1]))).astype(bf16)
            copy = hop(p, r, 1, 4 + (1 - q[1]))
            copy.start()
            started.append(copy)
        advance()
    for p in range(len(plan)):
        third = orders[p][2]
        lo, n = cols[p]
        stage[third - 1, :, pl.ds(lo, n)] = (held(p, third) + take(p, 2) + take(p, 4)).astype(bf16)
        copy = hop(p, third, 2, 6)
        copy.start()
        started.append(copy)
    advance()
    for p in range(len(plan)):
        lo, n = cols[p]
        o_ref[:, pl.ds(lo, n)] = held(p, 0) + take(p, 3) + take(p, 5)
    for p in range(len(plan)):
        lo, n = cols[p]
        o_ref[:, pl.ds(lo, n)] += take(p, 6)
    advance()
    for copy in started:
        copy.wait_send()
    for k in range(4):
        pair(k).wait_send()
    finish(place, extras, running)


def product_scatter(left, right, rhs_dim, cid, name, plan=EVEN, extras=()):
    tokens, inner = left.shape
    width = right.shape[1 - rhs_dim]
    tok = tokens // 16
    n = len(plan)
    scratch = [
        pltpu.VMEM((4, 2 * tok, width), f32),
        pltpu.VMEM((4, 2 * tok, width), bf16),
        pltpu.VMEM((4, 2 * tok, width), bf16),
        pltpu.VMEM((7, tok, width), bf16),
        pltpu.VMEM((7, tok, width), bf16),
        DMA((4,)), DMA((4,)), DMA((n, 7)), DMA((n, 7)),
    ]
    return call(
        functools.partial(scatter_kernel, plan, rhs_dim, tok), extras, [left, right], [IN_VMEM, IN_VMEM],
        [jax.ShapeDtypeStruct((tok, width), f32)], [IN_VMEM],
        scratch, cid, name, 2 * tokens * width * inner, 56 * 2**20,
    )


def norm_stats(v):
    mean = jnp.mean(v, axis=-1, keepdims=True)
    centred = v - mean
    root = lax.rsqrt(jnp.mean(centred * centred, axis=-1, keepdims=True) + EPS)
    return centred * root, root


def norm_back(d, n, root, gain):
    g = d * gain
    return root * (g - jnp.mean(g, axis=-1, keepdims=True) - n * jnp.mean(g * n, axis=-1, keepdims=True))


def gelu_pair(u):
    c = (2.0 / jnp.pi) ** 0.5
    t = jnp.tanh(c * (u + 0.044715 * u * u * u))
    act = 0.5 * u * (1.0 + t)
    der = 0.5 * (1.0 + t) + 0.5 * u * (1.0 - t * t) * c * (1.0 + 3 * 0.044715 * u * u)
    return act, der


def own_rows(g, swapped, rows):
    share = swapped.shape[1]
    mine = lax.dynamic_slice_in_dim(g, lax.axis_index("tree") * share, share)
    if lax.axis_size("tree") > 1:
        mine = (mine.astype(f32) + jnp.sum(swapped.astype(f32), axis=0)).astype(bf16)
    return mine.reshape(TREE_SEGS, rows, -1)


def scores_of(qkv_ref, parent_ref, s, tok):
    hd = HEAD_DIM
    own = pl.ds(pl.multiple_of(s * tok, tok), tok)
    branches = [pl.ds((TRUNK_SEGS + b) * tok, tok) for b in range(4)]
    trunk = pl.ds(0, TRUNK_SEGS * tok)
    parent = parent_ref[s]

    def rows(col):
        up = qkv_ref[branches[0], col]
        for b in range(1, 4):
            up = jnp.where(parent == TRUNK_SEGS + b, qkv_ref[branches[b], col], up)
        return jnp.concatenate([qkv_ref[trunk, col], up, qkv_ref[own, col]], axis=0)

    q = qkv_ref[own, pl.ds(0, hd)]
    k, v = rows(pl.ds(hd, hd)), rows(pl.ds(2 * hd, hd))
    raw = dot(q, k, 1, 1) * HEAD_DIM ** -0.5
    n_trunk = TRUNK_SEGS * tok
    row = lax.broadcasted_iota(jnp.int32, raw.shape, 0)
    col = lax.broadcasted_iota(jnp.int32, raw.shape, 1)
    limit_up = jnp.where(s >= 2 * TRUNK_SEGS, n_trunk + tok, 0)
    limit_own = jnp.where(s >= TRUNK_SEGS, n_trunk + tok, -1)
    in_trunk = (col < n_trunk) & (col <= s * tok + row)
    in_up = (col >= n_trunk) & (col < limit_up)
    in_own = (col >= n_trunk + tok) & (col <= limit_own + row)
    seen = in_trunk | in_up | in_own
    raw = jnp.where(seen, raw, -jnp.inf)
    e = jnp.exp(raw - jnp.max(raw, axis=-1, keepdims=True))
    probs = e / jnp.sum(e, axis=-1, keepdims=True)
    return q, k, v, probs, own, trunk, branches, parent


def attend_kernel(extras, trees, *refs):
    own_in, own_out, (held,), extra_refs = sorted_refs(extras, refs, 4, 3)
    parent_ref, x_ref, vecs_ref, w_ref = own_in
    n_ref, qkv_ref, ctx_ref = own_out
    place = Place(trees)

    @pl.when(pl.program_id(0) == 0)
    def _():
        greet(place, extras)
        for e, r in zip(extras, extra_refs):
            e.start(place, *r)

    step = pl.program_id(0)
    rows = x_ref.shape[0]
    tok = held.shape[0] // TREE_SEGS
    n, _ = norm_stats(x_ref[...].astype(f32))
    norm = (n * vecs_ref[pl.ds(0, 1), :] + vecs_ref[pl.ds(1, 1), :]).astype(bf16)
    n_ref[...] = norm
    head = pl.ds(pl.multiple_of(place.at * HEAD_DIM, HEAD_DIM), HEAD_DIM)
    b_query, b_value = vecs_ref[pl.ds(2, 1), head], vecs_ref[pl.ds(3, 1), head]
    b = jnp.concatenate([b_query, jnp.zeros_like(b_query), b_value], axis=1)
    qkv = (dot(norm, w_ref[...], 1, 0) + b).astype(bf16)
    qkv_ref[...] = qkv
    held[pl.ds(pl.multiple_of(step * rows, rows), rows), :] = qkv

    @pl.when(step == pl.num_programs(0) - 1)
    def _():
        def one(s):
            _, _, v, probs, own, _, _, _ = scores_of(held, parent_ref, s, tok)
            ctx_ref[own, :] = dot(probs.astype(bf16), v, 1, 0).astype(bf16)

        pl.loop(0, TREE_SEGS, unroll=2)(one)
        for e, r in zip(extras, extra_refs):
            e.finish(place, *r)


def attend(parent, x_full, vecs, w, extras, cid):
    tokens, width = x_full.shape
    n = 3 * HEAD_DIM
    rows = 256
    whole = lambda shape: pl.BlockSpec(shape, lambda i: (0,) * len(shape))
    by_row = lambda cols: pl.BlockSpec((rows, cols), lambda i: (i, 0))
    return pl.pallas_call(
        functools.partial(attend_kernel, extras, lax.axis_size("tree")),
        grid=(tokens // rows,),
        in_specs=[
            pl.BlockSpec(memory_space=pltpu.SMEM), by_row(width), whole(vecs.shape), whole((width, n)), *[i for e in extras for i in e.in_specs],
        ],
        out_specs=[by_row(width), by_row(n), whole((tokens, HEAD_DIM)), *[o for e in extras for o in e.out_specs]],
        scratch_shapes=[*[i for e in extras for i in e.scratch], pltpu.VMEM((tokens, n), bf16)],
        out_shape=[
            jax.ShapeDtypeStruct((tokens, width), bf16),
            jax.ShapeDtypeStruct((tokens, n), bf16),
            jax.ShapeDtypeStruct((tokens, HEAD_DIM), bf16),
            *[o for e in extras for o in e.outs],
        ],
        compiler_params=pltpu.CompilerParams(collective_id=cid, has_side_effects=True, vmem_limit_bytes=58 * 2**20),
        cost_estimate=pl.CostEstimate(flops=2 * tokens * width * n, bytes_accessed=60_000_000, transcendentals=0),
        name="attend",
    )(parent, x_full, vecs, w, *[a for e in extras for a in e.ins])


def halves(v):
    high = v.astype(bf16)
    return high, (v - high.astype(f32)).astype(bf16)


def attend_back_kernel(extras, trees, *refs):
    own_in, own_out, own_scratch, extra_refs = sorted_refs(extras, refs, 7, 3)
    parent_ref, qkv_ref, d_ref, w_ref, w_qkv_ref, ctx_ref, n_ref = own_in
    o_ref, g_ref, f_ref = own_out
    dk, dv, d_ctx, held, sem, g_rows, g_rows_low = own_scratch
    *soon, later = list(zip(extras, extra_refs))
    place = Place(trees)
    step = pl.program_id(0)

    @pl.when(step == 0)
    def _():
        greet(place, extras)
        for e, r in soon:
            e.start(place, *r)
        g_rows[...] = jnp.zeros_like(g_rows)
        pltpu.make_async_copy(n_ref, held, sem).start()

    rows = d_ref.shape[0]
    tok = qkv_ref.shape[0] // TREE_SEGS
    hd = HEAD_DIM
    scale = HEAD_DIM ** -0.5
    d_ctx[pl.ds(pl.multiple_of(step * rows, rows), rows), :] = dot(d_ref[...], w_ref[...], 1, 1).astype(bf16)
    tile = 512
    for j in range(d_ref.shape[1] // tile):
        at = pl.ds(j * tile, tile)
        g_rows[:, at] += dot(ctx_ref[...], d_ref[:, at], 0, 0)

    @pl.when(step == pl.num_programs(0) - 1)
    def _():
        g_rows_low[...] = g_rows[...].astype(bf16)
        later[0].start(place, g_rows_low, *later[1])
        dk[...] = jnp.zeros_like(dk)
        dv[...] = jnp.zeros_like(dv)

        def one(s):
            q, k, v, probs, own, trunk, branches, parent = scores_of(qkv_ref, parent_ref, s, tok)
            dc = d_ctx[own, :]
            dp = dot(dc, v, 1, 1)
            ds = (probs * (dp - jnp.sum(probs * dp, axis=-1, keepdims=True))).astype(bf16)
            o_ref[own, pl.ds(0, hd)] = (dot(ds, k, 1, 0) * scale).astype(bf16)
            gk = dot(ds, q, 0, 0)
            gv = dot(probs.astype(bf16), dc, 0, 0)
            n_trunk = TRUNK_SEGS * tok
            for acc, g in ((dk, gk), (dv, gv)):
                acc[trunk, :] += g[:n_trunk]
                for b in range(4):
                    acc[branches[b], :] += jnp.where(parent == TRUNK_SEGS + b, g[n_trunk : n_trunk + tok], 0.0)
                acc[own, :] += g[n_trunk + tok :]

        pl.loop(0, TREE_SEGS, unroll=2)(one)
        o_ref[:, pl.ds(hd, hd)] = (dk[...] * scale).astype(bf16)
        o_ref[:, pl.ds(2 * hd, hd)] = dv[...].astype(bf16)
        drain(held, sem)
        total = jnp.sum(o_ref[...].astype(f32).reshape(-1, 8, o_ref.shape[1]), axis=0)
        total = jnp.broadcast_to(jnp.sum(total, axis=0, keepdims=True), total.shape)
        f_ref[pl.ds(16, 16), :] = jnp.zeros((16, f_ref.shape[1]), f32)
        head = pl.ds(pl.multiple_of(place.at * hd, hd), hd)
        f_ref[pl.ds(16, 8), head] = total[:, :hd]
        f_ref[pl.ds(24, 8), head] = total[:, 2 * hd :]
        ones = jnp.ones(total.shape, bf16)
        block = 512
        for j in range(held.shape[1] // block):
            at = pl.ds(j * block, block)
            g = dot(held[:, at], o_ref[...], 0, 0)
            g_ref[at, :] = g.astype(bf16)
            w = w_qkv_ref[at, :]
            f_ref[pl.ds(0, 8), at] = sum(dot(ones, part, 1, 1) for part in halves(w.astype(f32) * g))
            f_ref[pl.ds(8, 8), at] = sum(dot(part, w, 1, 1) for part in halves(total))
        for e, r in soon:
            e.finish(place, *r)
        later[0].finish(place, g_rows_low, *later[1])


def attend_back(parent, qkv, d_full, w_rows, w_qkv, context, norm_one, extras, cid):
    tokens, width = d_full.shape
    n = qkv.shape[1]
    rows = 256
    whole = lambda shape: pl.BlockSpec(shape, lambda i: (0,) * len(shape))
    return pl.pallas_call(
        functools.partial(attend_back_kernel, extras, lax.axis_size("tree")),
        grid=(tokens // rows,),
        in_specs=[
            pl.BlockSpec(memory_space=pltpu.SMEM), whole((tokens, n)), pl.BlockSpec((rows, width), lambda i: (i, 0)),
            whole((HEAD_DIM, width)), whole((width, n)),
            pl.BlockSpec((rows, HEAD_DIM), lambda i: (i, 0)), ANYWHERE, *[i for e in extras for i in e.in_specs],
        ],
        out_specs=[whole((tokens, n)), whole((width, n)), whole((32, width)), *[o for e in extras for o in e.out_specs]],
        scratch_shapes=[
            *[i for e in extras for i in e.scratch],
            pltpu.VMEM((tokens, HEAD_DIM), f32), pltpu.VMEM((tokens, HEAD_DIM), f32), pltpu.VMEM((tokens, HEAD_DIM), bf16),
            pltpu.VMEM((tokens, width), bf16), DMA,
            pltpu.VMEM((HEAD_DIM, width), f32), pltpu.VMEM((HEAD_DIM, width), bf16),
        ],
        out_shape=[
            jax.ShapeDtypeStruct((tokens, n), bf16), jax.ShapeDtypeStruct((width, n), bf16),
            jax.ShapeDtypeStruct((32, width), f32), *[o for e in extras for o in e.outs],
        ],
        compiler_params=pltpu.CompilerParams(collective_id=cid, has_side_effects=True, vmem_limit_bytes=58 * 2**20),
        cost_estimate=pl.CostEstimate(flops=2 * tokens * width * HEAD_DIM, bytes_accessed=60_000_000, transcendentals=0),
        name="attend_back",
    )(parent, qkv, d_full, w_rows, w_qkv, context, norm_one, *[a for e in extras for a in e.ins])


def feed_forward_kernel(n_ref, c_ref, wu_ref, wd_ref, b_ref, active_ref, d_ref, sum_ref):
    fs = wu_ref.shape[1]
    at = lax.axis_index("blk") * 2 + lax.axis_index("rep")
    b = b_ref[:, pl.ds(pl.multiple_of(at * fs, fs), fs)]
    act, der = gelu_pair(dot(n_ref[...], wu_ref[...], 1, 0) + b)
    active_ref[...] = act.astype(bf16)
    d = (dot(c_ref[...], wd_ref[...], 1, 0) * der).astype(bf16)
    d_ref[...] = d

    @pl.when(pl.program_id(0) == 0)
    def _():
        sum_ref[...] = jnp.zeros_like(sum_ref)

    sum_ref[...] += jnp.sum(d.astype(f32).reshape(-1, 8, d.shape[1]), axis=0)


def feed_forward(n_full, c_full, wu, wd, b):
    tokens, width = n_full.shape
    n = wu.shape[1]
    rows = 512
    whole = lambda shape: pl.BlockSpec(shape, lambda i: (0,) * len(shape))
    by_row = lambda cols: pl.BlockSpec((rows, cols), lambda i: (i, 0))
    return pl.pallas_call(
        feed_forward_kernel,
        grid=(tokens // rows,),
        in_specs=[by_row(width), by_row(width), whole((width, n)), whole((width, n)), whole((1, b.shape[0]))],
        out_specs=[by_row(n), by_row(n), whole((8, n))],
        out_shape=[jax.ShapeDtypeStruct((tokens, n), bf16)] * 2 + [jax.ShapeDtypeStruct((8, n), f32)],
        compiler_params=pltpu.CompilerParams(vmem_limit_bytes=40 * 2**20),
        cost_estimate=pl.CostEstimate(flops=4 * tokens * width * n, bytes_accessed=4 * tokens * width, transcendentals=0),
        name="feed_forward",
    )(n_full, c_full, wu, wd, b[None])


def last_kernel(*refs):
    dn_ref, x_ref, d_res_ref, vecs_ref, res_ref, mlp_ref, down_ref, *shares = refs[:12]
    grad_ref, out_ref, down_out, *sums = refs[12:]
    n, root = norm_stats(x_ref[...].astype(f32))
    grad_ref[...] = d_res_ref[...] + norm_back(dn_ref[...], n, root, vecs_ref[pl.ds(0, 1), :])
    out_ref[...] = (res_ref[...] + mlp_ref[...] + vecs_ref[pl.ds(7, 1), :]).astype(bf16)
    down_out[...] = down_ref[...].astype(f32)
    for share, total in zip(shares, sums):
        total[...] = jnp.sum(share[...].astype(f32), axis=0)


def last(d_norm, x, d_res, vecs, residual, mlp, g_down, shares):
    tok, width = x.shape
    steps = 4
    by_row = pl.BlockSpec((tok // steps, width), lambda i: (i, 0))
    vectors = pl.BlockSpec(vecs.shape, lambda i: (0, 0))
    by_column = lambda v: pl.BlockSpec((v.shape[0], v.shape[1] // steps), lambda i: (0, i))
    by_column_3 = lambda v: pl.BlockSpec(v.shape[:2] + (v.shape[2] // steps,), lambda i: (0, 0, i))
    flat = [jax.ShapeDtypeStruct(v.shape[1:], f32) for v in shares]
    return pl.pallas_call(
        last_kernel,
        grid=(steps,),
        in_specs=[by_row, by_row, by_row, vectors, by_row, by_row, by_column(g_down), *map(by_column_3, shares)],
        out_specs=[by_row, by_row, by_column(g_down), *map(by_column, flat)],
        out_shape=[
            jax.ShapeDtypeStruct((tok, width), f32), jax.ShapeDtypeStruct((tok, width), bf16),
            jax.ShapeDtypeStruct(g_down.shape, f32), *flat,
        ],
        compiler_params=pltpu.CompilerParams(vmem_limit_bytes=58 * 2**20),
        name="last",
    )(d_norm, x, d_res, vecs, residual, mlp, g_down, *shares)


def body(
    inputs, gain_one, bias_one, w_query, b_query, w_key, w_value, b_value, w_out, b_out,
    gain_two, bias_two, w_up, b_up, w_down, b_down, parents, cotangent,
):
    tok, width = inputs.shape
    rows = w_query.shape[0]
    ff = w_up.shape[1]
    fs = ff // TREE_SEGS
    trees = lax.axis_size("tree")
    devices = trees * TREE_SEGS
    tree = lax.axis_index("tree")
    me = lax.axis_index(GROUP)

    vectors = (gain_one, bias_one, b_query, b_value, b_out, gain_two, bias_two, b_down, b_up)
    n_small = sum(v.shape[0] for v in vectors)
    block = jnp.zeros((16 * 128,), bf16)
    at = 0
    for v in vectors:
        block = block + jnp.pad(v, (at, 16 * 128 - at - v.shape[0]))
        at += v.shape[0]
    block = block.reshape(16, 128)

    x_full, box, w_att = tree_gather(inputs, 0, "gather_inputs", FIRST, extras=(
        SpreadSmall(block), DealAll(w_query, w_key, w_value),
    ))
    w_att = w_att.reshape(width, -1)
    packed = box.transpose(1, 0, 2, 3).reshape(devices, -1)[:, :n_small]
    vecs = packed[:, : 8 * rows].reshape(devices, 8, rows).transpose(1, 0, 2).reshape(8, width).astype(f32)
    gain_one, bias_one, _, _, b_out, gain_two, bias_two, _ = vecs
    b_up = packed[:, 8 * rows :].reshape(-1).astype(f32)

    local_seg = jnp.arange(TREE_SEGS, dtype=jnp.int32)
    own_parents = lax.dynamic_slice_in_dim(parents, tree * TREE_SEGS, TREE_SEGS) - tree * TREE_SEGS
    parent = jnp.where(local_seg >= 2 * TRUNK_SEGS, own_parents, local_seg)

    norm_one, qkv, context, w_orow, share_up, share_down = attend(
        parent, x_full, vecs, w_att,
        (HeadRows(w_out), DealColumns(w_up), DealColumns(w_down)), 9
    )
    att, wd, c_full = product_scatter(context, w_orow, 0, 2, "scatter_attended", LIGHT, extras=(
        ToTrees(share_down.reshape(-1, fs)), GatherRows(cotangent, ROOM),
    ))
    wd = wd.reshape(width, fs)
    x_own = inputs.astype(f32)
    residual = x_own + att + b_out
    n_two, root_two = norm_stats(residual)
    norm_two = (n_two * gain_two + bias_two).astype(bf16)
    nt_full, wu = tree_gather(norm_two, 3, "gather_norm_two", LIGHT, extras=(ToTrees(share_up.reshape(-1, fs)),))
    wu = wu.reshape(width, fs)

    active, d_up, gb_up = feed_forward(nt_full, c_full, wu, wd, b_up)
    g_up = dot(nt_full, d_up, 0, 0).astype(bf16)
    d_norm_two, g_up, g_down = product_scatter(d_up, wu, 1, 4, "scatter_d_norm_two", MIXED, extras=(
        DealAllRows(g_up.reshape(devices, rows, fs), (fs,)), Product(c_full, active, 0, bf16),
    ))

    cot = cotangent.astype(f32)
    d_res = cot + norm_back(d_norm_two, n_two, root_two, gain_two)
    d_att = d_res.astype(bf16)
    mlp, swap_down, da_full = product_scatter(active, wd, 1, 5, "scatter_mlp", LIGHT, extras=(
        SwapTrees(g_down), GatherRows(d_att, ROOM),
    ))
    g_down = own_rows(g_down, swap_down, rows)
    d_qkv, g_att, shares, g_down, g_o = attend_back(
        parent, qkv, da_full, w_orow, w_att, context, norm_one, (DealRows(g_down, (fs,)), HeadRowsBack(width, rows)), 10
    )

    gb_one = shares[8]
    gg_one = (shares[0] - bias_one * gb_one) / gain_one

    def placed(vec, total):
        return lax.dynamic_update_slice_in_dim(jnp.zeros((total,), f32), vec, me * vec.shape[0], axis=0)

    col = lambda a: jnp.sum(a, axis=0)
    sums = [
        gg_one, gb_one, shares[16], shares[24],
        col(d_att.astype(f32)), col(d_norm_two * n_two), col(d_norm_two), col(cot),
    ]
    sums = jnp.stack(sums).reshape(8, devices, rows).transpose(1, 0, 2).reshape(devices, 8 * rows)
    sums = jnp.concatenate([sums, placed(col(gb_up), ff).reshape(devices, -1)], axis=1)
    sums = jnp.pad(sums, ((0, 0), (0, 1024 - n_small))).reshape(trees, TREE_SEGS, 8, 128).transpose(1, 0, 2, 3)
    d_norm_one, sums, g_q, g_k, g_v = product_scatter(d_qkv, w_att, 1, 7, "scatter_d_norm_one", MIXED, extras=(
        ReduceSmall(sums), DealAllRows(g_att.reshape(devices, rows, -1), (HEAD_DIM,) * 3),
    ))
    sums = sums.reshape(-1)
    parts = [sums[j * rows : (j + 1) * rows] for j in range(8)]
    gb_up = sums[8 * rows : n_small]

    grad_inputs, layer_output, g_down, g_q, g_k, g_v, g_o, g_up = last(
        d_norm_one, inputs, d_res, vecs, residual, mlp, g_down, (g_q, g_k, g_v, g_o, g_up)
    )
    return (
        layer_output, grad_inputs, parts[0], parts[1], g_q, parts[2], g_k, g_v, parts[3], g_o, parts[4],
        parts[5], parts[6], g_up, gb_up, g_down, parts[7],
    )


def solution(mesh):
    names = mesh.axis_names
    shape = mesh.devices.shape
    blk = TREE_SEGS // shape[1]
    inner = Mesh(mesh.devices.reshape(shape[0] // blk, blk, shape[1]), ALL)
    mat, vec = P(ALL, None), P(ALL)
    in_specs = (
        mat, vec, vec, mat, vec, mat, mat, vec, mat, vec, vec, vec, mat, vec, mat, vec, P(), mat,
    )
    out_specs = (
        mat, mat, vec, vec, mat, vec, mat, mat, vec, mat, vec, vec, vec, mat, vec, mat, vec,
    )
    return jax.shard_map(body, mesh=inner, in_specs=in_specs, out_specs=out_specs, check_vma=False)
```

```python
import functools

import jax
import jax.numpy as jnp
from jax import lax
from jax.experimental import pallas as pl
from jax.experimental.pallas import tpu as pltpu
from jax.sharding import Mesh, PartitionSpec as P

HEAD_DIM = 128
TRUNK_SEGS = 4
TREE_SEGS = 16
EPS = 1e-05
GROUP = ("blk", "rep")
ALL = ("tree", "blk", "rep")
f32 = jnp.float32
bf16 = jnp.bfloat16


def dot(a, b, ca, cb):
    return lax.dot_general(a, b, (((ca,), (cb,)), ((), ())), preferred_element_type=f32)


MESH = pl.DeviceIdType.MESH
X, Y, Z = 1, 2, 4
COMM_BYTES = 120_000_000
EVEN = ((6, (X, Y, Z)), (5, (Y, Z, X)), (5, (Z, X, Y)))
ROOM = ((8, (X, Z, Y)), (8, (Y, Z, X)))
LIGHT = ((7, (Z, X, Y)), (7, (Z, Y, X)), (2, (X, Y, Z)))
MIXED = ((6, (X, Z, Y)), (6, (Y, Z, X)), (2, (Z, X, Y)), (2, (Z, Y, X)))
FIRST = ((6, (Z, X, Y)), (6, (Z, Y, X)), (4, (X, Y, Z)))


class Place:
    def __init__(self, trees):
        self.trees = trees
        self.tree = lax.axis_index("tree")
        blk = lax.axis_index("blk")
        self.x = lax.axis_index("rep")
        self.c = lax.rem(blk, 2)
        self.y = lax.rem(blk // 2, 2)
        self.z = blk // 4
        self.at = blk * 2 + self.x
        self.flat = self.tree * TREE_SEGS + self.at
        self.closing = False

    def flipped(self, r, other=0):
        flip = lambda v, on: 1 - v if on else v
        return flip(self.z, r & Z), flip(self.y, r & Y), flip(self.c, other), flip(self.x, r & X)

    def device(self, r, other=0):
        z, y, c, x = self.flipped(r, other)
        return (self.tree, (z * 2 + y) * 2 + c, x)

    def index(self, r, other=0):
        z, y, c, x = self.flipped(r, other)
        return ((z * 2 + y) * 2 + c) * 2 + x

    def in_tree(self, k):
        return (lax.rem(self.tree + k, self.trees), self.at // 2, self.x)

    def peer(self, k):
        j = lax.rem(self.at + k, TREE_SEGS)
        return j, (self.tree, j // 2, lax.rem(j, 2))

    def of_flat(self, flat):
        j = lax.rem(flat, TREE_SEGS)
        return (flat // TREE_SEGS, j // 2, lax.rem(j, 2))


def signal(device):
    pl.semaphore_signal(pltpu.get_barrier_semaphore(), inc=1, device_id=device, device_id_type=MESH)


def greet(place, extras=()):
    count = 0
    if any(e.everyone for e in extras):
        devices = place.trees * TREE_SEGS
        pl.loop(1, devices)(lambda k: signal(place.of_flat(lax.rem(place.flat + k, devices))))
        pl.semaphore_wait(pltpu.get_barrier_semaphore(), devices - 1)
        return
    if any(e.peers for e in extras):
        pl.loop(1, TREE_SEGS)(lambda k: signal(place.peer(k)[1]))
        count += TREE_SEGS - 1
    else:
        for r, other in ((X, 0), (Y, 0), (Z, 0), (0, 1)):
            signal(place.device(r, other))
        count += 4
    if any(e.trees for e in extras):
        for k in range(1, place.trees):
            signal(place.in_tree(k))
        count += place.trees - 1
    for e in extras:
        count += e.greet(place)
    pl.semaphore_wait(pltpu.get_barrier_semaphore(), count)


def push(src, dst, send, recv, device):
    return pltpu.make_async_remote_copy(
        src_ref=src, dst_ref=dst, send_sem=send, recv_sem=recv, device_id=device, device_id_type=MESH
    )


def drain(ref, sem):
    pltpu.make_async_copy(ref, ref, sem).wait()


DMA = pltpu.SemaphoreType.DMA
ANYWHERE = pl.BlockSpec(memory_space=pl.ANY)
IN_VMEM = pl.BlockSpec(memory_space=pltpu.VMEM)


class Extra:
    peers = trees = everyone = False
    bulk = 2
    ins, in_specs, outs, out_specs, scratch = (), (), (), (), ()

    def greet(self, place):
        return 0


class SpreadSmall(Extra):
    trees = True
    bulk = 0

    def __init__(self, block):
        n = lax.axis_size("tree")
        self.ins, self.in_specs = (block,), (IN_VMEM,)
        self.outs, self.out_specs = (jax.ShapeDtypeStruct((16, n) + block.shape, block.dtype),), (IN_VMEM,)
        self.scratch = (DMA((14 + n,)), DMA((14 + n,)))

    def stages(self, place, src, box, send, recv):
        here = place.at
        box[here, place.tree] = src[...]
        new = []
        for k in range(1, place.trees):
            new.append(push(src, box.at[here, place.tree], send.at[14 + k], recv.at[14 + k], place.in_tree(k)))
            new[-1].start()
        done = list(new)
        yield
        held = [(0, 0)]
        for j, (bit, other) in enumerate(((X, 0), (Y, 0), (0, 1), (Z, 0))):
            for copy in new:
                copy.wait_recv()
            new = []
            for k, (r, o) in enumerate(held):
                block = box.at[place.index(r, o)]
                slot = (1 << j) - 1 + k
                new.append(push(block, block, send.at[slot], recv.at[slot], place.device(bit, other)))
                new[-1].start()
            held += [(r | bit, o | other) for r, o in held]
            done += new
            yield
        while not place.closing:
            yield
        for copy in new:
            copy.wait_recv()
        for copy in done:
            copy.wait_send()


class ReduceSmall(Extra):
    trees = True

    def __init__(self, sums):
        n = sums.shape[1]
        tail = sums.shape[2:]
        self.ins, self.in_specs = (sums,), (IN_VMEM,)
        self.outs, self.out_specs = (jax.ShapeDtypeStruct(tail, f32),), (IN_VMEM,)
        self.scratch = (
            pltpu.VMEM((TREE_SEGS,) + tail, f32), pltpu.VMEM((15,) + tail, f32),
            pltpu.VMEM((max(n - 1, 1), TREE_SEGS) + tail, f32), DMA((14 + n,)), DMA((14 + n,)),
        )

    def stages(self, place, src, out, acc, inbox, tbox, send, recv):
        far = []
        for k in range(1, place.trees):
            tree = lax.rem(place.tree + k, place.trees)
            far.append(push(src.at[:, tree], tbox.at[k - 1], send.at[14 + k], recv.at[14 + k], place.in_tree(k)))
            far[-1].start()
        yield
        for copy in far:
            copy.wait_recv()
        for j in range(TREE_SEGS):
            total = src[j, place.tree]
            for k in range(1, place.trees):
                total = total + tbox[k - 1, j]
            acc[j] = total
        left = [(r, o) for r in range(8) for o in range(2)]
        done = []
        for bit, other in ((0, 1), (X, 0), (Y, 0), (Z, 0)):
            new = []
            keep = [(r, o) for r, o in left if not (r & bit or o & other)]
            for r, o in keep:
                slot = len(done) + len(new)
                block = acc.at[place.index(r | bit, o | other)]
                new.append(push(block, inbox.at[slot], send.at[slot], recv.at[slot], place.device(bit, other)))
                new[-1].start()
            yield
            if bit == Z:
                while not place.closing:
                    yield
            for k, (r, o) in enumerate(keep):
                new[k].wait_recv()
                at = place.index(r, o)
                acc[at] = acc[at] + inbox[len(done) + k]
            done += new
            left = keep
        out[...] = acc[place.index(0)]
        for copy in far + done:
            copy.wait_send()


class ToTrees(Extra):
    trees = True

    def __init__(self, src):
        n = lax.axis_size("tree")
        self.ins, self.in_specs = (src,), (ANYWHERE,)
        self.outs, self.out_specs = (jax.ShapeDtypeStruct((n,) + src.shape, src.dtype),), (ANYWHERE,)
        self.scratch = (DMA((n,)), DMA((n,)))

    def stages(self, place, src, dst, send, recv):
        copies = [
            push(src, dst.at[place.tree], send.at[k - 1], recv.at[k - 1], place.in_tree(k)) for k in range(1, place.trees)
        ]
        copies.append(pltpu.make_async_copy(src, dst.at[place.tree], send.at[place.trees - 1]))
        for copy in copies:
            copy.start()
        while not place.closing:
            yield
        for copy in copies:
            copy.wait()


class SwapTrees(Extra):
    trees = True

    def __init__(self, src):
        n = lax.axis_size("tree")
        self.ins, self.in_specs = (src,), (ANYWHERE,)
        shape = (max(n - 1, 1), src.shape[0] // n) + src.shape[1:]
        self.outs, self.out_specs = (jax.ShapeDtypeStruct(shape, src.dtype),), (ANYWHERE,)
        self.scratch = (DMA((n,)), DMA((n,)))

    def stages(self, place, src, dst, send, recv):
        share = dst.shape[1]
        copies = []
        for k in range(1, place.trees):
            tree = lax.rem(place.tree + k, place.trees)
            rows = src.at[pl.ds(pl.multiple_of(tree * share, share), share)]
            copies.append(push(rows, dst.at[k - 1], send.at[k - 1], recv.at[k - 1], place.in_tree(k)))
            copies[-1].start()
        while not place.closing:
            yield
        for copy in copies:
            copy.wait()


class DealColumns(Extra):
    peers = True

    def __init__(self, mat):
        rows, c = mat.shape[0], mat.shape[1] // TREE_SEGS
        self.ins, self.in_specs = (mat,), (ANYWHERE,)
        self.outs, self.out_specs = (jax.ShapeDtypeStruct((TREE_SEGS, rows, c), bf16),), (ANYWHERE,)
        self.scratch = (DMA, DMA, DMA)

    def start(self, place, mat, out, send, recv, keep):
        c = out.shape[2]
        columns = lambda j: mat.at[:, pl.ds(pl.multiple_of(j * c, c), c)]

        def one(k):
            j, device = place.peer(k)
            push(columns(j), out.at[place.at], send, recv, device).start()

        pl.loop(1, TREE_SEGS)(one)
        pltpu.make_async_copy(columns(place.at), out.at[place.at], keep).start()

    def finish(self, place, mat, out, send, recv, keep):
        most = out.at[pl.ds(0, TREE_SEGS - 1)]
        drain(most, send)
        drain(most, recv)
        drain(out.at[0], keep)

    def stages(self, place, *refs):
        self.start(place, *refs)
        while not place.closing:
            yield
        self.finish(place, *refs)


class DealAll(Extra):
    everyone = True

    def __init__(self, *mats):
        devices = lax.axis_size("tree") * TREE_SEGS
        self.widths = [m.shape[1] // TREE_SEGS for m in mats]
        self.ins, self.in_specs = tuple(mats), (ANYWHERE,) * len(mats)
        self.outs = (jax.ShapeDtypeStruct((devices, mats[0].shape[0], sum(self.widths)), bf16),)
        self.out_specs = (ANYWHERE,)
        self.scratch = (DMA, DMA, DMA)

    def pieces(self, place, refs, tree, j):
        mats, out = refs[:-4], refs[-4]
        lo = 0
        for m, c in zip(mats, self.widths):
            yield m.at[:, pl.ds(pl.multiple_of(j * c, c), c)], out.at[place.flat, :, pl.ds(lo, c)]
            lo += c

    def blocks(self, refs):
        return refs[-4]

    def stages(self, place, *refs):
        send, recv, keep = refs[-3:]

        def one(tree, j):
            device = (tree, j // 2, lax.rem(j, 2))
            for src, dst in self.pieces(place, refs, tree, j):
                push(src, dst, send, recv, device).start()

        for k in range(1, place.trees):
            tree = lax.rem(place.tree + k, place.trees)
            pl.loop(0, TREE_SEGS)(lambda i: one(tree, lax.rem(place.at + i, TREE_SEGS)))
        pl.loop(1, TREE_SEGS)(lambda i: one(place.tree, lax.rem(place.at + i, TREE_SEGS)))
        for src, dst in self.pieces(place, refs, place.tree, place.at):
            pltpu.make_async_copy(src, dst, keep).start()
        while not place.closing:
            yield
        whole = self.blocks(refs)
        most = whole.at[pl.ds(0, whole.shape[0] - 1)]
        drain(most, send)
        drain(most, recv)
        drain(whole.at[0], keep)


class DealAllRows(DealAll):
    def __init__(self, src, widths):
        self.widths = widths
        rows = src.shape[1]
        self.ins, self.in_specs = (src,), (ANYWHERE,)
        shape = lambda c: (src.shape[0] // TREE_SEGS, rows, TREE_SEGS * c)
        self.outs = tuple(jax.ShapeDtypeStruct(shape(c), bf16) for c in widths)
        self.out_specs = (ANYWHERE,) * len(widths)
        self.scratch = (DMA, DMA, DMA)

    def pieces(self, place, refs, tree, j):
        src, outs = refs[0], refs[1:-3]
        lo = 0
        for out, c in zip(outs, self.widths):
            columns = pl.ds(pl.multiple_of(place.at * c, c), c)
            yield src.at[tree * TREE_SEGS + j, :, pl.ds(lo, c)], out.at[place.tree, :, columns]
            lo += c

    def blocks(self, refs):
        return refs[0]


class DealRows(Extra):
    peers = True

    def __init__(self, src, widths):
        self.widths = widths
        rows = src.shape[1]
        self.ins, self.in_specs = (src,), (ANYWHERE,)
        self.outs = tuple(jax.ShapeDtypeStruct((rows, TREE_SEGS * c), bf16) for c in widths)
        self.out_specs = (ANYWHERE,) * len(widths)
        self.scratch = (DMA, DMA, DMA)

    def start(self, place, src, *refs):
        outs, (send, recv, keep) = refs[:-3], refs[-3:]

        def pieces(j):
            lo = 0
            for out, c in zip(outs, self.widths):
                yield src.at[j, :, pl.ds(lo, c)], out.at[:, pl.ds(pl.multiple_of(place.at * c, c), c)]
                lo += c

        def one(k):
            j, device = place.peer(k)
            for block, dst in pieces(j):
                push(block, dst, send, recv, device).start()

        pl.loop(1, TREE_SEGS)(one)
        for block, dst in pieces(place.at):
            pltpu.make_async_copy(block, dst, keep).start()

    def finish(self, place, src, *refs):
        send, recv, keep = refs[-3:]
        most = src.at[pl.ds(0, TREE_SEGS - 1)]
        drain(most, send)
        drain(most, recv)
        drain(src.at[0], keep)

    def stages(self, place, *refs):
        self.start(place, *refs)
        while not place.closing:
            yield
        self.finish(place, *refs)


class HeadRows(Extra):
    def __init__(self, shard):
        self.rows = shard.shape[0]
        self.ins, self.in_specs = (shard,), (ANYWHERE,)
        self.outs = (jax.ShapeDtypeStruct((HEAD_DIM, shard.shape[1]), shard.dtype),)
        self.out_specs = (ANYWHERE,)
        self.scratch = (DMA((lax.axis_size("tree"),)), DMA)

    def greet(self, place):
        per_head = HEAD_DIM // self.rows
        for b in range(per_head):
            signal(place.of_flat(place.at * per_head + b))
        return place.trees

    def each(self, place, src, out, send, recv, do_far, do_own):
        at = place.flat * self.rows
        head = at // HEAD_DIM
        dst = out.at[pl.ds(pl.multiple_of(lax.rem(at, HEAD_DIM), self.rows), self.rows)]
        for t in range(place.trees):
            own = (place.tree == t) & (place.at == head)
            pl.when(jnp.logical_not(own))(lambda t=t: do_far(
                push(src, dst, send.at[t], recv, (t, head // 2, lax.rem(head, 2)))
            ))
            if do_own:
                pl.when(own)(lambda: do_own(pltpu.make_async_copy(src, dst, recv)))

    def start(self, place, *refs):
        self.each(place, *refs, lambda copy: copy.start(), lambda copy: copy.start())

    def finish(self, place, *refs):
        self.each(place, *refs, lambda copy: copy.wait_send(), None)
        drain(refs[1], refs[3])


class HeadRowsBack(Extra):
    def __init__(self, width, rows):
        self.rows = rows
        n = lax.axis_size("tree")
        self.outs, self.out_specs = (jax.ShapeDtypeStruct((n, rows, width), bf16),), (ANYWHERE,)
        self.scratch = (DMA((HEAD_DIM // rows,)), DMA)

    def greet(self, place):
        head = place.flat * self.rows // HEAD_DIM
        for t in range(place.trees):
            signal((t, head // 2, lax.rem(head, 2)))
        return HEAD_DIM // self.rows

    def each(self, place, src, out, send, recv, do_far, do_own):
        per_head = HEAD_DIM // self.rows
        for b in range(per_head):
            flat = place.at * per_head + b
            own = place.flat == flat
            block, dst = src.at[pl.ds(b * self.rows, self.rows)], out.at[place.tree]
            pl.when(jnp.logical_not(own))(lambda b=b, block=block, dst=dst, flat=flat: do_far(
                push(block, dst, send.at[b], recv, place.of_flat(flat))
            ))
            if do_own:
                pl.when(own)(lambda block=block, dst=dst: do_own(pltpu.make_async_copy(block, dst, recv)))

    def start(self, place, *refs):
        self.each(place, *refs, lambda copy: copy.start(), lambda copy: copy.start())

    def finish(self, place, *refs):
        self.each(place, *refs, lambda copy: copy.wait_send(), None)
        drain(refs[1], refs[3])


class Product(Extra):
    def __init__(self, left, right, dim, kind):
        self.dim = dim
        m, n = left.shape[1 - dim], right.shape[1]
        self.ins, self.in_specs = (left, right), (ANYWHERE, IN_VMEM)
        self.outs, self.out_specs = (jax.ShapeDtypeStruct((m, n), kind),), (IN_VMEM,)
        self.scratch = (pltpu.VMEM(left.shape, left.dtype), DMA)

    def stages(self, place, left, right, out, held, sem):
        copy = pltpu.make_async_copy(left, held, sem)
        copy.start()
        yield
        copy.wait()
        count = 4
        block = out.shape[0] // count
        for j in range(count):
            at = pl.ds(j * block, block)
            part = held[at, :] if self.dim == 1 else held[:, at]
            out[at, :] = dot(part, right[...], self.dim, 0).astype(out.dtype)
            yield


def finish(place, extras, running):
    place.closing = True
    order = [s for e, s in zip(extras, running) if isinstance(e, GatherRows)]
    order += [s for s in running if s not in order]
    for stages in order:
        for _ in stages:
            pass


def sorted_refs(extras, refs, n_in, n_out):
    refs = list(refs)
    take = lambda n: [refs.pop(0) for _ in range(n)]
    own_in, ins = take(n_in), [take(len(e.ins)) for e in extras]
    own_out, outs = take(n_out), [take(len(e.outs)) for e in extras]
    scratch = [take(len(e.scratch)) for e in extras]
    return own_in, own_out, refs, [i + o + s for i, o, s in zip(ins, outs, scratch)]


def call(kernel, extras, args, in_specs, out_shape, out_specs, scratch, cid, name, flops=0, vmem=None):
    out = pl.pallas_call(
        functools.partial(kernel, extras, lax.axis_size("tree")),
        out_shape=out_shape + [o for e in extras for o in e.outs],
        in_specs=in_specs + [i for e in extras for i in e.in_specs],
        out_specs=out_specs + [o for e in extras for o in e.out_specs],
        scratch_shapes=[i for e in extras for i in e.scratch] + scratch,
        compiler_params=pltpu.CompilerParams(collective_id=cid, has_side_effects=True, vmem_limit_bytes=vmem),
        cost_estimate=pl.CostEstimate(flops=flops, bytes_accessed=COMM_BYTES, transcendentals=0),
        name=name,
    )(*args, *[a for e in extras for a in e.ins])
    return out if len(out) > 1 else out[0]


def part_columns(width, plan):
    cuts = [0]
    for share, _ in plan:
        cuts.append(cuts[-1] + share * width // 16)
    return [(cuts[p], cuts[p + 1] - cuts[p]) for p in range(len(plan))]


class GatherRows(Extra):
    bulk = 1

    def __init__(self, x, plan):
        tok, width = x.shape
        self.plan = plan
        n = len(plan)
        self.ins, self.in_specs = (x,), (ANYWHERE,)
        self.outs, self.out_specs = (jax.ShapeDtypeStruct((16 * tok, width), x.dtype),), (ANYWHERE,)
        self.scratch = (DMA((n, 7)), DMA((n, 7)), DMA((n, 8)), DMA((n, 8)), DMA)

    def stages(self, place, x_ref, o_ref, send, recv, psend, precv, local):
        orders = [order for _, order in self.plan]
        tok, width = x_ref.shape
        cols = part_columns(width, self.plan)

        def rows(r, other=0):
            return pl.ds(pl.multiple_of(place.index(r, other) * tok, tok), tok)

        def remote(src, r, p, dim):
            lo, n = cols[p]
            slot = r | dim
            return pltpu.make_async_remote_copy(
                src_ref=src, dst_ref=o_ref.at[rows(r), pl.ds(lo, n)],
                send_sem=send.at[p, slot - 1], recv_sem=recv.at[p, slot - 1],
                device_id=place.device(dim), device_id_type=MESH,
            )

        def pair(r, p):
            lo, n = cols[p]
            src = o_ref.at[rows(r), pl.ds(lo, n)]
            return pltpu.make_async_remote_copy(
                src_ref=src, dst_ref=src, send_sem=psend.at[p, r], recv_sem=precv.at[p, r],
                device_id=place.device(0, 1), device_id_type=MESH,
            )

        started = []
        own = [x_ref.at[:, pl.ds(lo, n)] for lo, n in cols]
        for step in range(3):
            for p in range(len(orders)):
                copy = remote(own[p], 0, p, orders[p][step])
                copy.start()
                started.append(copy)
        keep = pltpu.make_async_copy(x_ref, o_ref.at[rows(0)], local)
        keep.start()
        for p in range(len(orders)):
            lo, n = cols[p]
            copy = pltpu.make_async_remote_copy(
                src_ref=own[p], dst_ref=o_ref.at[rows(0), pl.ds(lo, n)], send_sem=psend.at[p, 0], recv_sem=precv.at[p, 0],
                device_id=place.device(0, 1), device_id_type=MESH,
            )
            copy.start()
            started.append(copy)

        def arrived(p, slot):
            lo, n = cols[p]
            ref = o_ref.at[rows(slot), pl.ds(lo, n)]
            pltpu.make_async_remote_copy(
                src_ref=ref, dst_ref=ref, send_sem=send.at[p, slot - 1], recv_sem=recv.at[p, slot - 1],
                device_id=place.device(X), device_id_type=MESH,
            ).wait_recv()

        for which in ((1, 0, 0), (0, 1, 0), (1, 1, 0), (0, 0, 1), (1, 0, 1), (0, 1, 1), (1, 1, 1)):
            yield
            for p in range(len(orders)):
                dims = orders[p]
                slot = sum(d for d, on in zip(dims, which) if on)
                arrived(p, slot)
                lo, n = cols[p]
                src = o_ref.at[rows(slot), pl.ds(lo, n)]
                top = max(j for j in range(3) if which[j])
                for j in range(top + 1, 3):
                    copy = remote(src, slot, p, dims[j])
                    copy.start()
                    started.append(copy)
                copy = pair(slot, p)
                copy.start()
                started.append(copy)
        for copy in started:
            copy.wait_send()
        for p in range(len(orders)):
            lo, n = cols[p]
            for r in range(8):
                ref = o_ref.at[rows(r, 1), pl.ds(lo, n)]
                pltpu.make_async_remote_copy(
                    src_ref=ref, dst_ref=ref, send_sem=psend.at[p, r], recv_sem=precv.at[p, r],
                    device_id=place.device(0, 1), device_id_type=MESH,
                ).wait_recv()
        keep.wait()


def gather_kernel(extras, trees, *refs):
    _, _, _, extra_refs = sorted_refs(extras, refs, 0, 0)
    place = Place(trees)
    greet(place, extras)
    running = [e.stages(place, *r) for e, r in zip(extras, extra_refs)]
    turn = sorted(zip(extras, running), key=lambda e: e[0].bulk)
    for _ in range(8):
        for _, stages in turn:
            next(stages, None)
    finish(place, extras, running)


def tree_gather(x, cid, name, plan=EVEN, extras=()):
    out = call(gather_kernel, tuple(extras) + (GatherRows(x, plan),), [], [], [], [], [], cid, name)
    return (out[-1], *out[:-1]) if extras else out


def scatter_kernel(plan, rhs_dim, tok, extras, trees, *refs):
    orders = [order[::-1] for _, order in plan]
    (l_ref, r_ref), (o_ref,), scratch, extra_refs = sorted_refs(extras, refs, 2, 1)
    acc, pout, pin, stage, inbox, psend, precv, send, recv = scratch
    place = Place(trees)
    width = o_ref.shape[1]
    cols = part_columns(width, plan)
    greet(place, extras)
    tile = 512

    running = [e.stages(place, *r) for e, r in zip(extras, extra_refs)]

    def advance():
        for stages in running:
            next(stages, None)

    advance()

    def product(zy, other, put):
        z, y, c, _ = place.flipped(zy, other)
        start = pl.multiple_of(((z * 2 + y) * 2 + c) * 2 * tok, 2 * tok)

        def one(j):
            at = pl.multiple_of(j * tile, tile)
            left = l_ref[pl.ds(start, 2 * tok), :]
            if rhs_dim == 1:
                res = lax.dot_general(left, r_ref[pl.ds(at, tile), pl.ds(0, l_ref.shape[1])], (((1,), (1,)), ((), ())), preferred_element_type=f32)
            else:
                res = lax.dot_general(left, r_ref[:, pl.ds(at, tile)], (((1,), (0,)), ((), ())), preferred_element_type=f32)
            put(at, res)

        pl.loop(0, width // tile)(one)

    def pair(k):
        return pltpu.make_async_remote_copy(
            src_ref=pout.at[k], dst_ref=pin.at[k], send_sem=psend.at[k], recv_sem=precv.at[k],
            device_id=place.device(0, 1), device_id_type=MESH,
        )

    groups = (Z | Y, Z, Y, 0)

    def for_partner(k):
        def put_out(at, res):
            pout[k, :, pl.ds(at, tile)] = res.astype(bf16)
        product(groups[k], 1, put_out)
        pair(k).start()

    for_partner(0)
    for_partner(1)

    def hop(p, r, step, slot):
        lo, n = cols[p]
        return pltpu.make_async_remote_copy(
            src_ref=stage.at[r - 1, :, pl.ds(lo, n)], dst_ref=inbox.at[slot, :, pl.ds(lo, n)],
            send_sem=send.at[p, r - 1], recv_sem=recv.at[p, slot],
            device_id=place.device(orders[p][step]), device_id_type=MESH,
        )

    started = []
    for k, zy in enumerate(groups):
        def put_own(at, res, k=k):
            acc[k, :, pl.ds(at, tile)] = res
        product(zy, 0, put_own)
        if k + 2 < len(groups):
            for_partner(k + 2)
        if k == 1:
            advance()
        pair(k).wait_recv()
        for rx in (X, 0):
            r = zy | rx
            xx = place.flipped(rx)[3]
            at = pl.ds(pl.multiple_of(xx * tok, tok), tok)
            for p in range(len(plan)):
                lo, n = cols[p]
                total = acc[k, at, pl.ds(lo, n)] + pin[k, at, pl.ds(lo, n)].astype(f32)
                first, second, third = orders[p]
                if r & first:
                    stage[r - 1, :, pl.ds(lo, n)] = total.astype(bf16)
                    slot = 3 - (2 * bool(r & second) + bool(r & third))
                    copy = hop(p, r, 0, slot)
                    copy.start()
                    started.append(copy)
                else:
                    acc[k, at, pl.ds(lo, n)] = total

    def held(p, r):
        k = groups.index(r & (Z | Y))
        xx = place.flipped(r & X)[3]
        lo, n = cols[p]
        return acc[k, pl.ds(pl.multiple_of(xx * tok, tok), tok), pl.ds(lo, n)]

    def take(p, slot):
        lo, n = cols[p]
        hop(p, 1, 0, slot).wait_recv()
        return inbox[slot, :, pl.ds(lo, n)].astype(f32)

    advance()
    for q in ((1, 1), (1, 0)):
        for p in range(len(plan)):
            first, second, third = orders[p]
            lo, n = cols[p]
            r = second + third * q[1]
            stage[r - 1, :, pl.ds(lo, n)] = (held(p, r) + take(p, 3 - (2 * q[0] + q[1]))).astype(bf16)
            copy = hop(p, r, 1, 4 + (1 - q[1]))
            copy.start()
            started.append(copy)
        advance()
    for p in range(len(plan)):
        third = orders[p][2]
        lo, n = cols[p]
        stage[third - 1, :, pl.ds(lo, n)] = (held(p, third) + take(p, 2) + take(p, 4)).astype(bf16)
        copy = hop(p, third, 2, 6)
        copy.start()
        started.append(copy)
    advance()
    for p in range(len(plan)):
        lo, n = cols[p]
        o_ref[:, pl.ds(lo, n)] = held(p, 0) + take(p, 3) + take(p, 5)
    for p in range(len(plan)):
        lo, n = cols[p]
        o_ref[:, pl.ds(lo, n)] += take(p, 6)
    advance()
    for copy in started:
        copy.wait_send()
    for k in range(4):
        pair(k).wait_send()
    finish(place, extras, running)


def product_scatter(left, right, rhs_dim, cid, name, plan=EVEN, extras=()):
    tokens, inner = left.shape
    width = right.shape[1 - rhs_dim]
    tok = tokens // 16
    n = len(plan)
    scratch = [
        pltpu.VMEM((4, 2 * tok, width), f32),
        pltpu.VMEM((4, 2 * tok, width), bf16),
        pltpu.VMEM((4, 2 * tok, width), bf16),
        pltpu.VMEM((7, tok, width), bf16),
        pltpu.VMEM((7, tok, width), bf16),
        DMA((4,)), DMA((4,)), DMA((n, 7)), DMA((n, 7)),
    ]
    return call(
        functools.partial(scatter_kernel, plan, rhs_dim, tok), extras, [left, right], [IN_VMEM, IN_VMEM],
        [jax.ShapeDtypeStruct((tok, width), f32)], [IN_VMEM],
        scratch, cid, name, 2 * tokens * width * inner, 56 * 2**20,
    )


def norm_stats(v):
    mean = jnp.mean(v, axis=-1, keepdims=True)
    centred = v - mean
    root = lax.rsqrt(jnp.mean(centred * centred, axis=-1, keepdims=True) + EPS)
    return centred * root, root


def norm_back(d, n, root, gain):
    g = d * gain
    return root * (g - jnp.mean(g, axis=-1, keepdims=True) - n * jnp.mean(g * n, axis=-1, keepdims=True))


def gelu_pair(u):
    c = (2.0 / jnp.pi) ** 0.5
    t = jnp.tanh(c * (u + 0.044715 * u * u * u))
    act = 0.5 * u * (1.0 + t)
    der = 0.5 * (1.0 + t) + 0.5 * u * (1.0 - t * t) * c * (1.0 + 3 * 0.044715 * u * u)
    return act, der


def own_rows(g, swapped, rows):
    share = swapped.shape[1]
    mine = lax.dynamic_slice_in_dim(g, lax.axis_index("tree") * share, share)
    if lax.axis_size("tree") > 1:
        mine = (mine.astype(f32) + jnp.sum(swapped.astype(f32), axis=0)).astype(bf16)
    return mine.reshape(TREE_SEGS, rows, -1)


def scores_of(qkv_ref, parent_ref, s, tok):
    hd = HEAD_DIM
    own = pl.ds(pl.multiple_of(s * tok, tok), tok)
    branches = [pl.ds((TRUNK_SEGS + b) * tok, tok) for b in range(4)]
    trunk = pl.ds(0, TRUNK_SEGS * tok)
    parent = parent_ref[s]

    def rows(col):
        up = qkv_ref[branches[0], col]
        for b in range(1, 4):
            up = jnp.where(parent == TRUNK_SEGS + b, qkv_ref[branches[b], col], up)
        return jnp.concatenate([qkv_ref[trunk, col], up, qkv_ref[own, col]], axis=0)

    q = qkv_ref[own, pl.ds(0, hd)]
    k, v = rows(pl.ds(hd, hd)), rows(pl.ds(2 * hd, hd))
    raw = dot(q, k, 1, 1) * HEAD_DIM ** -0.5
    n_trunk = TRUNK_SEGS * tok
    row = lax.broadcasted_iota(jnp.int32, raw.shape, 0)
    col = lax.broadcasted_iota(jnp.int32, raw.shape, 1)
    limit_up = jnp.where(s >= 2 * TRUNK_SEGS, n_trunk + tok, 0)
    limit_own = jnp.where(s >= TRUNK_SEGS, n_trunk + tok, -1)
    in_trunk = (col < n_trunk) & (col <= s * tok + row)
    in_up = (col >= n_trunk) & (col < limit_up)
    in_own = (col >= n_trunk + tok) & (col <= limit_own + row)
    seen = in_trunk | in_up | in_own
    raw = jnp.where(seen, raw, -jnp.inf)
    e = jnp.exp(raw - jnp.max(raw, axis=-1, keepdims=True))
    probs = e / jnp.sum(e, axis=-1, keepdims=True)
    return q, k, v, probs, own, trunk, branches, parent


def attend_kernel(extras, trees, *refs):
    own_in, own_out, (held,), extra_refs = sorted_refs(extras, refs, 4, 3)
    parent_ref, x_ref, vecs_ref, w_ref = own_in
    n_ref, qkv_ref, ctx_ref = own_out
    place = Place(trees)

    @pl.when(pl.program_id(0) == 0)
    def _():
        greet(place, extras)
        for e, r in zip(extras, extra_refs):
            e.start(place, *r)

    step = pl.program_id(0)
    rows = x_ref.shape[0]
    tok = held.shape[0] // TREE_SEGS
    n, _ = norm_stats(x_ref[...].astype(f32))
    norm = (n * vecs_ref[pl.ds(0, 1), :] + vecs_ref[pl.ds(1, 1), :]).astype(bf16)
    n_ref[...] = norm
    head = pl.ds(pl.multiple_of(place.at * HEAD_DIM, HEAD_DIM), HEAD_DIM)
    b_query, b_value = vecs_ref[pl.ds(2, 1), head], vecs_ref[pl.ds(3, 1), head]
    b = jnp.concatenate([b_query, jnp.zeros_like(b_query), b_value], axis=1)
    qkv = (dot(norm, w_ref[...], 1, 0) + b).astype(bf16)
    qkv_ref[...] = qkv
    held[pl.ds(pl.multiple_of(step * rows, rows), rows), :] = qkv

    @pl.when(step == pl.num_programs(0) - 1)
    def _():
        def one(s):
            _, _, v, probs, own, _, _, _ = scores_of(held, parent_ref, s, tok)
            ctx_ref[own, :] = dot(probs.astype(bf16), v, 1, 0).astype(bf16)

        pl.loop(0, TREE_SEGS, unroll=2)(one)
        for e, r in zip(extras, extra_refs):
            e.finish(place, *r)


def attend(parent, x_full, vecs, w, extras, cid):
    tokens, width = x_full.shape
    n = 3 * HEAD_DIM
    rows = 256
    whole = lambda shape: pl.BlockSpec(shape, lambda i: (0,) * len(shape))
    by_row = lambda cols: pl.BlockSpec((rows, cols), lambda i: (i, 0))
    return pl.pallas_call(
        functools.partial(attend_kernel, extras, lax.axis_size("tree")),
        grid=(tokens // rows,),
        in_specs=[
            pl.BlockSpec(memory_space=pltpu.SMEM), by_row(width), whole(vecs.shape), whole((width, n)), *[i for e in extras for i in e.in_specs],
        ],
        out_specs=[by_row(width), by_row(n), whole((tokens, HEAD_DIM)), *[o for e in extras for o in e.out_specs]],
        scratch_shapes=[*[i for e in extras for i in e.scratch], pltpu.VMEM((tokens, n), bf16)],
        out_shape=[
            jax.ShapeDtypeStruct((tokens, width), bf16),
            jax.ShapeDtypeStruct((tokens, n), bf16),
            jax.ShapeDtypeStruct((tokens, HEAD_DIM), bf16),
            *[o for e in extras for o in e.outs],
        ],
        compiler_params=pltpu.CompilerParams(collective_id=cid, has_side_effects=True, vmem_limit_bytes=58 * 2**20),
        cost_estimate=pl.CostEstimate(flops=2 * tokens * width * n, bytes_accessed=60_000_000, transcendentals=0),
        name="attend",
    )(parent, x_full, vecs, w, *[a for e in extras for a in e.ins])


def halves(v):
    high = v.astype(bf16)
    return high, (v - high.astype(f32)).astype(bf16)


def attend_back_kernel(extras, trees, *refs):
    own_in, own_out, own_scratch, extra_refs = sorted_refs(extras, refs, 7, 3)
    parent_ref, qkv_ref, d_ref, w_ref, w_qkv_ref, ctx_ref, n_ref = own_in
    o_ref, g_ref, f_ref = own_out
    dk, dv, d_ctx, held, sem, g_rows, g_rows_low = own_scratch
    *soon, later = list(zip(extras, extra_refs))
    place = Place(trees)
    step = pl.program_id(0)

    @pl.when(step == 0)
    def _():
        greet(place, extras)
        for e, r in soon:
            e.start(place, *r)
        g_rows[...] = jnp.zeros_like(g_rows)
        pltpu.make_async_copy(n_ref, held, sem).start()

    rows = d_ref.shape[0]
    tok = qkv_ref.shape[0] // TREE_SEGS
    hd = HEAD_DIM
    scale = HEAD_DIM ** -0.5
    d_ctx[pl.ds(pl.multiple_of(step * rows, rows), rows), :] = dot(d_ref[...], w_ref[...], 1, 1).astype(bf16)
    tile = 512
    for j in range(d_ref.shape[1] // tile):
        at = pl.ds(j * tile, tile)
        g_rows[:, at] += dot(ctx_ref[...], d_ref[:, at], 0, 0)

    @pl.when(step == pl.num_programs(0) - 1)
    def _():
        g_rows_low[...] = g_rows[...].astype(bf16)
        later[0].start(place, g_rows_low, *later[1])
        dk[...] = jnp.zeros_like(dk)
        dv[...] = jnp.zeros_like(dv)

        def one(s):
            q, k, v, probs, own, trunk, branches, parent = scores_of(qkv_ref, parent_ref, s, tok)
            dc = d_ctx[own, :]
            dp = dot(dc, v, 1, 1)
            ds = (probs * (dp - jnp.sum(probs * dp, axis=-1, keepdims=True))).astype(bf16)
            o_ref[own, pl.ds(0, hd)] = (dot(ds, k, 1, 0) * scale).astype(bf16)
            gk = dot(ds, q, 0, 0)
            gv = dot(probs.astype(bf16), dc, 0, 0)
            n_trunk = TRUNK_SEGS * tok
            for acc, g in ((dk, gk), (dv, gv)):
                acc[trunk, :] += g[:n_trunk]
                for b in range(4):
                    acc[branches[b], :] += jnp.where(parent == TRUNK_SEGS + b, g[n_trunk : n_trunk + tok], 0.0)
                acc[own, :] += g[n_trunk + tok :]

        pl.loop(0, TREE_SEGS, unroll=2)(one)
        o_ref[:, pl.ds(hd, hd)] = (dk[...] * scale).astype(bf16)
        o_ref[:, pl.ds(2 * hd, hd)] = dv[...].astype(bf16)
        drain(held, sem)
        total = jnp.sum(o_ref[...].astype(f32).reshape(-1, 8, o_ref.shape[1]), axis=0)
        total = jnp.broadcast_to(jnp.sum(total, axis=0, keepdims=True), total.shape)
        f_ref[pl.ds(16, 16), :] = jnp.zeros((16, f_ref.shape[1]), f32)
        head = pl.ds(pl.multiple_of(place.at * hd, hd), hd)
        f_ref[pl.ds(16, 8), head] = total[:, :hd]
        f_ref[pl.ds(24, 8), head] = total[:, 2 * hd :]
        ones = jnp.ones(total.shape, bf16)
        block = 512
        for j in range(held.shape[1] // block):
            at = pl.ds(j * block, block)
            g = dot(held[:, at], o_ref[...], 0, 0)
            g_ref[at, :] = g.astype(bf16)
            w = w_qkv_ref[at, :]
            f_ref[pl.ds(0, 8), at] = sum(dot(ones, part, 1, 1) for part in halves(w.astype(f32) * g))
            f_ref[pl.ds(8, 8), at] = sum(dot(part, w, 1, 1) for part in halves(total))
        for e, r in soon:
            e.finish(place, *r)
        later[0].finish(place, g_rows_low, *later[1])


def attend_back(parent, qkv, d_full, w_rows, w_qkv, context, norm_one, extras, cid):
    tokens, width = d_full.shape
    n = qkv.shape[1]
    rows = 256
    whole = lambda shape: pl.BlockSpec(shape, lambda i: (0,) * len(shape))
    return pl.pallas_call(
        functools.partial(attend_back_kernel, extras, lax.axis_size("tree")),
        grid=(tokens // rows,),
        in_specs=[
            pl.BlockSpec(memory_space=pltpu.SMEM), whole((tokens, n)), pl.BlockSpec((rows, width), lambda i: (i, 0)),
            whole((HEAD_DIM, width)), whole((width, n)),
            pl.BlockSpec((rows, HEAD_DIM), lambda i: (i, 0)), ANYWHERE, *[i for e in extras for i in e.in_specs],
        ],
        out_specs=[whole((tokens, n)), whole((width, n)), whole((32, width)), *[o for e in extras for o in e.out_specs]],
        scratch_shapes=[
            *[i for e in extras for i in e.scratch],
            pltpu.VMEM((tokens, HEAD_DIM), f32), pltpu.VMEM((tokens, HEAD_DIM), f32), pltpu.VMEM((tokens, HEAD_DIM), bf16),
            pltpu.VMEM((tokens, width), bf16), DMA,
            pltpu.VMEM((HEAD_DIM, width), f32), pltpu.VMEM((HEAD_DIM, width), bf16),
        ],
        out_shape=[
            jax.ShapeDtypeStruct((tokens, n), bf16), jax.ShapeDtypeStruct((width, n), bf16),
            jax.ShapeDtypeStruct((32, width), f32), *[o for e in extras for o in e.outs],
        ],
        compiler_params=pltpu.CompilerParams(collective_id=cid, has_side_effects=True, vmem_limit_bytes=58 * 2**20),
        cost_estimate=pl.CostEstimate(flops=2 * tokens * width * HEAD_DIM, bytes_accessed=60_000_000, transcendentals=0),
        name="attend_back",
    )(parent, qkv, d_full, w_rows, w_qkv, context, norm_one, *[a for e in extras for a in e.ins])


def feed_forward_kernel(n_ref, c_ref, wu_ref, wd_ref, b_ref, active_ref, d_ref, sum_ref):
    fs = wu_ref.shape[1]
    at = lax.axis_index("blk") * 2 + lax.axis_index("rep")
    b = b_ref[:, pl.ds(pl.multiple_of(at * fs, fs), fs)]
    act, der = gelu_pair(dot(n_ref[...], wu_ref[...], 1, 0) + b)
    active_ref[...] = act.astype(bf16)
    d = (dot(c_ref[...], wd_ref[...], 1, 0) * der).astype(bf16)
    d_ref[...] = d

    @pl.when(pl.program_id(0) == 0)
    def _():
        sum_ref[...] = jnp.zeros_like(sum_ref)

    sum_ref[...] += jnp.sum(d.astype(f32).reshape(-1, 8, d.shape[1]), axis=0)


def feed_forward(n_full, c_full, wu, wd, b):
    tokens, width = n_full.shape
    n = wu.shape[1]
    rows = 512
    whole = lambda shape: pl.BlockSpec(shape, lambda i: (0,) * len(shape))
    by_row = lambda cols: pl.BlockSpec((rows, cols), lambda i: (i, 0))
    return pl.pallas_call(
        feed_forward_kernel,
        grid=(tokens // rows,),
        in_specs=[by_row(width), by_row(width), whole((width, n)), whole((width, n)), whole((1, b.shape[0]))],
        out_specs=[by_row(n), by_row(n), whole((8, n))],
        out_shape=[jax.ShapeDtypeStruct((tokens, n), bf16)] * 2 + [jax.ShapeDtypeStruct((8, n), f32)],
        compiler_params=pltpu.CompilerParams(vmem_limit_bytes=40 * 2**20),
        cost_estimate=pl.CostEstimate(flops=4 * tokens * width * n, bytes_accessed=4 * tokens * width, transcendentals=0),
        name="feed_forward",
    )(n_full, c_full, wu, wd, b[None])


def last_kernel(*refs):
    dn_ref, x_ref, d_res_ref, vecs_ref, res_ref, mlp_ref, down_ref, *shares = refs[:12]
    grad_ref, out_ref, down_out, *sums = refs[12:]
    n, root = norm_stats(x_ref[...].astype(f32))
    grad_ref[...] = d_res_ref[...] + norm_back(dn_ref[...], n, root, vecs_ref[pl.ds(0, 1), :])
    out_ref[...] = (res_ref[...] + mlp_ref[...] + vecs_ref[pl.ds(7, 1), :]).astype(bf16)
    down_out[...] = down_ref[...].astype(f32)
    for share, total in zip(shares, sums):
        total[...] = jnp.sum(share[...].astype(f32), axis=0)


def last(d_norm, x, d_res, vecs, residual, mlp, g_down, shares):
    tok, width = x.shape
    steps = 4
    by_row = pl.BlockSpec((tok // steps, width), lambda i: (i, 0))
    vectors = pl.BlockSpec(vecs.shape, lambda i: (0, 0))
    by_column = lambda v: pl.BlockSpec((v.shape[0], v.shape[1] // steps), lambda i: (0, i))
    by_column_3 = lambda v: pl.BlockSpec(v.shape[:2] + (v.shape[2] // steps,), lambda i: (0, 0, i))
    flat = [jax.ShapeDtypeStruct(v.shape[1:], f32) for v in shares]
    return pl.pallas_call(
        last_kernel,
        grid=(steps,),
        in_specs=[by_row, by_row, by_row, vectors, by_row, by_row, by_column(g_down), *map(by_column_3, shares)],
        out_specs=[by_row, by_row, by_column(g_down), *map(by_column, flat)],
        out_shape=[
            jax.ShapeDtypeStruct((tok, width), f32), jax.ShapeDtypeStruct((tok, width), bf16),
            jax.ShapeDtypeStruct(g_down.shape, f32), *flat,
        ],
        compiler_params=pltpu.CompilerParams(vmem_limit_bytes=58 * 2**20),
        name="last",
    )(d_norm, x, d_res, vecs, residual, mlp, g_down, *shares)


def body(
    inputs, gain_one, bias_one, w_query, b_query, w_key, w_value, b_value, w_out, b_out,
    gain_two, bias_two, w_up, b_up, w_down, b_down, parents, cotangent,
):
    tok, width = inputs.shape
    rows = w_query.shape[0]
    ff = w_up.shape[1]
    fs = ff // TREE_SEGS
    trees = lax.axis_size("tree")
    devices = trees * TREE_SEGS
    tree = lax.axis_index("tree")
    me = lax.axis_index(GROUP)

    vectors = (gain_one, bias_one, b_query, b_value, b_out, gain_two, bias_two, b_down, b_up)
    n_small = sum(v.shape[0] for v in vectors)
    block = jnp.zeros((16 * 128,), bf16)
    at = 0
    for v in vectors:
        block = block + jnp.pad(v, (at, 16 * 128 - at - v.shape[0]))
        at += v.shape[0]
    block = block.reshape(16, 128)

    x_full, box, w_att = tree_gather(inputs, 0, "gather_inputs", FIRST, extras=(
        SpreadSmall(block), DealAll(w_query, w_key, w_value),
    ))
    w_att = w_att.reshape(width, -1)
    packed = box.transpose(1, 0, 2, 3).reshape(devices, -1)[:, :n_small]
    vecs = packed[:, : 8 * rows].reshape(devices, 8, rows).transpose(1, 0, 2).reshape(8, width).astype(f32)
    gain_one, bias_one, _, _, b_out, gain_two, bias_two, _ = vecs
    b_up = packed[:, 8 * rows :].reshape(-1).astype(f32)

    local_seg = jnp.arange(TREE_SEGS, dtype=jnp.int32)
    own_parents = lax.dynamic_slice_in_dim(parents, tree * TREE_SEGS, TREE_SEGS) - tree * TREE_SEGS
    parent = jnp.where(local_seg >= 2 * TRUNK_SEGS, own_parents, local_seg)

    norm_one, qkv, context, w_orow, share_up, share_down = attend(
        parent, x_full, vecs, w_att,
        (HeadRows(w_out), DealColumns(w_up), DealColumns(w_down)), 9
    )
    att, c_full, wd = product_scatter(context, w_orow, 0, 2, "scatter_attended", ROOM, extras=(
        GatherRows(cotangent, LIGHT), ToTrees(share_down.reshape(-1, fs)),
    ))
    wd = wd.reshape(width, fs)
    x_own = inputs.astype(f32)
    residual = x_own + att + b_out
    n_two, root_two = norm_stats(residual)
    norm_two = (n_two * gain_two + bias_two).astype(bf16)
    nt_full, wu = tree_gather(norm_two, 3, "gather_norm_two", LIGHT, extras=(ToTrees(share_up.reshape(-1, fs)),))
    wu = wu.reshape(width, fs)

    active, d_up, gb_up = feed_forward(nt_full, c_full, wu, wd, b_up)
    g_up = dot(nt_full, d_up, 0, 0).astype(bf16)
    d_norm_two, g_up, g_down = product_scatter(d_up, wu, 1, 4, "scatter_d_norm_two", MIXED, extras=(
        DealAllRows(g_up.reshape(devices, rows, fs), (fs,)), Product(c_full, active, 0, bf16),
    ))

    cot = cotangent.astype(f32)
    d_res = cot + norm_back(d_norm_two, n_two, root_two, gain_two)
    d_att = d_res.astype(bf16)
    mlp, da_full, swap_down = product_scatter(active, wd, 1, 5, "scatter_mlp", ROOM, extras=(
        GatherRows(d_att, LIGHT), SwapTrees(g_down),
    ))
    g_down = own_rows(g_down, swap_down, rows)
    d_qkv, g_att, shares, g_down, g_o = attend_back(
        parent, qkv, da_full, w_orow, w_att, context, norm_one, (DealRows(g_down, (fs,)), HeadRowsBack(width, rows)), 10
    )

    gb_one = shares[8]
    gg_one = (shares[0] - bias_one * gb_one) / gain_one

    def placed(vec, total):
        return lax.dynamic_update_slice_in_dim(jnp.zeros((total,), f32), vec, me * vec.shape[0], axis=0)

    col = lambda a: jnp.sum(a, axis=0)
    sums = [
        gg_one, gb_one, shares[16], shares[24],
        col(d_att.astype(f32)), col(d_norm_two * n_two), col(d_norm_two), col(cot),
    ]
    sums = jnp.stack(sums).reshape(8, devices, rows).transpose(1, 0, 2).reshape(devices, 8 * rows)
    sums = jnp.concatenate([sums, placed(col(gb_up), ff).reshape(devices, -1)], axis=1)
    sums = jnp.pad(sums, ((0, 0), (0, 1024 - n_small))).reshape(trees, TREE_SEGS, 8, 128).transpose(1, 0, 2, 3)
    d_norm_one, sums, g_q, g_k, g_v = product_scatter(d_qkv, w_att, 1, 7, "scatter_d_norm_one", MIXED, extras=(
        ReduceSmall(sums), DealAllRows(g_att.reshape(devices, rows, -1), (HEAD_DIM,) * 3),
    ))
    sums = sums.reshape(-1)
    parts = [sums[j * rows : (j + 1) * rows] for j in range(8)]
    gb_up = sums[8 * rows : n_small]

    grad_inputs, layer_output, g_down, g_q, g_k, g_v, g_o, g_up = last(
        d_norm_one, inputs, d_res, vecs, residual, mlp, g_down, (g_q, g_k, g_v, g_o, g_up)
    )
    return (
        layer_output, grad_inputs, parts[0], parts[1], g_q, parts[2], g_k, g_v, parts[3], g_o, parts[4],
        parts[5], parts[6], g_up, gb_up, g_down, parts[7],
    )


def solution(mesh):
    names = mesh.axis_names
    shape = mesh.devices.shape
    blk = TREE_SEGS // shape[1]
    inner = Mesh(mesh.devices.reshape(shape[0] // blk, blk, shape[1]), ALL)
    mat, vec = P(ALL, None), P(ALL)
    in_specs = (
        mat, vec, vec, mat, vec, mat, mat, vec, mat, vec, vec, vec, mat, vec, mat, vec, P(), mat,
    )
    out_specs = (
        mat, mat, vec, vec, mat, vec, mat, mat, vec, mat, vec, vec, vec, mat, vec, mat, vec,
    )
    return jax.shard_map(body, mesh=inner, in_specs=in_specs, out_specs=out_specs, check_vma=False)
```
